128 devices in a mesh: rep: 16 (over z, x_hi, core), sec: 2 (over x_lo), mdl: 4 (over y).
Axes of the slice: x: 4 (x_hi: 2, x_lo: 2; x = x_hi * 2 + x_lo), y: 4, z: 4, core: 2. Of those that a mesh axis runs over, the one named last changes fastest.
Arguments:
- obs: bfloat16 [2, 8192, 1536], P('sec', 'rep'), may hold values from -6 to 6
- a_query: bfloat16 [1536, 1536], P(None, 'mdl'), may hold values from -0.15309311 to 0.15309311
- a_keyval: bfloat16 [2, 1536, 512], P(None, None, 'mdl'), may hold values from -0.15309311 to 0.15309311
- a_out: bfloat16 [1536, 1536], P('mdl'), may hold values from -0.15625 to 0.15625
- w_policy: bfloat16 [1536, 128], replicated, may hold values from -0.15625 to 0.15625
- c_in: bfloat16 [1536, 2048], P(None, 'mdl'), may hold values from -0.15309311 to 0.15309311
- c_query: bfloat16 [2048, 2048], P(None, 'mdl'), may hold values from -0.13258252 to 0.13258252
- c_keyval: bfloat16 [2, 2048, 512], P(None, None, 'mdl'), may hold values from -0.13258252 to 0.13258252
- c_out: bfloat16 [2048, 2048], P('mdl'), may hold values from -0.125 to 0.125
- w_value: bfloat16 [2048], replicated, may hold values from -0.110485435 to 0.110485435
- actions: int32 [2, 8192], P('sec', 'rep'), may hold values from 0 to 127
- advantages: float32 [2, 8192], P('sec', 'rep'), may hold values from -6 to 6
- old_logp: float32 [2, 8192], P('sec', 'rep'), may hold values from -7 to -4
- returns: float32 [2, 8192], P('sec', 'rep'), may hold values from -6 to 6
- robot_count: int32 [2], replicated, may hold values from 2048 to 8192, as said below
Outputs:
- values: float32 [2, 8192], P('sec', ('rep', 'mdl'))
- grad_a_out: float32 [1536, 1536], P('mdl')
- grad_c_out: float32 [2048, 2048], P('mdl')
The draws below stay inside these ranges and needn't reach their ends.
Inputs may be any that keep to these rules, and one draw needn't show every extreme that they name: `robot_count`: one of the two micro-batches holds all 8192 robots, the other at least 2048; live robots are the first ones.
All inputs are finite; a program needn't handle non-finite values.
Results may differ from the reference program's by a relative error of at most 0.023.
Values may be sent and summed in bfloat16 or wider, within the bound.
A program may use at most 128 MiB of HBM per device.

```python
import math
import jax
import jax.numpy as jnp
from jax import lax

DA = 1536
HA = 12
KVA = 4
DC = 2048
HC = 16
KVC = 4
HEAD = 128
ACTIONS = 128
ROBOTS = 8192


def draw_robot_count(key, part):
    partial_value = jax.random.randint(jax.random.fold_in(key, 11), (), ROBOTS // 4, ROBOTS + 1)
    leading = jax.random.randint(jax.random.fold_in(key, 12), (), 0, 2)
    return jnp.where(jnp.arange(2) == leading, ROBOTS, partial_value).astype(jnp.int32)


def drawn_weight(key, tag, shape, fan_in):
    return jnp.clip(jax.random.normal(jax.random.fold_in(key, tag), shape, jnp.float32), -5.0, 5.0) * fan_in ** (-0.5)


def draw_obs(key, part):
    values_out = jnp.clip(jax.random.normal(jax.random.fold_in(key, 21), (2, ROBOTS, DA), jnp.float32), -6.0, 6.0)
    return values_out.astype(jnp.bfloat16)


def draw_a_query(key, part):
    shape = (DA, HA * HEAD)
    values_out = drawn_weight(key, 41, shape, DA)
    return values_out.astype(jnp.bfloat16)


def draw_a_keyval(key, part):
    shape = (2, DA, KVA * HEAD)
    values_out = drawn_weight(key, 42, shape, DA)
    return values_out.astype(jnp.bfloat16)


def draw_c_in(key, part):
    shape = (DA, DC)
    values_out = drawn_weight(key, 43, shape, DA)
    return values_out.astype(jnp.bfloat16)


def draw_c_query(key, part):
    shape = (DC, HC * HEAD)
    values_out = drawn_weight(key, 44, shape, DC)
    return values_out.astype(jnp.bfloat16)


def draw_c_keyval(key, part):
    shape = (2, DC, KVC * HEAD)
    values_out = drawn_weight(key, 45, shape, DC)
    return values_out.astype(jnp.bfloat16)


def draw_w_value(key, part):
    values_out = drawn_weight(key, 46, (DC,), DC)
    return values_out.astype(jnp.bfloat16)


def with_ends(drawn, own_key, low, largest):
    spot = [jax.random.randint(jax.random.fold_in(own_key, axis), (), 0, length) for axis, length in enumerate(drawn.shape)]
    main_axis = drawn.shape.index(max(drawn.shape))
    next_to = spot[:main_axis] + [(spot[main_axis] + 1) % drawn.shape[main_axis]] + spot[main_axis + 1:]
    return drawn.at[tuple(spot)].set(low).at[tuple(next_to)].set(largest)


def levels(stream_key, extent, pieces, low, top_value):
    gain = 1.0
    for dim, shards_of in pieces:
        heights = jax.random.uniform(jax.random.fold_in(jax.random.fold_in(stream_key, 6), dim), (shards_of,), jnp.float32, low / len(pieces), top_value / len(pieces))
        gain = gain * jnp.repeat(jnp.exp(heights), extent[dim] // shards_of).reshape((-1,) + (1,) * (len(extent) - 1 - dim))
    return gain


def centred(own_key, extent, deviation, most, split=(), kind=jnp.bfloat16):
    entries = jax.random.normal(own_key, extent, jnp.float32) * deviation
    if len(split) > 0:
        entries = levels(own_key, extent, split, -0.22, 0.18) * entries
    return jnp.clip(entries, min=-most, max=most).astype(kind)


def setup_inputs(seed: int = 0) -> dict:
    key_list = jax.random.split(jax.random.key(seed), 16)
    return {
        "obs": draw_obs(jax.random.fold_in(key_list[15], 71), 0),
        "a_query": draw_a_query(jax.random.fold_in(key_list[15], 71), 0),
        "a_keyval": draw_a_keyval(jax.random.fold_in(key_list[15], 71), 0),
        "a_out": centred(key_list[3], (HA * HEAD, DA), (HA * HEAD) ** -0.5, 0.15625, ((0, 4),)),
        "w_policy": centred(key_list[4], (DA, ACTIONS), DA ** -0.5, 0.15625),
        "c_in": draw_c_in(jax.random.fold_in(key_list[15], 71), 0),
        "c_query": draw_c_query(jax.random.fold_in(key_list[15], 71), 0),
        "c_keyval": draw_c_keyval(jax.random.fold_in(key_list[15], 71), 0),
        "c_out": centred(key_list[8], (HC * HEAD, DC), (HC * HEAD) ** -0.5, 0.125, ((0, 4),)),
        "w_value": draw_w_value(jax.random.fold_in(key_list[15], 71), 0),
        "actions": with_ends(jax.random.randint(key_list[10], (2, ROBOTS), 0, ACTIONS), jax.random.fold_in(key_list[10], 1), 0, ACTIONS - 1).astype(jnp.int32),
        "advantages": centred(key_list[11], (2, ROBOTS), 1.0, 6.0, ((0, 2), (1, 16)), jnp.float32),
        "old_logp": jnp.clip(-7.0 + 3.0 * jax.random.uniform(key_list[12], (2, ROBOTS), jnp.float32) ** levels(key_list[12], (2, ROBOTS), ((0, 2), (1, 16)), -0.2, 0.2), -7.0, -4.0),
        "returns": centred(key_list[13], (2, ROBOTS), 1.0, 6.0, ((0, 2), (1, 16)), jnp.float32),
        "robot_count": draw_robot_count(jax.random.fold_in(key_list[15], 71), 0),
    }


epsilon = 1e-05
clip_range = 0.2
masked_score = -1e+30

def rms_normed(values_in):
    return values_in * lax.rsqrt(lax.optimization_barrier(jnp.mean(values_in * values_in, axis=-1, keepdims=True)) + epsilon)

def norm_backward(source, normed, grad_in):
    factor = lax.rsqrt(lax.optimization_barrier(jnp.mean(source * source, axis=-1, keepdims=True)) + epsilon)
    return factor * (grad_in - normed * lax.optimization_barrier(jnp.mean(grad_in * normed, axis=-1, keepdims=True)))

def project(source, w_query, w_keyval):
    normed = rms_normed(source).astype(jnp.bfloat16)
    queries = (jnp.dot(normed, w_query, preferred_element_type=jnp.float32) * HEAD ** (-0.5)).astype(jnp.bfloat16)
    keyval = jnp.stack([jnp.dot(normed, w_keyval[0], preferred_element_type=jnp.float32), jnp.dot(normed, w_keyval[1], preferred_element_type=jnp.float32)]).astype(jnp.bfloat16)
    return (queries, keyval)

def policy_backward(hidden, action_ids, advantage, old_values, live_mask, live_total, w_policy):
    source = hidden.astype(jnp.float32)
    normed = rms_normed(source)
    logits = jnp.dot(normed.astype(jnp.bfloat16), w_policy, preferred_element_type=jnp.float32)
    log_probs = jax.nn.log_softmax(logits, axis=-1)
    onehot = (action_ids[:, None] == lax.broadcasted_iota(jnp.int32, logits.shape, 1)).astype(jnp.float32)
    chosen = lax.optimization_barrier(jnp.sum(onehot * log_probs, axis=-1))
    prob_ratio = jnp.exp(chosen - old_values)
    plain_term = prob_ratio * advantage
    bounded = jnp.clip(prob_ratio, 1.0 - clip_range, 1.0 + clip_range) * advantage
    slope_term = jnp.where(live_mask & (plain_term <= bounded), -plain_term / live_total, jnp.float32(0.0))
    dlogits = slope_term[:, None] * (onehot - jnp.exp(log_probs))
    dnormed = jnp.dot(dlogits, w_policy.astype(jnp.float32).T, precision=lax.Precision.HIGHEST)
    return norm_backward(source, normed, dnormed)

def value_backward(mixed_out, target, live_mask, live_total, w_value):
    normed = rms_normed(mixed_out)
    value_pred = jnp.dot(normed.astype(jnp.bfloat16), w_value, preferred_element_type=jnp.float32)
    slope_term = jnp.where(live_mask, value_pred - target, jnp.float32(0.0)) / live_total
    dnormed = slope_term[:, None] * w_value.astype(jnp.float32)[None, :]
    return (value_pred, norm_backward(mixed_out, normed, dnormed))

def attend(queries, keyval, live_mask):
    row_count = queries.shape[0]
    kv_heads = keyval.shape[2] // HEAD
    groups = queries.shape[1] // HEAD // kv_heads
    key_rows = keyval[0].reshape(row_count, kv_heads, HEAD).astype(jnp.float32)
    value_rows = keyval[1].reshape(row_count, kv_heads, HEAD).astype(jnp.float32)
    block_rows = math.gcd(row_count, 512)

    def absorb_block(query_block):
        query_f = query_block.reshape(block_rows, kv_heads, groups, HEAD).astype(jnp.float32)
        scores = jnp.einsum('bkgd,jkd->kgbj', query_f, key_rows)
        scores = jnp.where(live_mask, scores, masked_score)
        row_top = lax.optimization_barrier(jnp.max(scores, axis=-1, keepdims=True))
        weights = jnp.exp(scores - row_top)
        row_sum = lax.optimization_barrier(jnp.sum(weights, axis=-1))
        combined = jnp.einsum('kgbj,jkd->bkgd', weights, value_rows, precision=lax.Precision.HIGHEST)
        combined = combined / jnp.transpose(row_sum, (2, 0, 1))[..., None]
        return combined.reshape(block_rows, kv_heads * groups * HEAD)
    attended = lax.map(absorb_block, queries.reshape(row_count // block_rows, block_rows, -1))
    return attended.reshape(row_count, -1).astype(jnp.bfloat16)

def reference(obs, a_query, a_keyval, a_out, w_policy, c_in, c_query, c_keyval, c_out, w_value, actions, advantages, old_logp, returns, robot_count):
    live_total = jnp.sum(robot_count).astype(jnp.float32)
    actor_grad = jnp.zeros((HA * HEAD, DA), jnp.float32)
    critic_grad = jnp.zeros((HC * HEAD, DC), jnp.float32)
    value_list = []
    for batch_index in range(2):
        live_mask = lax.iota(jnp.int32, ROBOTS) < robot_count[batch_index]
        obs_float = obs[batch_index].astype(jnp.float32)
        queries, keyval = project(obs_float, a_query, a_keyval)
        attended = attend(queries, keyval, live_mask)
        hidden = (obs_float + jnp.dot(attended, a_out, preferred_element_type=jnp.float32)).astype(jnp.bfloat16)
        dhidden = policy_backward(hidden, actions[batch_index], advantages[batch_index], old_logp[batch_index], live_mask, live_total, w_policy).astype(jnp.bfloat16)
        actor_grad = actor_grad + jnp.dot(attended.T, dhidden, preferred_element_type=jnp.float32)
        embedded = jnp.dot(hidden, c_in, preferred_element_type=jnp.float32).astype(jnp.bfloat16)
        embed_float = embedded.astype(jnp.float32)
        critic_queries, critic_keyval = project(embed_float, c_query, c_keyval)
        critic_attended = attend(critic_queries, critic_keyval, live_mask)
        mixed_out = embed_float + jnp.dot(critic_attended, c_out, preferred_element_type=jnp.float32)
        value_pred, dmixed = value_backward(mixed_out, returns[batch_index], live_mask, live_total, w_value)
        critic_grad = critic_grad + jnp.dot(critic_attended.T, dmixed.astype(jnp.bfloat16), preferred_element_type=jnp.float32)
        value_list.append(value_pred)
    return (jnp.stack(value_list), actor_grad, critic_grad)
```

```python
import functools

import jax
import jax.numpy as jnp
from jax import lax
from jax.experimental import pallas as pl
from jax.experimental.pallas import tpu as pltpu
from jax.sharding import PartitionSpec as P

HEAD = 128
LOG2E = 1.4426950408889634
MESH = pl.DeviceIdType.MESH
BF = jnp.bfloat16
F32 = jnp.float32

epsilon = 1e-05
clip_range = 0.2
masked_score = -1e30
sum_low = 1e-20
sum_high = 1e25


def rms_normed(values_in):
    return values_in * lax.rsqrt(jnp.mean(values_in * values_in, axis=-1, keepdims=True) + epsilon)


def norm_backward(source, normed, grad_in):
    factor = lax.rsqrt(jnp.mean(source * source, axis=-1, keepdims=True) + epsilon)
    return factor * (grad_in - normed * jnp.mean(grad_in * normed, axis=-1, keepdims=True))


def policy_backward(hidden, action_ids, advantage, old_values, live_mask, live_total, w_policy):
    source = hidden.astype(F32)
    normed = rms_normed(source)
    logits = jnp.dot(normed.astype(BF), w_policy, preferred_element_type=F32)
    log_probs = jax.nn.log_softmax(logits, axis=-1)
    onehot = (action_ids[:, None] == lax.broadcasted_iota(jnp.int32, logits.shape, 1)).astype(F32)
    chosen = jnp.sum(onehot * log_probs, axis=-1)
    prob_ratio = jnp.exp(chosen - old_values)
    plain_term = prob_ratio * advantage
    bounded = jnp.clip(prob_ratio, 1.0 - clip_range, 1.0 + clip_range) * advantage
    slope_term = jnp.where(
        live_mask & (plain_term <= bounded), -plain_term / live_total, jnp.float32(0.0)
    )
    dlogits = slope_term[:, None] * (onehot - jnp.exp(log_probs))
    dnormed = lax.dot_general(
        dlogits.astype(BF), w_policy, (((1,), (1,)), ((), ())), preferred_element_type=F32
    )
    return norm_backward(source, normed, dnormed)


def value_backward(mixed_out, target, live_mask, live_total, w_value):
    normed = rms_normed(mixed_out)
    value_pred = jnp.dot(normed.astype(BF), w_value, preferred_element_type=F32)
    slope_term = jnp.where(live_mask, value_pred - target, jnp.float32(0.0)) / live_total
    dnormed = slope_term[:, None] * w_value.astype(F32)[None, :]
    return (value_pred, norm_backward(mixed_out, normed, dnormed))


PIECES = 2


def attend_kernel(
    heads, with_w, total_ref, q_ref, kv_ref, *refs
):
    if with_w:
        w_ref, out_ref, sums_ref, kvout_ref, wfull_ref = refs[:5]
        refs = refs[5:]
        buf, acc, send, recv, local, wsend, wrecv, wlocal = refs
    else:
        out_ref, sums_ref, kvout_ref = refs[:3]
        buf, acc, send, recv, local = refs[3:]
    rows = kv_ref.shape[0]
    piece = rows // PIECES
    all_keys = buf.shape[0]
    me = lax.axis_index("rep")
    count = 16
    core = lax.rem(me, 2)
    xpos = lax.rem(me // 2, 2)
    other = me + 1 - 2 * core
    xpeer = me + 2 - 4 * xpos
    zp = lax.rem(me + 4, count)
    zm = lax.rem(me + 12, count)
    src = [
        zm,
        zp,
        lax.rem(me + 8, count),
        xpeer,
        lax.rem(xpeer + 12, count),
        lax.rem(xpeer + 4, count),
        lax.rem(xpeer + 8, count),
    ]
    src = src + [other] + [s + 1 - 2 * core for s in src]

    ypos = lax.axis_index("mdl")
    yp = lax.rem(ypos + 1, 4)
    ym = lax.rem(ypos + 3, 4)
    y2 = lax.rem(ypos + 2, 4)

    barrier = pltpu.get_barrier_semaphore()
    peers = [{"rep": zp}, {"rep": zm}, {"rep": xpeer}, {"rep": other}]
    if with_w:
        peers += [{"mdl": yp}, {"mdl": ym}]
    for peer in peers:
        pl.semaphore_signal(barrier, inc=1, device_id=peer, device_id_type=MESH)
    pl.semaphore_wait(barrier, len(peers))

    started = []

    def block_rows(block, part):
        return pl.ds(pl.multiple_of(block * rows + part * piece, piece), piece)

    def transfer(block, part, slot, target, lane, own=False):
        where = buf.at[block_rows(block, part), pl.ds(0, 2 * HEAD)]
        source = kv_ref.at[pl.ds(part * piece, piece)] if own else where
        return pltpu.make_async_remote_copy(
            src_ref=source,
            dst_ref=where,
            send_sem=send.at[lane, part],
            recv_sem=recv.at[slot, part],
            device_id={"rep": target},
            device_id_type=MESH,
        )

    plan = [
        (None, 3, xpeer),
        (None, 1, zm),
        (None, 0, zp),
        (None, 7, other),
        (1, 9, other),
        (0, 2, zp),
        (0, 8, other),
        (3, 5, zm),
        (3, 4, zp),
        (3, 11, other),
        (2, 10, other),
        (5, 6, zm),
        (5, 13, other),
        (4, 12, other),
        (6, 14, other),
    ]

    def plan_copy(index, part):
        from_slot, to_slot, target = plan[index]
        block = me if from_slot is None else src[from_slot]
        return transfer(block, part, to_slot, target, index, own=from_slot is None)

    def arrived(slot, part):
        where = buf.at[block_rows(src[slot], part), pl.ds(0, 2 * HEAD)]
        pltpu.make_async_copy(where, where, recv.at[slot, part]).wait()

    def keep(slot):
        block = me if slot is None else src[slot]
        where = pl.ds(pl.multiple_of(block * rows, rows), rows)
        index = 15 if slot is None else slot
        source = kv_ref if slot is None else buf.at[where, pl.ds(0, 2 * HEAD)]
        return pltpu.make_async_copy(source, kvout_ref.at[where], local.at[index])

    def pass_on(slot):
        for part in range(PIECES):
            arrived(slot, part)
            for index, (from_slot, _, _) in enumerate(plan):
                if from_slot == slot:
                    plan_copy(index, part).start()
        keep(slot).start()

    def take(slot):
        for part in range(PIECES):
            arrived(slot, part)
        keep(slot).start()

    for part in range(PIECES):
        for index in range(4):
            plan_copy(index, part).start()
    own_copy = pltpu.make_async_copy(
        kv_ref,
        buf.at[pl.ds(pl.multiple_of(me * rows, rows), rows), pl.ds(0, 2 * HEAD)],
        local.at[16],
    )
    own_copy.start()
    keep(None).start()

    if with_w:
        wrows = w_ref.shape[0]
        wpiece = wrows // 4
        wown = pltpu.make_async_copy(w_ref, wfull_ref.at[ypos], wlocal.at[0])
        wown.start()

        wsrc = [ym, yp, y2]

        def wcopy(source_y, which, part, slot, target, lane, own=False):
            span = pl.ds((2 * which + part) * wpiece, wpiece)
            where = wfull_ref.at[source_y, span]
            return pltpu.make_async_remote_copy(
                src_ref=w_ref.at[span] if own else where,
                dst_ref=where,
                send_sem=wsend.at[lane, part],
                recv_sem=wrecv.at[slot, part],
                device_id=target,
                device_id_type=MESH,
            )

        def wfirst(part):
            return [
                wcopy(ypos, core, part, 0, {"mdl": yp}, 0, own=True),
                wcopy(ypos, core, part, 1, {"mdl": ym}, 1, own=True),
            ]

        def wrelay(part):
            if part == 0:
                return wcopy(ym, core, 0, 2, {"mdl": yp}, 2)
            return wcopy(yp, core, 1, 2, {"mdl": ym}, 2)

        def wshare(slot, part):
            return wcopy(wsrc[slot], core, part, 3 + slot, {"rep": other}, 3 + slot)

        def warrived(slot, part):
            which = core if slot < 3 else 1 - core
            span = pl.ds((2 * which + part) * wpiece, wpiece)
            where = wfull_ref.at[wsrc[slot % 3], span]
            pltpu.make_async_copy(where, where, wrecv.at[slot, part]).wait()

        for part in range(2):
            for copy in wfirst(part):
                copy.start()

    total = total_ref[0]
    key_index = lax.broadcasted_iota(jnp.int32, (all_keys, HEAD), 0)
    buf[:, 2 * HEAD :] = jnp.where(key_index < total, 1.0, 0.0).astype(BF)
    acc[...] = jnp.zeros_like(acc)
    own_copy.wait()

    chip_rows = 2 * rows
    zpos = me // 4

    def step(i, carry):
        @pl.when(i == 0)
        def _():
            take(7)

        @pl.when(i == 1)
        def _():
            pass_on(1)
            pass_on(0)
            take(9)

        @pl.when(i == 2)
        def _():
            pass_on(3)
            take(8)

        @pl.when(i == 3)
        def _():
            pass_on(2)
            take(10)

        @pl.when(i == 4)
        def _():
            pass_on(5)
            take(11)

        if with_w:

            @pl.when(i == 5)
            def _():
                for part in range(2):
                    warrived(0, part)
                    warrived(1, part)
                    wrelay(part).start()
                    wshare(0, part).start()
                    wshare(1, part).start()

        @pl.when(i == 5)
        def _():
            pass_on(4)
            take(13)

        @pl.when(i == 6)
        def _():
            pass_on(6)
            take(12)

        @pl.when(i == 7)
        def _():
            take(14)

        j = lax.rem(i, 4)
        dz = j + (j // 2) * (1 - 2 * lax.rem(j, 2))
        dx = i // 4
        chip = lax.rem(zpos + dz, 4) * 2 + lax.rem(xpos + dx, 2)
        span = pl.ds(pl.multiple_of(chip * chip_rows, chip_rows), chip_rows)
        scores = lax.dot_general(
            q_ref[...],
            buf[span, :HEAD],
            (((1,), (1,)), ((), ())),
            preferred_element_type=F32,
        )
        weights = jnp.exp2(scores).astype(BF)
        acc[...] += jnp.dot(weights, buf[span, HEAD:], preferred_element_type=F32)
        return carry

    lax.fori_loop(0, 8, step, 0)

    if with_w:
        for part in range(2):
            warrived(2, part)
            wshare(2, part).start()

    for head in range(heads):
        part = acc[head * rows : (head + 1) * rows, :]
        sums = part[:, HEAD:]
        out_ref[:, head * HEAD : (head + 1) * HEAD] = (part[:, :HEAD] / sums).astype(BF)
        low = jnp.min(sums, axis=0, keepdims=True)
        high = jnp.max(sums, axis=0, keepdims=True)
        sums_ref[2 * head : 2 * head + 1, :] = low
        sums_ref[2 * head + 1 : 2 * head + 2, :] = high

    if with_w:
        for slot in range(3, 6):
            for part in range(2):
                warrived(slot, part)
        for part in range(2):
            for copy in wfirst(part):
                copy.wait_send()
            wrelay(part).wait_send()
            for slot in range(3):
                wshare(slot, part).wait_send()
        wown.wait()
    for part in range(PIECES):
        for index in range(len(plan)):
            plan_copy(index, part).wait_send()
    keep(None).wait()
    for slot in range(15):
        keep(slot).wait()


def attend_call(total, queries, keyval, w, ident):
    heads = queries.shape[0] // keyval.shape[0]
    rows = keyval.shape[0]
    keys = rows * 16
    vmem = pl.BlockSpec(memory_space=pltpu.VMEM)
    anywhere = pl.BlockSpec(memory_space=pl.ANY)
    out_shape = [
        jax.ShapeDtypeStruct((rows, heads * HEAD), BF),
        jax.ShapeDtypeStruct((2 * heads, HEAD), F32),
        jax.ShapeDtypeStruct((keys, 2 * HEAD), BF),
    ]
    out_specs = [vmem, vmem, anywhere]
    in_specs = [pl.BlockSpec(memory_space=pltpu.SMEM), vmem, vmem]
    args = [total, queries, keyval]
    scratch = [
        pltpu.VMEM((keys, 3 * HEAD), BF),
        pltpu.VMEM((heads * rows, 2 * HEAD), F32),
        pltpu.SemaphoreType.DMA((15, PIECES)),
        pltpu.SemaphoreType.DMA((15, PIECES)),
        pltpu.SemaphoreType.DMA((17,)),
    ]
    if w is not None:
        out_shape.append(jax.ShapeDtypeStruct((4,) + w.shape, BF))
        out_specs.append(anywhere)
        in_specs.append(anywhere)
        args.append(w)
        scratch += [
            pltpu.SemaphoreType.DMA((6, 2)),
            pltpu.SemaphoreType.DMA((6, 2)),
            pltpu.SemaphoreType.DMA((1,)),
        ]
    return pl.pallas_call(
        functools.partial(attend_kernel, heads, w is not None),
        out_shape=out_shape,
        in_specs=in_specs,
        out_specs=out_specs,
        scratch_shapes=scratch,
        compiler_params=pltpu.CompilerParams(
            collective_id=ident, has_side_effects=True, vmem_limit_bytes=48 * 2**20
        ),
        cost_estimate=pl.CostEstimate(
            flops=4 * heads * rows * keys * HEAD,
            bytes_accessed=keys * 4 * HEAD,
            transcendentals=heads * rows * keys,
        ),
    )(*args)


def careful_kernel(total_ref, q_ref, kv_ref, out_ref, top, acc, total_sum):
    step = pl.program_id(0)
    block = kv_ref.shape[0]

    @pl.when(step == 0)
    def _():
        top[...] = jnp.full_like(top, masked_score)
        acc[...] = jnp.zeros_like(acc)
        total_sum[...] = jnp.zeros_like(total_sum)

    scores = lax.dot_general(
        q_ref[...], kv_ref[:, :HEAD], (((1,), (1,)), ((), ())), preferred_element_type=F32
    )
    key_index = step * block + lax.broadcasted_iota(jnp.int32, scores.shape, 1)
    live = key_index < total_ref[0]
    scores = jnp.where(live, scores, masked_score)
    old = top[...]
    new = jnp.maximum(old, jnp.max(scores, axis=1, keepdims=True))
    top[...] = new
    rescale = jnp.exp2(old - new)
    weights = jnp.where(live, jnp.exp2(scores - new[:, :1]), 0.0)
    total_sum[...] = total_sum[...] * rescale + jnp.sum(weights, axis=1, keepdims=True)
    acc[...] = acc[...] * rescale + jnp.dot(
        weights.astype(BF), kv_ref[:, HEAD:], preferred_element_type=F32
    )

    @pl.when(step == pl.num_programs(0) - 1)
    def _():
        rows, width = out_ref.shape
        for head in range(width // HEAD):
            span = slice(head * rows, (head + 1) * rows)
            out_ref[:, head * HEAD : (head + 1) * HEAD] = (acc[span, :] / total_sum[span, :]).astype(
                BF
            )


def careful_call(total, queries, kv_full, rows):
    heads = queries.shape[0] // rows
    block = 512
    return pl.pallas_call(
        careful_kernel,
        out_shape=jax.ShapeDtypeStruct((rows, heads * HEAD), BF),
        grid=(kv_full.shape[0] // block,),
        in_specs=[
            pl.BlockSpec(memory_space=pltpu.SMEM),
            pl.BlockSpec(queries.shape, lambda i: (0, 0)),
            pl.BlockSpec((block, 2 * HEAD), lambda i: (i, 0)),
        ],
        out_specs=pl.BlockSpec((rows, heads * HEAD), lambda i: (0, 0)),
        scratch_shapes=[pltpu.VMEM((heads * rows, HEAD), F32)] * 3,
        compiler_params=pltpu.CompilerParams(vmem_limit_bytes=48 * 2**20),
    )(total, queries, kv_full)


def attend(total, queries, keyval, w, ident):
    results = attend_call(total, queries, keyval, w, ident)
    plain, sums, kv_full = results[:3]
    safe = jnp.all((sums > sum_low) & (sums < sum_high))
    attended = lax.cond(
        safe,
        lambda: plain,
        lambda: careful_call(total, queries, kv_full, keyval.shape[0]),
    )
    return attended if w is None else (attended, results[3])


def gather_kernel(x_ref, out_ref, send, recv, local):
    rows, width = x_ref.shape
    half = rows // 2
    ypos = lax.axis_index("mdl")
    yp = lax.rem(ypos + 1, 4)
    ym = lax.rem(ypos + 3, 4)
    y2 = lax.rem(ypos + 2, 4)
    barrier = pltpu.get_barrier_semaphore()
    for peer in (yp, ym):
        pl.semaphore_signal(barrier, inc=1, device_id={"mdl": peer}, device_id_type=MESH)
    pl.semaphore_wait(barrier, 2)

    def place(source_y, part):
        return out_ref.at[
            pl.ds(part * half, half), pl.ds(pl.multiple_of(source_y * width, HEAD), width)
        ]

    def copy(source_y, part, slot, target, lane, own=False):
        where = place(source_y, part)
        return pltpu.make_async_remote_copy(
            src_ref=x_ref.at[pl.ds(part * half, half)] if own else where,
            dst_ref=where,
            send_sem=send.at[lane, part],
            recv_sem=recv.at[slot, part],
            device_id={"mdl": target},
            device_id_type=MESH,
        )

    def arrived(slot, source_y, part):
        where = place(source_y, part)
        pltpu.make_async_copy(where, where, recv.at[slot, part]).wait()

    first = [
        copy(ypos, 0, 0, yp, 0, own=True),
        copy(ypos, 1, 1, ym, 1, own=True),
        copy(ypos, 1, 0, yp, 0, own=True),
        copy(ypos, 0, 1, ym, 1, own=True),
    ]
    for item in first:
        item.start()
    mine = pltpu.make_async_copy(
        x_ref, out_ref.at[:, pl.ds(pl.multiple_of(ypos * width, HEAD), width)], local.at[0]
    )
    mine.start()
    arrived(0, ym, 0)
    up = copy(ym, 0, 2, yp, 2)
    up.start()
    arrived(1, yp, 1)
    down = copy(yp, 1, 2, ym, 2)
    down.start()
    arrived(0, ym, 1)
    arrived(1, yp, 0)
    arrived(2, y2, 0)
    arrived(2, y2, 1)
    for item in first:
        item.wait_send()
    up.wait_send()
    down.wait_send()
    mine.wait()


def gather_columns(x, ident):
    vmem = pl.BlockSpec(memory_space=pltpu.VMEM)
    return pl.pallas_call(
        gather_kernel,
        out_shape=jax.ShapeDtypeStruct((x.shape[0], 4 * x.shape[1]), x.dtype),
        in_specs=[vmem],
        out_specs=vmem,
        scratch_shapes=[
            pltpu.SemaphoreType.DMA((3, 2)),
            pltpu.SemaphoreType.DMA((3, 2)),
            pltpu.SemaphoreType.DMA((1,)),
        ],
        compiler_params=pltpu.CompilerParams(
            collective_id=ident, has_side_effects=True, vmem_limit_bytes=48 * 2**20
        ),
    )(x)


def project(source, w_query, w_keyval, live_mask):
    rows = source.shape[0]
    normed = rms_normed(source).astype(BF)
    queries = (
        jnp.dot(normed, w_query, preferred_element_type=F32) * (HEAD ** (-0.5) * LOG2E)
    ).astype(BF)
    heads = queries.shape[1] // HEAD
    stacked = jnp.transpose(queries.reshape(rows, heads, HEAD), (1, 0, 2)).reshape(
        heads * rows, HEAD
    )
    keyval = [jnp.dot(normed, w_keyval[part], preferred_element_type=F32) for part in range(2)]
    joined = jnp.where(live_mask[:, None], jnp.concatenate(keyval, axis=1), 0.0).astype(BF)
    return (stacked, joined)


def on_device(
    obs,
    a_query,
    a_keyval,
    a_out,
    w_policy,
    c_in,
    c_query,
    c_keyval,
    c_out,
    w_value,
    actions,
    advantages,
    old_logp,
    returns,
    robot_count,
):
    row_count = obs.shape[1]
    batch_index = lax.axis_index("sec")
    robot_total = robot_count[batch_index]
    total = robot_total.reshape(1)
    live_total = jnp.sum(robot_count).astype(F32)
    first_row = lax.axis_index("rep") * row_count
    live_mask = first_row + lax.iota(jnp.int32, row_count) < robot_total
    mdl_count = lax.axis_size("mdl")
    part_rows = row_count // mdl_count
    row_start = lax.axis_index("mdl") * part_rows
    obs_float = obs[0].astype(F32)

    queries, keyval = project(obs_float, a_query, a_keyval, live_mask)
    attended, a_out_full = attend(total, queries, keyval, a_out, 1)
    attended_full = gather_columns(attended, 3)
    hidden = (
        obs_float
        + jnp.dot(
            attended_full,
            a_out_full.reshape(4 * a_out.shape[0], a_out.shape[1]),
            preferred_element_type=F32,
        )
    ).astype(BF)
    embed_part = jnp.dot(hidden, c_in, preferred_element_type=F32).astype(BF)
    embedded = gather_columns(embed_part, 4)
    dhidden = policy_backward(
        hidden, actions[0], advantages[0], old_logp[0], live_mask, live_total, w_policy
    ).astype(BF)
    actor_grad = lax.dot_general(
        attended, dhidden, (((0,), (0,)), ((), ())), preferred_element_type=F32
    ).astype(BF)
    embed_float = embedded.astype(F32)
    critic_queries, critic_keyval = project(embed_float, c_query, c_keyval, live_mask)
    critic_attended = attend(total, critic_queries, critic_keyval, None, 2)
    critic_sum = lax.psum(
        jnp.dot(critic_attended, c_out, preferred_element_type=F32).astype(BF),
        "mdl",
    ).astype(F32)
    value_pred, dmixed = value_backward(
        embed_float + critic_sum, returns[0], live_mask, live_total, w_value
    )
    value_part = lax.dynamic_slice_in_dim(value_pred, row_start, part_rows, 0)
    critic_grad = lax.dot_general(
        critic_attended, dmixed.astype(BF), (((0,), (0,)), ((), ())), preferred_element_type=F32
    )
    actor_summed = lax.psum(actor_grad, ("rep", "sec")).astype(F32)
    critic_summed = lax.psum(critic_grad.astype(BF), ("rep", "sec")).astype(F32)
    return (value_part[None, :], actor_summed, critic_summed)


def solution(mesh):
    return jax.shard_map(
        on_device,
        mesh=mesh,
        in_specs=(
            P("sec", "rep", None),
            P(None, "mdl"),
            P(None, None, "mdl"),
            P("mdl", None),
            P(),
            P(None, "mdl"),
            P(None, "mdl"),
            P(None, None, "mdl"),
            P("mdl", None),
            P(),
            P("sec", "rep"),
            P("sec", "rep"),
            P("sec", "rep"),
            P("sec", "rep"),
            P(),
        ),
        out_specs=(P("sec", ("rep", "mdl")), P("mdl", None), P("mdl", None)),
        check_vma=False,
    )
```

```python
import functools

import jax
import jax.numpy as jnp
from jax import lax
from jax.experimental import pallas as pl
from jax.experimental.pallas import tpu as pltpu
from jax.sharding import PartitionSpec as P

HEAD = 128
LOG2E = 1.4426950408889634
MESH = pl.DeviceIdType.MESH
BF = jnp.bfloat16
F32 = jnp.float32

epsilon = 1e-05
clip_range = 0.2
masked_score = -1e30
sum_low = 1e-20
sum_high = 1e25


def rms_normed(values_in):
    return values_in * lax.rsqrt(jnp.mean(values_in * values_in, axis=-1, keepdims=True) + epsilon)


def norm_backward(source, normed, grad_in):
    factor = lax.rsqrt(jnp.mean(source * source, axis=-1, keepdims=True) + epsilon)
    return factor * (grad_in - normed * jnp.mean(grad_in * normed, axis=-1, keepdims=True))


def policy_backward(hidden, action_ids, advantage, old_values, live_mask, live_total, w_policy):
    source = hidden.astype(F32)
    normed = rms_normed(source)
    logits = jnp.dot(normed.astype(BF), w_policy, preferred_element_type=F32)
    log_probs = jax.nn.log_softmax(logits, axis=-1)
    onehot = (action_ids[:, None] == lax.broadcasted_iota(jnp.int32, logits.shape, 1)).astype(F32)
    chosen = jnp.sum(onehot * log_probs, axis=-1)
    prob_ratio = jnp.exp(chosen - old_values)
    plain_term = prob_ratio * advantage
    bounded = jnp.clip(prob_ratio, 1.0 - clip_range, 1.0 + clip_range) * advantage
    slope_term = jnp.where(
        live_mask & (plain_term <= bounded), -plain_term / live_total, jnp.float32(0.0)
    )
    dlogits = slope_term[:, None] * (onehot - jnp.exp(log_probs))
    dnormed = lax.dot_general(
        dlogits.astype(BF), w_policy, (((1,), (1,)), ((), ())), preferred_element_type=F32
    )
    return norm_backward(source, normed, dnormed)


def value_backward(mixed_out, target, live_mask, live_total, w_value):
    normed = rms_normed(mixed_out)
    value_pred = jnp.dot(normed.astype(BF), w_value, preferred_element_type=F32)
    slope_term = jnp.where(live_mask, value_pred - target, jnp.float32(0.0)) / live_total
    dnormed = slope_term[:, None] * w_value.astype(F32)[None, :]
    return (value_pred, norm_backward(mixed_out, normed, dnormed))


PIECES = 2


def attend_kernel(
    heads, with_w, total_ref, q_ref, kv_ref, *refs
):
    if with_w:
        w_ref, out_ref, sums_ref, kvout_ref, wfull_ref = refs[:5]
        refs = refs[5:]
        buf, acc, send, recv, local, wsend, wrecv, wlocal = refs
    else:
        out_ref, sums_ref, kvout_ref = refs[:3]
        buf, acc, send, recv, local = refs[3:]
    rows = kv_ref.shape[0]
    piece = rows // PIECES
    all_keys = buf.shape[0]
    me = lax.axis_index("rep")
    count = 16
    core = lax.rem(me, 2)
    xpos = lax.rem(me // 2, 2)
    other = me + 1 - 2 * core
    xpeer = me + 2 - 4 * xpos
    zp = lax.rem(me + 4, count)
    zm = lax.rem(me + 12, count)
    src = [
        zm,
        zp,
        lax.rem(me + 8, count),
        xpeer,
        lax.rem(xpeer + 12, count),
        lax.rem(xpeer + 4, count),
        lax.rem(xpeer + 8, count),
    ]
    src = src + [other] + [s + 1 - 2 * core for s in src]

    ypos = lax.axis_index("mdl")
    yp = lax.rem(ypos + 1, 4)
    ym = lax.rem(ypos + 3, 4)
    y2 = lax.rem(ypos + 2, 4)

    barrier = pltpu.get_barrier_semaphore()
    peers = [{"rep": zp}, {"rep": zm}, {"rep": xpeer}, {"rep": other}]
    if with_w:
        peers += [{"mdl": yp}, {"mdl": ym}]
    for peer in peers:
        pl.semaphore_signal(barrier, inc=1, device_id=peer, device_id_type=MESH)
    pl.semaphore_wait(barrier, len(peers))

    def block_rows(block, part):
        return pl.ds(pl.multiple_of(block * rows + part * piece, piece), piece)

    def transfer(block, part, slot, target, lane, own=False):
        where = buf.at[block_rows(block, part), pl.ds(0, 2 * HEAD)]
        source = kv_ref.at[pl.ds(part * piece, piece)] if own else where
        return pltpu.make_async_remote_copy(
            src_ref=source,
            dst_ref=where,
            send_sem=send.at[lane, part],
            recv_sem=recv.at[slot, part],
            device_id={"rep": target},
            device_id_type=MESH,
        )

    plan = [
        (None, 3, xpeer),
        (None, 1, zm),
        (None, 0, zp),
        (None, 7, other),
        (1, 9, other),
        (0, 2, zp),
        (0, 8, other),
        (3, 5, zm),
        (3, 4, zp),
        (3, 11, other),
        (2, 10, other),
        (5, 6, zm),
        (5, 13, other),
        (4, 12, other),
        (6, 14, other),
    ]

    def plan_copy(index, part):
        from_slot, to_slot, target = plan[index]
        block = me if from_slot is None else src[from_slot]
        return transfer(block, part, to_slot, target, index, own=from_slot is None)

    def arrived(slot, part):
        where = buf.at[block_rows(src[slot], part), pl.ds(0, 2 * HEAD)]
        pltpu.make_async_copy(where, where, recv.at[slot, part]).wait()

    def keep(slot):
        block = me if slot is None else src[slot]
        where = pl.ds(pl.multiple_of(block * rows, rows), rows)
        index = 15 if slot is None else slot
        source = kv_ref if slot is None else buf.at[where, pl.ds(0, 2 * HEAD)]
        return pltpu.make_async_copy(source, kvout_ref.at[where], local.at[index])

    def pass_on(slot):
        for part in range(PIECES):
            arrived(slot, part)
            for index, (from_slot, _, _) in enumerate(plan):
                if from_slot == slot:
                    plan_copy(index, part).start()
        keep(slot).start()

    def take(slot):
        for part in range(PIECES):
            arrived(slot, part)
        keep(slot).start()

    for part in range(PIECES):
        for index in range(4):
            plan_copy(index, part).start()
    own_copy = pltpu.make_async_copy(
        kv_ref,
        buf.at[pl.ds(pl.multiple_of(me * rows, rows), rows), pl.ds(0, 2 * HEAD)],
        local.at[16],
    )
    own_copy.start()
    keep(None).start()

    if with_w:
        wrows = w_ref.shape[0]
        wpiece = wrows // 4
        wown = pltpu.make_async_copy(w_ref, wfull_ref.at[ypos], wlocal.at[0])
        wown.start()

        wsrc = [ym, yp, y2]

        def wcopy(source_y, which, part, slot, target, lane, own=False):
            span = pl.ds((2 * which + part) * wpiece, wpiece)
            where = wfull_ref.at[source_y, span]
            return pltpu.make_async_remote_copy(
                src_ref=w_ref.at[span] if own else where,
                dst_ref=where,
                send_sem=wsend.at[lane, part],
                recv_sem=wrecv.at[slot, part],
                device_id=target,
                device_id_type=MESH,
            )

        def wfirst(part):
            return [
                wcopy(ypos, core, part, 0, {"mdl": yp}, 0, own=True),
                wcopy(ypos, core, part, 1, {"mdl": ym}, 1, own=True),
            ]

        def wrelay(part):
            if part == 0:
                return wcopy(ym, core, 0, 2, {"mdl": yp}, 2)
            return wcopy(yp, core, 1, 2, {"mdl": ym}, 2)

        def wshare(slot, part):
            return wcopy(wsrc[slot], core, part, 3 + slot, {"rep": other}, 3 + slot)

        def warrived(slot, part):
            which = core if slot < 3 else 1 - core
            span = pl.ds((2 * which + part) * wpiece, wpiece)
            where = wfull_ref.at[wsrc[slot % 3], span]
            pltpu.make_async_copy(where, where, wrecv.at[slot, part]).wait()

        for part in range(2):
            for copy in wfirst(part):
                copy.start()

    total = total_ref[0]
    key_index = lax.broadcasted_iota(jnp.int32, (all_keys, HEAD), 0)
    buf[:, 2 * HEAD :] = jnp.where(key_index < total, 1.0, 0.0).astype(BF)
    acc[...] = jnp.zeros_like(acc)
    own_copy.wait()

    chip_rows = 2 * rows
    zpos = me // 4

    def step(i, carry):
        @pl.when(i == 0)
        def _():
            take(7)

        @pl.when(i == 1)
        def _():
            pass_on(1)
            pass_on(0)
            take(9)

        @pl.when(i == 2)
        def _():
            pass_on(3)
            take(8)

        @pl.when(i == 3)
        def _():
            pass_on(2)
            take(10)

        @pl.when(i == 4)
        def _():
            pass_on(5)
            take(11)

        if with_w:

            @pl.when(i == 5)
            def _():
                for part in range(2):
                    warrived(0, part)
                    warrived(1, part)
                    wrelay(part).start()
                    wshare(0, part).start()
                    wshare(1, part).start()

        @pl.when(i == 5)
        def _():
            pass_on(4)
            take(13)

        @pl.when(i == 6)
        def _():
            pass_on(6)
            take(12)

        @pl.when(i == 7)
        def _():
            take(14)

        j = lax.rem(i, 4)
        dz = j + (j // 2) * (1 - 2 * lax.rem(j, 2))
        dx = i // 4
        chip = lax.rem(zpos + dz, 4) * 2 + lax.rem(xpos + dx, 2)
        span = pl.ds(pl.multiple_of(chip * chip_rows, chip_rows), chip_rows)
        scores = lax.dot_general(
            q_ref[...],
            buf[span, :HEAD],
            (((1,), (1,)), ((), ())),
            preferred_element_type=F32,
        )
        weights = jnp.exp2(scores).astype(BF)
        acc[...] += jnp.dot(weights, buf[span, HEAD:], preferred_element_type=F32)
        return carry

    lax.fori_loop(0, 8, step, 0)

    if with_w:
        for part in range(2):
            warrived(2, part)
            wshare(2, part).start()

    for head in range(heads):
        part = acc[head * rows : (head + 1) * rows, :]
        sums = part[:, HEAD:]
        out_ref[:, head * HEAD : (head + 1) * HEAD] = (part[:, :HEAD] / sums).astype(BF)
        low = jnp.min(sums, axis=0, keepdims=True)
        high = jnp.max(sums, axis=0, keepdims=True)
        sums_ref[2 * head : 2 * head + 1, :] = low
        sums_ref[2 * head + 1 : 2 * head + 2, :] = high

    if with_w:
        for slot in range(3, 6):
            for part in range(2):
                warrived(slot, part)
        for part in range(2):
            for copy in wfirst(part):
                copy.wait_send()
            wrelay(part).wait_send()
            for slot in range(3):
                wshare(slot, part).wait_send()
        wown.wait()
    for part in range(PIECES):
        for index in range(len(plan)):
            plan_copy(index, part).wait_send()
    keep(None).wait()
    for slot in range(15):
        keep(slot).wait()


def attend_call(total, queries, keyval, w, ident):
    heads = queries.shape[0] // keyval.shape[0]
    rows = keyval.shape[0]
    keys = rows * 16
    vmem = pl.BlockSpec(memory_space=pltpu.VMEM)
    anywhere = pl.BlockSpec(memory_space=pl.ANY)
    out_shape = [
        jax.ShapeDtypeStruct((rows, heads * HEAD), BF),
        jax.ShapeDtypeStruct((2 * heads, HEAD), F32),
        jax.ShapeDtypeStruct((keys, 2 * HEAD), BF),
    ]
    out_specs = [vmem, vmem, anywhere]
    in_specs = [pl.BlockSpec(memory_space=pltpu.SMEM), vmem, vmem]
    args = [total, queries, keyval]
    scratch = [
        pltpu.VMEM((keys, 3 * HEAD), BF),
        pltpu.VMEM((heads * rows, 2 * HEAD), F32),
        pltpu.SemaphoreType.DMA((15, PIECES)),
        pltpu.SemaphoreType.DMA((15, PIECES)),
        pltpu.SemaphoreType.DMA((17,)),
    ]
    if w is not None:
        out_shape.append(jax.ShapeDtypeStruct((4,) + w.shape, BF))
        out_specs.append(anywhere)
        in_specs.append(anywhere)
        args.append(w)
        scratch += [
            pltpu.SemaphoreType.DMA((6, 2)),
            pltpu.SemaphoreType.DMA((6, 2)),
            pltpu.SemaphoreType.DMA((1,)),
        ]
    return pl.pallas_call(
        functools.partial(attend_kernel, heads, w is not None),
        out_shape=out_shape,
        in_specs=in_specs,
        out_specs=out_specs,
        scratch_shapes=scratch,
        compiler_params=pltpu.CompilerParams(
            collective_id=ident, has_side_effects=True, vmem_limit_bytes=48 * 2**20
        ),
        cost_estimate=pl.CostEstimate(
            flops=4 * heads * rows * keys * HEAD,
            bytes_accessed=keys * 4 * HEAD,
            transcendentals=heads * rows * keys,
        ),
    )(*args)


def careful_kernel(total_ref, q_ref, kv_ref, out_ref, top, acc, total_sum):
    step = pl.program_id(0)
    block = kv_ref.shape[0]

    @pl.when(step == 0)
    def _():
        top[...] = jnp.full_like(top, masked_score)
        acc[...] = jnp.zeros_like(acc)
        total_sum[...] = jnp.zeros_like(total_sum)

    scores = lax.dot_general(
        q_ref[...], kv_ref[:, :HEAD], (((1,), (1,)), ((), ())), preferred_element_type=F32
    )
    key_index = step * block + lax.broadcasted_iota(jnp.int32, scores.shape, 1)
    live = key_index < total_ref[0]
    scores = jnp.where(live, scores, masked_score)
    old = top[...]
    new = jnp.maximum(old, jnp.max(scores, axis=1, keepdims=True))
    top[...] = new
    rescale = jnp.exp2(old - new)
    weights = jnp.where(live, jnp.exp2(scores - new[:, :1]), 0.0)
    total_sum[...] = total_sum[...] * rescale + jnp.sum(weights, axis=1, keepdims=True)
    acc[...] = acc[...] * rescale + jnp.dot(
        weights.astype(BF), kv_ref[:, HEAD:], preferred_element_type=F32
    )

    @pl.when(step == pl.num_programs(0) - 1)
    def _():
        rows, width = out_ref.shape
        for head in range(width // HEAD):
            span = slice(head * rows, (head + 1) * rows)
            out_ref[:, head * HEAD : (head + 1) * HEAD] = (acc[span, :] / total_sum[span, :]).astype(
                BF
            )


def careful_call(total, queries, kv_full, rows):
    heads = queries.shape[0] // rows
    block = 512
    return pl.pallas_call(
        careful_kernel,
        out_shape=jax.ShapeDtypeStruct((rows, heads * HEAD), BF),
        grid=(kv_full.shape[0] // block,),
        in_specs=[
            pl.BlockSpec(memory_space=pltpu.SMEM),
            pl.BlockSpec(queries.shape, lambda i: (0, 0)),
            pl.BlockSpec((block, 2 * HEAD), lambda i: (i, 0)),
        ],
        out_specs=pl.BlockSpec((rows, heads * HEAD), lambda i: (0, 0)),
        scratch_shapes=[pltpu.VMEM((heads * rows, HEAD), F32)] * 3,
        compiler_params=pltpu.CompilerParams(vmem_limit_bytes=48 * 2**20),
    )(total, queries, kv_full)


def attend(total, queries, keyval, w, ident):
    results = attend_call(total, queries, keyval, w, ident)
    plain, sums, kv_full = results[:3]
    safe = jnp.all((sums > sum_low) & (sums < sum_high))
    attended = lax.cond(
        safe,
        lambda: plain,
        lambda: careful_call(total, queries, kv_full, keyval.shape[0]),
    )
    return attended if w is None else (attended, results[3])


def gather_kernel(x_ref, out_ref, send, recv, local):
    rows, width = x_ref.shape
    half = rows // 2
    ypos = lax.axis_index("mdl")
    yp = lax.rem(ypos + 1, 4)
    ym = lax.rem(ypos + 3, 4)
    y2 = lax.rem(ypos + 2, 4)
    barrier = pltpu.get_barrier_semaphore()
    for peer in (yp, ym):
        pl.semaphore_signal(barrier, inc=1, device_id={"mdl": peer}, device_id_type=MESH)
    pl.semaphore_wait(barrier, 2)

    def place(source_y, part):
        return out_ref.at[
            pl.ds(part * half, half), pl.ds(pl.multiple_of(source_y * width, HEAD), width)
        ]

    def copy(source_y, part, slot, target, lane, own=False):
        where = place(source_y, part)
        return pltpu.make_async_remote_copy(
            src_ref=x_ref.at[pl.ds(part * half, half)] if own else where,
            dst_ref=where,
            send_sem=send.at[lane, part],
            recv_sem=recv.at[slot, part],
            device_id={"mdl": target},
            device_id_type=MESH,
        )

    def arrived(slot, source_y, part):
        where = place(source_y, part)
        pltpu.make_async_copy(where, where, recv.at[slot, part]).wait()

    first = [
        copy(ypos, 0, 0, yp, 0, own=True),
        copy(ypos, 1, 1, ym, 1, own=True),
        copy(ypos, 1, 0, yp, 0, own=True),
        copy(ypos, 0, 1, ym, 1, own=True),
    ]
    for item in first:
        item.start()
    mine = pltpu.make_async_copy(
        x_ref, out_ref.at[:, pl.ds(pl.multiple_of(ypos * width, HEAD), width)], local.at[0]
    )
    mine.start()
    arrived(0, ym, 0)
    up = copy(ym, 0, 2, yp, 2)
    up.start()
    arrived(1, yp, 1)
    down = copy(yp, 1, 2, ym, 2)
    down.start()
    arrived(0, ym, 1)
    arrived(1, yp, 0)
    arrived(2, y2, 0)
    arrived(2, y2, 1)
    for item in first:
        item.wait_send()
    up.wait_send()
    down.wait_send()
    mine.wait()


def gather_columns(x, ident):
    vmem = pl.BlockSpec(memory_space=pltpu.VMEM)
    return pl.pallas_call(
        gather_kernel,
        out_shape=jax.ShapeDtypeStruct((x.shape[0], 4 * x.shape[1]), x.dtype),
        in_specs=[vmem],
        out_specs=vmem,
        scratch_shapes=[
            pltpu.SemaphoreType.DMA((3, 2)),
            pltpu.SemaphoreType.DMA((3, 2)),
            pltpu.SemaphoreType.DMA((1,)),
        ],
        compiler_params=pltpu.CompilerParams(
            collective_id=ident, has_side_effects=True, vmem_limit_bytes=8 * 2**20
        ),
    )(x)


def reduce_kernel(att_ref, d_ref, out_ref, theirs, mine, got, part_in, part_sum, sub_in, send, recv, csend, crecv):
    half = theirs.shape[0]
    block = half // 2
    width = out_ref.shape[1] // 4
    sub = block // 4
    me = lax.axis_index("rep")
    xlow = lax.axis_index("sec")
    core = lax.rem(me, 2)
    other = me + 1 - 2 * core
    zpos = me // 4
    xpos = lax.rem(me // 2, 2) * 2 + xlow

    def at_x(k):
        there = lax.rem(xpos + k, 4)
        return {"rep": zpos * 4 + (there // 2) * 2 + core, "sec": lax.rem(there, 2)}

    def at_z(k):
        return {"rep": lax.rem(me + 4 * k, 16)}

    near = [at_x, at_z]
    first = [xpos, zpos]
    second = [zpos, xpos]

    barrier = pltpu.get_barrier_semaphore()
    for k in range(1, 4):
        pl.semaphore_signal(barrier, inc=1, device_id=at_x(k), device_id_type=MESH)
        pl.semaphore_signal(barrier, inc=1, device_id=at_z(k), device_id_type=MESH)
    pl.semaphore_signal(barrier, inc=1, device_id={"rep": other}, device_id_type=MESH)

    def grad_rows(which):
        span = pl.ds(pl.multiple_of(which * half, half), half)
        return lax.dot_general(
            att_ref[:, span], d_ref[...], (((0,), (0,)), ((), ())), preferred_element_type=F32
        )

    theirs[...] = grad_rows(1 - core).astype(BF)
    pl.semaphore_wait(barrier, 7)
    swap = pltpu.make_async_remote_copy(
        src_ref=theirs,
        dst_ref=got,
        send_sem=csend.at[0],
        recv_sem=crecv.at[0],
        device_id={"rep": other},
        device_id_type=MESH,
    )
    swap.start()
    own = grad_rows(core)
    swap.wait_recv()
    mine[...] = (own + got[...].astype(F32)).astype(BF)

    def columns(index):
        return pl.ds(pl.multiple_of(index * width, width), width)

    def scatter_one(part, k):
        return pltpu.make_async_remote_copy(
            src_ref=mine.at[pl.ds(part * block, block), columns(lax.rem(first[part] + k, 4))],
            dst_ref=part_in.at[part, k - 1],
            send_sem=send.at[0, part, k - 1],
            recv_sem=recv.at[0, part, k - 1],
            device_id=near[part](k),
            device_id_type=MESH,
        )

    def sub_rows(index):
        return pl.ds(pl.multiple_of(index * sub, sub), sub)

    def scatter_two(part, k):
        return pltpu.make_async_remote_copy(
            src_ref=part_sum.at[part, sub_rows(lax.rem(second[part] + k, 4))],
            dst_ref=sub_in.at[part, k - 1],
            send_sem=send.at[1, part, k - 1],
            recv_sem=recv.at[1, part, k - 1],
            device_id=near[1 - part](k),
            device_id_type=MESH,
        )

    def out_rows(which, part, offset, size):
        return pl.ds(pl.multiple_of(which * half + part * block + offset, size), size)

    def gather_two(part, k):
        where = out_ref.at[
            out_rows(core, part, second[part] * sub, sub), columns(first[part])
        ]
        return pltpu.make_async_remote_copy(
            src_ref=where,
            dst_ref=where,
            send_sem=send.at[2, part, k - 1],
            recv_sem=recv.at[2, part, k - 1],
            device_id=near[1 - part](k),
            device_id_type=MESH,
        )

    def gather_one(part, k):
        where = out_ref.at[out_rows(core, part, 0, block), columns(first[part])]
        return pltpu.make_async_remote_copy(
            src_ref=where,
            dst_ref=where,
            send_sem=send.at[3, part, k - 1],
            recv_sem=recv.at[3, part, k - 1],
            device_id=near[part](k),
            device_id_type=MESH,
        )

    def share(part, k, which):
        where = out_ref.at[
            out_rows(which, part, 0, block), columns(lax.rem(first[part] + 4 - k, 4))
        ]
        index = 1 + part * 4 + k
        return pltpu.make_async_remote_copy(
            src_ref=where,
            dst_ref=where,
            send_sem=csend.at[index],
            recv_sem=crecv.at[index],
            device_id={"rep": other},
            device_id_type=MESH,
        )

    parts = range(2)
    hops = (2, 1, 3)
    for k in hops:
        for part in parts:
            scatter_one(part, k).start()
    for part in parts:
        total = mine[pl.ds(part * block, block), columns(first[part])].astype(F32)
        for k in (1, 3, 2):
            scatter_one(part, k).wait_recv()
            total += part_in[part, k - 1].astype(F32)
        part_sum[part] = total.astype(BF)
        for k in hops:
            scatter_two(part, k).start()
    for part in parts:
        total = part_sum[part, sub_rows(second[part])].astype(F32)
        for k in (1, 3, 2):
            scatter_two(part, k).wait_recv()
            total += sub_in[part, k - 1].astype(F32)
        out_ref[out_rows(core, part, second[part] * sub, sub), columns(first[part])] = total.astype(
            BF
        )
        for k in hops:
            gather_two(part, k).start()
    for part in parts:
        for k in range(1, 4):
            gather_two(part, k).wait_recv()
        for k in hops:
            gather_one(part, k).start()
        share(part, 0, core).start()
    for k in (1, 3, 2):
        for part in parts:
            gather_one(part, k).wait_recv()
            share(part, k, core).start()
    for part in parts:
        for k in range(4):
            share(part, k, 1 - core).wait_recv()
    swap.wait_send()
    for part in parts:
        for k in range(1, 4):
            scatter_one(part, k).wait_send()
            scatter_two(part, k).wait_send()
            gather_two(part, k).wait_send()
            gather_one(part, k).wait_send()
        for k in range(4):
            share(part, k, core).wait_send()


def reduced_grad(attended, grad_in, ident):
    heads_width = attended.shape[1]
    columns = grad_in.shape[1]
    half = heads_width // 2
    block = half // 2
    vmem = pl.BlockSpec(memory_space=pltpu.VMEM)
    return pl.pallas_call(
        reduce_kernel,
        out_shape=jax.ShapeDtypeStruct((heads_width, columns), BF),
        in_specs=[vmem, vmem],
        out_specs=vmem,
        scratch_shapes=[
            pltpu.VMEM((half, columns), BF),
            pltpu.VMEM((half, columns), BF),
            pltpu.VMEM((half, columns), BF),
            pltpu.VMEM((2, 3, block, columns // 4), BF),
            pltpu.VMEM((2, block, columns // 4), BF),
            pltpu.VMEM((2, 3, block // 4, columns // 4), BF),
            pltpu.SemaphoreType.DMA((4, 2, 3)),
            pltpu.SemaphoreType.DMA((4, 2, 3)),
            pltpu.SemaphoreType.DMA((9,)),
            pltpu.SemaphoreType.DMA((9,)),
        ],
        compiler_params=pltpu.CompilerParams(
            collective_id=ident, has_side_effects=True, vmem_limit_bytes=24 * 2**20
        ),
    )(attended, grad_in)


def project(source, w_query, w_keyval, live_mask):
    rows = source.shape[0]
    normed = rms_normed(source).astype(BF)
    queries = (
        jnp.dot(normed, w_query, preferred_element_type=F32) * (HEAD ** (-0.5) * LOG2E)
    ).astype(BF)
    heads = queries.shape[1] // HEAD
    stacked = jnp.transpose(queries.reshape(rows, heads, HEAD), (1, 0, 2)).reshape(
        heads * rows, HEAD
    )
    keyval = [jnp.dot(normed, w_keyval[part], preferred_element_type=F32) for part in range(2)]
    joined = jnp.where(live_mask[:, None], jnp.concatenate(keyval, axis=1), 0.0).astype(BF)
    return (stacked, joined)


def on_device(
    obs,
    a_query,
    a_keyval,
    a_out,
    w_policy,
    c_in,
    c_query,
    c_keyval,
    c_out,
    w_value,
    actions,
    advantages,
    old_logp,
    returns,
    robot_count,
):
    row_count = obs.shape[1]
    batch_index = lax.axis_index("sec")
    robot_total = robot_count[batch_index]
    total = robot_total.reshape(1)
    live_total = jnp.sum(robot_count).astype(F32)
    first_row = lax.axis_index("rep") * row_count
    live_mask = first_row + lax.iota(jnp.int32, row_count) < robot_total
    mdl_count = lax.axis_size("mdl")
    part_rows = row_count // mdl_count
    row_start = lax.axis_index("mdl") * part_rows
    obs_float = obs[0].astype(F32)

    queries, keyval = project(obs_float, a_query, a_keyval, live_mask)
    attended, a_out_full = attend(total, queries, keyval, a_out, 1)
    attended_full = gather_columns(attended, 3)
    hidden = (
        obs_float
        + jnp.dot(
            attended_full,
            a_out_full.reshape(4 * a_out.shape[0], a_out.shape[1]),
            preferred_element_type=F32,
        )
    ).astype(BF)
    embed_part = jnp.dot(hidden, c_in, preferred_element_type=F32).astype(BF)
    embedded = gather_columns(embed_part, 4)
    dhidden = policy_backward(
        hidden, actions[0], advantages[0], old_logp[0], live_mask, live_total, w_policy
    ).astype(BF)
    actor_grad = lax.dot_general(
        attended, dhidden, (((0,), (0,)), ((), ())), preferred_element_type=F32
    ).astype(BF)
    embed_float = embedded.astype(F32)
    critic_queries, critic_keyval = project(embed_float, c_query, c_keyval, live_mask)
    critic_attended, c_out_full = attend(total, critic_queries, critic_keyval, c_out, 2)
    critic_full = gather_columns(critic_attended, 5)
    critic_sum = jnp.dot(
        critic_full,
        c_out_full.reshape(4 * c_out.shape[0], c_out.shape[1]),
        preferred_element_type=F32,
    )
    value_pred, dmixed = value_backward(
        embed_float + critic_sum, returns[0], live_mask, live_total, w_value
    )
    value_part = lax.dynamic_slice_in_dim(value_pred, row_start, part_rows, 0)
    critic_summed = reduced_grad(critic_attended, dmixed.astype(BF), 6).astype(F32)
    actor_summed = lax.psum(actor_grad, ("rep", "sec")).astype(F32)
    return (value_part[None, :], actor_summed, critic_summed)


def solution(mesh):
    return jax.shard_map(
        on_device,
        mesh=mesh,
        in_specs=(
            P("sec", "rep", None),
            P(None, "mdl"),
            P(None, None, "mdl"),
            P("mdl", None),
            P(),
            P(None, "mdl"),
            P(None, "mdl"),
            P(None, None, "mdl"),
            P("mdl", None),
            P(),
            P("sec", "rep"),
            P("sec", "rep"),
            P("sec", "rep"),
            P("sec", "rep"),
            P(),
        ),
        out_specs=(P("sec", ("rep", "mdl")), P("mdl", None), P("mdl", None)),
        check_vma=False,
    )
```

```python
import functools

import jax
import jax.numpy as jnp
from jax import lax
from jax.experimental import pallas as pl
from jax.experimental.pallas import tpu as pltpu
from jax.sharding import PartitionSpec as P

HEAD = 128
LOG2E = 1.4426950408889634
MESH = pl.DeviceIdType.MESH
BF = jnp.bfloat16
F32 = jnp.float32

epsilon = 1e-05
clip_range = 0.2
masked_score = -1e30
sum_low = 1e-20
sum_high = 1e25


def rms_normed(values_in):
    return values_in * lax.rsqrt(jnp.mean(values_in * values_in, axis=-1, keepdims=True) + epsilon)


def norm_backward(source, normed, grad_in):
    factor = lax.rsqrt(jnp.mean(source * source, axis=-1, keepdims=True) + epsilon)
    return factor * (grad_in - normed * jnp.mean(grad_in * normed, axis=-1, keepdims=True))


def policy_backward(hidden, action_ids, advantage, old_values, live_mask, live_total, w_policy):
    source = hidden.astype(F32)
    normed = rms_normed(source)
    logits = jnp.dot(normed.astype(BF), w_policy, preferred_element_type=F32)
    log_probs = jax.nn.log_softmax(logits, axis=-1)
    onehot = (action_ids[:, None] == lax.broadcasted_iota(jnp.int32, logits.shape, 1)).astype(F32)
    chosen = jnp.sum(onehot * log_probs, axis=-1)
    prob_ratio = jnp.exp(chosen - old_values)
    plain_term = prob_ratio * advantage
    bounded = jnp.clip(prob_ratio, 1.0 - clip_range, 1.0 + clip_range) * advantage
    slope_term = jnp.where(
        live_mask & (plain_term <= bounded), -plain_term / live_total, jnp.float32(0.0)
    )
    dlogits = slope_term[:, None] * (onehot - jnp.exp(log_probs))
    dnormed = lax.dot_general(
        dlogits.astype(BF), w_policy, (((1,), (1,)), ((), ())), preferred_element_type=F32
    )
    return norm_backward(source, normed, dnormed)


def value_backward(mixed_out, target, live_mask, live_total, w_value):
    normed = rms_normed(mixed_out)
    value_pred = jnp.dot(normed.astype(BF), w_value, preferred_element_type=F32)
    slope_term = jnp.where(live_mask, value_pred - target, jnp.float32(0.0)) / live_total
    dnormed = slope_term[:, None] * w_value.astype(F32)[None, :]
    return (value_pred, norm_backward(mixed_out, normed, dnormed))


PIECES = 2


def attend_kernel(
    heads, with_w, total_ref, q_ref, kv_ref, *refs
):
    if with_w:
        w_ref, out_ref, sums_ref, kvout_ref, wfull_ref = refs[:5]
        refs = refs[5:]
        buf, acc, send, recv, local, wsend, wrecv, wlocal = refs
    else:
        out_ref, sums_ref, kvout_ref = refs[:3]
        buf, acc, send, recv, local = refs[3:]
    rows = kv_ref.shape[0]
    piece = rows // PIECES
    all_keys = buf.shape[0]
    me = lax.axis_index("rep")
    count = 16
    core = lax.rem(me, 2)
    xpos = lax.rem(me // 2, 2)
    other = me + 1 - 2 * core
    xpeer = me + 2 - 4 * xpos
    zp = lax.rem(me + 4, count)
    zm = lax.rem(me + 12, count)
    src = [
        zm,
        zp,
        lax.rem(me + 8, count),
        xpeer,
        lax.rem(xpeer + 12, count),
        lax.rem(xpeer + 4, count),
        lax.rem(xpeer + 8, count),
    ]
    src = src + [other] + [s + 1 - 2 * core for s in src]

    ypos = lax.axis_index("mdl")
    yp = lax.rem(ypos + 1, 4)
    ym = lax.rem(ypos + 3, 4)
    y2 = lax.rem(ypos + 2, 4)

    barrier = pltpu.get_barrier_semaphore()
    peers = [{"rep": zp}, {"rep": zm}, {"rep": xpeer}, {"rep": other}]
    if with_w:
        peers += [{"mdl": yp}, {"mdl": ym}]
    for peer in peers:
        pl.semaphore_signal(barrier, inc=1, device_id=peer, device_id_type=MESH)
    pl.semaphore_wait(barrier, len(peers))

    def block_rows(block, part):
        return pl.ds(pl.multiple_of(block * rows + part * piece, piece), piece)

    def transfer(block, part, slot, target, lane, own=False):
        where = buf.at[block_rows(block, part), pl.ds(0, 2 * HEAD)]
        source = kv_ref.at[pl.ds(part * piece, piece)] if own else where
        return pltpu.make_async_remote_copy(
            src_ref=source,
            dst_ref=where,
            send_sem=send.at[lane, part],
            recv_sem=recv.at[slot, part],
            device_id={"rep": target},
            device_id_type=MESH,
        )

    plan = [
        (None, 3, xpeer),
        (None, 1, zm),
        (None, 0, zp),
        (None, 7, other),
        (1, 9, other),
        (0, 2, zp),
        (0, 8, other),
        (3, 5, zm),
        (3, 4, zp),
        (3, 11, other),
        (2, 10, other),
        (5, 6, zm),
        (5, 13, other),
        (4, 12, other),
        (6, 14, other),
    ]

    def plan_copy(index, part):
        from_slot, to_slot, target = plan[index]
        block = me if from_slot is None else src[from_slot]
        return transfer(block, part, to_slot, target, index, own=from_slot is None)

    def arrived(slot, part):
        where = buf.at[block_rows(src[slot], part), pl.ds(0, 2 * HEAD)]
        pltpu.make_async_copy(where, where, recv.at[slot, part]).wait()

    def keep(slot):
        block = me if slot is None else src[slot]
        where = pl.ds(pl.multiple_of(block * rows, rows), rows)
        index = 15 if slot is None else slot
        source = kv_ref if slot is None else buf.at[where, pl.ds(0, 2 * HEAD)]
        return pltpu.make_async_copy(source, kvout_ref.at[where], local.at[index])

    def pass_on(slot):
        for part in range(PIECES):
            arrived(slot, part)
            for index, (from_slot, _, _) in enumerate(plan):
                if from_slot == slot:
                    plan_copy(index, part).start()
        keep(slot).start()

    def take(slot):
        for part in range(PIECES):
            arrived(slot, part)
        keep(slot).start()

    for part in range(PIECES):
        for index in range(4):
            plan_copy(index, part).start()
    own_copy = pltpu.make_async_copy(
        kv_ref,
        buf.at[pl.ds(pl.multiple_of(me * rows, rows), rows), pl.ds(0, 2 * HEAD)],
        local.at[16],
    )
    own_copy.start()
    keep(None).start()

    if with_w:
        wrows = w_ref.shape[0]
        wpiece = wrows // 4
        wown = pltpu.make_async_copy(w_ref, wfull_ref.at[ypos], wlocal.at[0])
        wown.start()

        wsrc = [ym, yp, y2]

        def wcopy(source_y, which, part, slot, target, lane, own=False):
            span = pl.ds((2 * which + part) * wpiece, wpiece)
            where = wfull_ref.at[source_y, span]
            return pltpu.make_async_remote_copy(
                src_ref=w_ref.at[span] if own else where,
                dst_ref=where,
                send_sem=wsend.at[lane, part],
                recv_sem=wrecv.at[slot, part],
                device_id=target,
                device_id_type=MESH,
            )

        def wfirst(part):
            return [
                wcopy(ypos, core, part, 0, {"mdl": yp}, 0, own=True),
                wcopy(ypos, core, part, 1, {"mdl": ym}, 1, own=True),
            ]

        def wrelay(part):
            if part == 0:
                return wcopy(ym, core, 0, 2, {"mdl": yp}, 2)
            return wcopy(yp, core, 1, 2, {"mdl": ym}, 2)

        def wshare(slot, part):
            return wcopy(wsrc[slot], core, part, 3 + slot, {"rep": other}, 3 + slot)

        def warrived(slot, part):
            which = core if slot < 3 else 1 - core
            span = pl.ds((2 * which + part) * wpiece, wpiece)
            where = wfull_ref.at[wsrc[slot % 3], span]
            pltpu.make_async_copy(where, where, wrecv.at[slot, part]).wait()

        for part in range(2):
            for copy in wfirst(part):
                copy.start()

    total = total_ref[0]
    key_index = lax.broadcasted_iota(jnp.int32, (all_keys, HEAD), 0)
    buf[:, 2 * HEAD :] = jnp.where(key_index < total, 1.0, 0.0).astype(BF)
    acc[...] = jnp.zeros_like(acc)
    own_copy.wait()

    chip_rows = 2 * rows
    zpos = me // 4

    def step(i, carry):
        @pl.when(i == 0)
        def _():
            take(7)

        @pl.when(i == 1)
        def _():
            pass_on(1)
            pass_on(0)
            take(9)

        @pl.when(i == 2)
        def _():
            pass_on(3)
            take(8)

        @pl.when(i == 3)
        def _():
            pass_on(2)
            take(10)

        @pl.when(i == 4)
        def _():
            pass_on(5)
            take(11)

        if with_w:

            @pl.when(i == 5)
            def _():
                for part in range(2):
                    warrived(0, part)
                    warrived(1, part)
                    wrelay(part).start()
                    wshare(0, part).start()
                    wshare(1, part).start()

        @pl.when(i == 5)
        def _():
            pass_on(4)
            take(13)

        @pl.when(i == 6)
        def _():
            pass_on(6)
            take(12)

        @pl.when(i == 7)
        def _():
            take(14)

        j = lax.rem(i, 4)
        dz = j + (j // 2) * (1 - 2 * lax.rem(j, 2))
        dx = i // 4
        chip = lax.rem(zpos + dz, 4) * 2 + lax.rem(xpos + dx, 2)
        span = pl.ds(pl.multiple_of(chip * chip_rows, chip_rows), chip_rows)
        scores = lax.dot_general(
            q_ref[...],
            buf[span, :HEAD],
            (((1,), (1,)), ((), ())),
            preferred_element_type=F32,
        )
        weights = jnp.exp2(scores).astype(BF)
        acc[...] += jnp.dot(weights, buf[span, HEAD:], preferred_element_type=F32)
        return carry

    lax.fori_loop(0, 8, step, 0)

    if with_w:
        for part in range(2):
            warrived(2, part)
            wshare(2, part).start()

    for head in range(heads):
        part = acc[head * rows : (head + 1) * rows, :]
        sums = part[:, HEAD:]
        out_ref[:, head * HEAD : (head + 1) * HEAD] = (part[:, :HEAD] / sums).astype(BF)
        low = jnp.min(sums, axis=0, keepdims=True)
        high = jnp.max(sums, axis=0, keepdims=True)
        sums_ref[2 * head : 2 * head + 1, :] = low
        sums_ref[2 * head + 1 : 2 * head + 2, :] = high

    if with_w:
        for slot in range(3, 6):
            for part in range(2):
                warrived(slot, part)
        for part in range(2):
            for copy in wfirst(part):
                copy.wait_send()
            wrelay(part).wait_send()
            for slot in range(3):
                wshare(slot, part).wait_send()
        wown.wait()
    for part in range(PIECES):
        for index in range(len(plan)):
            plan_copy(index, part).wait_send()
    keep(None).wait()
    for slot in range(15):
        keep(slot).wait()


def attend_call(total, queries, keyval, w, ident):
    heads = queries.shape[0] // keyval.shape[0]
    rows = keyval.shape[0]
    keys = rows * 16
    vmem = pl.BlockSpec(memory_space=pltpu.VMEM)
    anywhere = pl.BlockSpec(memory_space=pl.ANY)
    out_shape = [
        jax.ShapeDtypeStruct((rows, heads * HEAD), BF),
        jax.ShapeDtypeStruct((2 * heads, HEAD), F32),
        jax.ShapeDtypeStruct((keys, 2 * HEAD), BF),
    ]
    out_specs = [vmem, vmem, anywhere]
    in_specs = [pl.BlockSpec(memory_space=pltpu.SMEM), vmem, vmem]
    args = [total, queries, keyval]
    scratch = [
        pltpu.VMEM((keys, 3 * HEAD), BF),
        pltpu.VMEM((heads * rows, 2 * HEAD), F32),
        pltpu.SemaphoreType.DMA((15, PIECES)),
        pltpu.SemaphoreType.DMA((15, PIECES)),
        pltpu.SemaphoreType.DMA((17,)),
    ]
    if w is not None:
        out_shape.append(jax.ShapeDtypeStruct((4,) + w.shape, BF))
        out_specs.append(anywhere)
        in_specs.append(anywhere)
        args.append(w)
        scratch += [
            pltpu.SemaphoreType.DMA((6, 2)),
            pltpu.SemaphoreType.DMA((6, 2)),
            pltpu.SemaphoreType.DMA((1,)),
        ]
    return pl.pallas_call(
        functools.partial(attend_kernel, heads, w is not None),
        out_shape=out_shape,
        in_specs=in_specs,
        out_specs=out_specs,
        scratch_shapes=scratch,
        compiler_params=pltpu.CompilerParams(
            collective_id=ident, has_side_effects=True, vmem_limit_bytes=48 * 2**20
        ),
        cost_estimate=pl.CostEstimate(
            flops=4 * heads * rows * keys * HEAD,
            bytes_accessed=keys * 4 * HEAD,
            transcendentals=heads * rows * keys,
        ),
    )(*args)


def careful_kernel(total_ref, q_ref, kv_ref, out_ref, top, acc, total_sum):
    step = pl.program_id(0)
    block = kv_ref.shape[0]

    @pl.when(step == 0)
    def _():
        top[...] = jnp.full_like(top, masked_score)
        acc[...] = jnp.zeros_like(acc)
        total_sum[...] = jnp.zeros_like(total_sum)

    scores = lax.dot_general(
        q_ref[...], kv_ref[:, :HEAD], (((1,), (1,)), ((), ())), preferred_element_type=F32
    )
    key_index = step * block + lax.broadcasted_iota(jnp.int32, scores.shape, 1)
    live = key_index < total_ref[0]
    scores = jnp.where(live, scores, masked_score)
    old = top[...]
    new = jnp.maximum(old, jnp.max(scores, axis=1, keepdims=True))
    top[...] = new
    rescale = jnp.exp2(old - new)
    weights = jnp.where(live, jnp.exp2(scores - new[:, :1]), 0.0)
    total_sum[...] = total_sum[...] * rescale + jnp.sum(weights, axis=1, keepdims=True)
    acc[...] = acc[...] * rescale + jnp.dot(
        weights.astype(BF), kv_ref[:, HEAD:], preferred_element_type=F32
    )

    @pl.when(step == pl.num_programs(0) - 1)
    def _():
        rows, width = out_ref.shape
        for head in range(width // HEAD):
            span = slice(head * rows, (head + 1) * rows)
            out_ref[:, head * HEAD : (head + 1) * HEAD] = (acc[span, :] / total_sum[span, :]).astype(
                BF
            )


def careful_call(total, queries, kv_full, rows):
    heads = queries.shape[0] // rows
    block = 512
    return pl.pallas_call(
        careful_kernel,
        out_shape=jax.ShapeDtypeStruct((rows, heads * HEAD), BF),
        grid=(kv_full.shape[0] // block,),
        in_specs=[
            pl.BlockSpec(memory_space=pltpu.SMEM),
            pl.BlockSpec(queries.shape, lambda i: (0, 0)),
            pl.BlockSpec((block, 2 * HEAD), lambda i: (i, 0)),
        ],
        out_specs=pl.BlockSpec((rows, heads * HEAD), lambda i: (0, 0)),
        scratch_shapes=[pltpu.VMEM((heads * rows, HEAD), F32)] * 3,
        compiler_params=pltpu.CompilerParams(vmem_limit_bytes=48 * 2**20),
    )(total, queries, kv_full)


def attend(total, queries, keyval, w, ident):
    results = attend_call(total, queries, keyval, w, ident)
    plain, sums, kv_full = results[:3]
    safe = jnp.all((sums > sum_low) & (sums < sum_high))
    attended = lax.cond(
        safe,
        lambda: plain,
        lambda: careful_call(total, queries, kv_full, keyval.shape[0]),
    )
    return attended if w is None else (attended, results[3])


class YGather:
    def __init__(self, own_half, place, send, recv):
        self.ypos = lax.axis_index("mdl")
        self.yp = lax.rem(self.ypos + 1, 4)
        self.ym = lax.rem(self.ypos + 3, 4)
        self.y2 = lax.rem(self.ypos + 2, 4)
        self.own_half, self.place, self.send, self.recv = own_half, place, send, recv

    def greet(self, barrier):
        for peer in (self.yp, self.ym):
            pl.semaphore_signal(barrier, inc=1, device_id={"mdl": peer}, device_id_type=MESH)
        return 2

    def copy(self, source_y, part, slot, target, lane, own=False):
        return pltpu.make_async_remote_copy(
            src_ref=self.own_half(part) if own else self.place(source_y, part, lane - 2),
            dst_ref=self.place(source_y, part, slot),
            send_sem=self.send.at[lane, part],
            recv_sem=self.recv.at[slot, part],
            device_id={"mdl": target},
            device_id_type=MESH,
        )

    def first(self):
        return [
            self.copy(self.ypos, 0, 0, self.yp, 0, own=True),
            self.copy(self.ypos, 1, 1, self.ym, 1, own=True),
            self.copy(self.ypos, 1, 0, self.yp, 0, own=True),
            self.copy(self.ypos, 0, 1, self.ym, 1, own=True),
        ]

    def start(self):
        for item in self.first():
            item.start()

    def arrived(self, slot, part):
        where = self.place((self.ym, self.yp, self.y2)[slot], part, slot)
        pltpu.make_async_copy(where, where, self.recv.at[slot, part]).wait()

    def relay(self, part):
        if part == 0:
            return self.copy(self.ym, 0, 2, self.yp, 2)
        return self.copy(self.yp, 1, 2, self.ym, 3)

    def pass_on(self, part):
        self.arrived(part, part)
        self.relay(part).start()

    def wait_sent(self):
        for item in self.first():
            item.wait_send()
        for part in range(2):
            self.relay(part).wait_send()


def gather_kernel(x_ref, out_ref, send, recv, local):
    rows, width = x_ref.shape
    half = rows // 2

    def place(source_y, part, slot):
        return out_ref.at[
            pl.ds(part * half, half), pl.ds(pl.multiple_of(source_y * width, HEAD), width)
        ]

    ring = YGather(lambda part: x_ref.at[pl.ds(part * half, half)], place, send, recv)
    barrier = pltpu.get_barrier_semaphore()
    pl.semaphore_wait(barrier, ring.greet(barrier))
    ring.start()
    mine = pltpu.make_async_copy(
        x_ref, out_ref.at[:, pl.ds(pl.multiple_of(ring.ypos * width, HEAD), width)], local.at[0]
    )
    mine.start()
    ring.pass_on(0)
    ring.pass_on(1)
    ring.arrived(0, 1)
    ring.arrived(1, 0)
    ring.arrived(2, 0)
    ring.arrived(2, 1)
    ring.wait_sent()
    mine.wait()


def gather_columns(x, ident):
    vmem = pl.BlockSpec(memory_space=pltpu.VMEM)
    return pl.pallas_call(
        gather_kernel,
        out_shape=jax.ShapeDtypeStruct((x.shape[0], 4 * x.shape[1]), x.dtype),
        in_specs=[vmem],
        out_specs=vmem,
        scratch_shapes=[
            pltpu.SemaphoreType.DMA((4, 2)),
            pltpu.SemaphoreType.DMA((3, 2)),
            pltpu.SemaphoreType.DMA((1,)),
        ],
        compiler_params=pltpu.CompilerParams(
            collective_id=ident, has_side_effects=True, vmem_limit_bytes=8 * 2**20
        ),
    )(x)


class Geometry:
    def __init__(self, rows, columns, by_rows):
        self.by_rows = by_rows
        self.rows, self.columns = rows, columns
        if by_rows:
            self.half = (rows // 2, columns)
            self.quarter_shape = [(rows // 4, columns // 4)] * 2
            self.sub_shape = [(rows // 16, columns // 4)] * 2
        else:
            third = columns // 6
            self.half = (rows, columns // 2)
            self.quarter_shape = [(rows // 4, 2 * third), (rows // 4, third)]
            self.sub_shape = [(rows // 4, third // 2), (rows // 8, third // 2)]

    def whole(self, core):
        if self.by_rows:
            return (core * self.half[0], 0)
        return (0, core * self.half[1])

    def quarter(self, part, index):
        rows, columns = self.quarter_shape[part]
        if self.by_rows:
            return (part * rows, index * columns)
        return (index * rows, part * self.quarter_shape[0][1])

    def sub(self, part, index):
        rows, columns = self.sub_shape[part]
        if self.by_rows:
            return (index * rows, 0)
        if part == 0:
            return (0, index * columns)
        return ((index // 2) * rows, lax.rem(index, 2) * columns)

    def scratch(self):
        vmem = pltpu.VMEM
        shapes = [vmem(self.half, BF)] * 3
        for part in range(2):
            shapes.append(vmem((3,) + self.quarter_shape[part], BF))
            shapes.append(vmem(self.quarter_shape[part], BF))
            shapes.append(vmem((3,) + self.sub_shape[part], BF))
        dma = pltpu.SemaphoreType.DMA
        return shapes + [dma((4, 2, 3)), dma((4, 2, 3)), dma((9,)), dma((9,))]


def box(start, shape):
    row, column = start
    return (
        pl.ds(row if isinstance(row, int) else pl.multiple_of(row, 16), shape[0]),
        pl.ds(column if isinstance(column, int) else pl.multiple_of(column, HEAD), shape[1]),
    )


def plus(left, right):
    return (left[0] + right[0], left[1] + right[1])


class Reduce:
    hops = (2, 1, 3)

    def __init__(self, shape, att_ref, d_ref, out_ref, scratch):
        self.g = shape
        self.att, self.d, self.out = att_ref, d_ref, out_ref
        self.theirs, self.mine, self.got = scratch[:3]
        self.part_in = [scratch[3], scratch[6]]
        self.part_sum = [scratch[4], scratch[7]]
        self.sub_in = [scratch[5], scratch[8]]
        self.send, self.recv, self.csend, self.crecv = scratch[9:13]
        me = lax.axis_index("rep")
        self.me = me
        self.core = lax.rem(me, 2)
        self.other = me + 1 - 2 * self.core
        self.zpos = me // 4
        self.xpos = lax.rem(me // 2, 2) * 2 + lax.axis_index("sec")
        self.first = [self.xpos, self.zpos]
        self.second = [self.zpos, self.xpos]
        self.near = [self.at_x, self.at_z]

    def at_x(self, k):
        there = lax.rem(self.xpos + k, 4)
        return {"rep": self.zpos * 4 + (there // 2) * 2 + self.core, "sec": lax.rem(there, 2)}

    def at_z(self, k):
        return {"rep": lax.rem(self.me + 4 * k, 16)}

    def greet(self, barrier):
        for k in range(1, 4):
            pl.semaphore_signal(barrier, inc=1, device_id=self.at_x(k), device_id_type=MESH)
            pl.semaphore_signal(barrier, inc=1, device_id=self.at_z(k), device_id_type=MESH)
        pl.semaphore_signal(barrier, inc=1, device_id={"rep": self.other}, device_id_type=MESH)
        return 7

    def grad(self, which):
        left, right = self.att, self.d
        if self.g.by_rows:
            size = self.g.half[0]
            left = left[:, pl.ds(pl.multiple_of(which * size, size), size)]
            right = right[...]
        else:
            size = self.g.half[1]
            left = left[...]
            right = right[:, pl.ds(pl.multiple_of(which * size, HEAD), size)]
        return lax.dot_general(left, right, (((0,), (0,)), ((), ())), preferred_element_type=F32)

    def copy(self, source, target, send, recv, device):
        return pltpu.make_async_remote_copy(
            src_ref=source,
            dst_ref=target,
            send_sem=send,
            recv_sem=recv,
            device_id=device,
            device_id_type=MESH,
        )

    def swap(self):
        return self.copy(
            self.theirs, self.got, self.csend.at[0], self.crecv.at[0], {"rep": self.other}
        )

    def stage(self, level, part, k, source, target, device):
        return self.copy(
            source,
            target,
            self.send.at[level, part, k - 1],
            self.recv.at[level, part, k - 1],
            device,
        )

    def scatter_one(self, part, k):
        start = self.g.quarter(part, lax.rem(self.first[part] + k, 4))
        return self.stage(
            0,
            part,
            k,
            self.mine.at[box(start, self.g.quarter_shape[part])],
            self.part_in[part].at[k - 1],
            self.near[part](k),
        )

    def scatter_two(self, part, k):
        start = self.g.sub(part, lax.rem(self.second[part] + k, 4))
        return self.stage(
            1,
            part,
            k,
            self.part_sum[part].at[box(start, self.g.sub_shape[part])],
            self.sub_in[part].at[k - 1],
            self.near[1 - part](k),
        )

    def my_sub(self, part):
        start = plus(
            self.g.whole(self.core),
            plus(self.g.quarter(part, self.first[part]), self.g.sub(part, self.second[part])),
        )
        return box(start, self.g.sub_shape[part])

    def out_quarter(self, core, part, index):
        start = plus(self.g.whole(core), self.g.quarter(part, index))
        return self.out.at[box(start, self.g.quarter_shape[part])]

    def gather_two(self, part, k):
        where = self.out.at[self.my_sub(part)]
        return self.stage(2, part, k, where, where, self.near[1 - part](k))

    def gather_one(self, part, k):
        where = self.out_quarter(self.core, part, self.first[part])
        return self.stage(3, part, k, where, where, self.near[part](k))

    def share(self, part, k, core):
        where = self.out_quarter(core, part, lax.rem(self.first[part] + 4 - k, 4))
        index = 1 + part * 4 + k
        return self.copy(
            where, where, self.csend.at[index], self.crecv.at[index], {"rep": self.other}
        )

    def begin(self):
        self.theirs[...] = self.grad(1 - self.core).astype(BF)

    def swap_and_scatter(self):
        self.swap().start()
        own = self.grad(self.core)
        self.swap().wait_recv()
        self.mine[...] = (own + self.got[...].astype(F32)).astype(BF)
        for k in self.hops:
            for part in range(2):
                self.scatter_one(part, k).start()

    def second_scatter(self):
        for part in range(2):
            start = self.g.quarter(part, self.first[part])
            total = self.mine[box(start, self.g.quarter_shape[part])].astype(F32)
            for k in (1, 3, 2):
                self.scatter_one(part, k).wait_recv()
                total += self.part_in[part][k - 1].astype(F32)
            self.part_sum[part][...] = total.astype(BF)
            for k in self.hops:
                self.scatter_two(part, k).start()

    def first_gather(self):
        for part in range(2):
            start = self.g.sub(part, self.second[part])
            total = self.part_sum[part][box(start, self.g.sub_shape[part])].astype(F32)
            for k in (1, 3, 2):
                self.scatter_two(part, k).wait_recv()
                total += self.sub_in[part][k - 1].astype(F32)
            self.out[self.my_sub(part)] = total.astype(BF)
            for k in self.hops:
                self.gather_two(part, k).start()

    def second_gather(self):
        for part in range(2):
            for k in range(1, 4):
                self.gather_two(part, k).wait_recv()
            for k in self.hops:
                self.gather_one(part, k).start()
            self.share(part, 0, self.core).start()

    def last_shares(self):
        for k in (1, 3, 2):
            for part in range(2):
                self.gather_one(part, k).wait_recv()
                self.share(part, k, self.core).start()

    def finish(self):
        for part in range(2):
            for k in range(4):
                self.share(part, k, 1 - self.core).wait_recv()
        self.swap().wait_send()
        for part in range(2):
            for k in range(1, 4):
                self.scatter_one(part, k).wait_send()
                self.scatter_two(part, k).wait_send()
                self.gather_two(part, k).wait_send()
                self.gather_one(part, k).wait_send()
            for k in range(4):
                self.share(part, k, self.core).wait_send()


def reduce_kernel(shape, att_ref, d_ref, out_ref, *scratch):
    work = Reduce(shape, att_ref, d_ref, out_ref, scratch)
    barrier = pltpu.get_barrier_semaphore()
    expected = work.greet(barrier)
    work.begin()
    pl.semaphore_wait(barrier, expected)
    work.swap_and_scatter()
    work.second_scatter()
    work.first_gather()
    work.second_gather()
    work.last_shares()
    work.finish()


def reduced_grad(attended, grad_in, ident):
    shape = Geometry(attended.shape[1], grad_in.shape[1], True)
    vmem = pl.BlockSpec(memory_space=pltpu.VMEM)
    return pl.pallas_call(
        functools.partial(reduce_kernel, shape),
        out_shape=jax.ShapeDtypeStruct((shape.rows, shape.columns), BF),
        in_specs=[vmem, vmem],
        out_specs=vmem,
        scratch_shapes=shape.scratch(),
        compiler_params=pltpu.CompilerParams(
            collective_id=ident, has_side_effects=True, vmem_limit_bytes=24 * 2**20
        ),
    )(attended, grad_in)


def output_kernel(shape, x_ref, w_ref, base_ref, *refs):
    if shape is None:
        out_ref, acc, blocks, send, recv = refs
        work = None
    else:
        att_ref, d_ref, out_ref, grad_ref, acc, blocks, send, recv = refs[:8]
        work = Reduce(shape, att_ref, d_ref, grad_ref, refs[8:])
    rows = x_ref.shape[0]
    half = rows // 2
    ring = YGather(
        lambda part: x_ref.at[pl.ds(part * half, half)],
        lambda source_y, part, slot: blocks.at[slot, pl.ds(part * half, half)],
        send,
        recv,
    )
    barrier = pltpu.get_barrier_semaphore()
    expected = ring.greet(barrier)
    if work is not None:
        expected += work.greet(barrier)
    pl.semaphore_wait(barrier, expected)
    ring.start()
    if work is not None:
        work.begin()
        work.swap_and_scatter()
    acc[...] = base_ref[...].astype(F32) + jnp.dot(
        x_ref[...], w_ref[ring.ypos], preferred_element_type=F32
    )

    def add(slot, part):
        source_y = (ring.ym, ring.yp, ring.y2)[slot]
        span = pl.ds(part * half, half)
        acc[span, :] += jnp.dot(
            blocks[slot, span, :], w_ref[source_y], preferred_element_type=F32
        )

    ring.pass_on(0)
    ring.pass_on(1)
    add(0, 0)
    add(1, 1)
    if work is not None:
        work.second_scatter()
    ring.arrived(0, 1)
    add(0, 1)
    if work is not None:
        work.first_gather()
    ring.arrived(1, 0)
    add(1, 0)
    if work is not None:
        work.second_gather()
    ring.arrived(2, 0)
    add(2, 0)
    ring.arrived(2, 1)
    add(2, 1)
    out_ref[...] = acc[...].astype(out_ref.dtype)
    if work is not None:
        work.last_shares()
        work.finish()
    ring.wait_sent()


def output_call(x, w_full, base, out_type, grads, ident):
    rows, width = x.shape
    columns = w_full.shape[2]
    vmem = pl.BlockSpec(memory_space=pltpu.VMEM)
    args = [x, w_full, base]
    out_shape = [jax.ShapeDtypeStruct((rows, columns), out_type)]
    scratch = [
        pltpu.VMEM((rows, columns), F32),
        pltpu.VMEM((3, rows, width), BF),
        pltpu.SemaphoreType.DMA((4, 2)),
        pltpu.SemaphoreType.DMA((3, 2)),
    ]
    shape = None
    if grads is not None:
        shape = Geometry(grads[0].shape[1], grads[1].shape[1], False)
        args += list(grads)
        out_shape.append(jax.ShapeDtypeStruct((shape.rows, shape.columns), BF))
        scratch += shape.scratch()
    return pl.pallas_call(
        functools.partial(output_kernel, shape),
        out_shape=out_shape,
        in_specs=[vmem] * len(args),
        out_specs=[vmem] * len(out_shape),
        scratch_shapes=scratch,
        compiler_params=pltpu.CompilerParams(
            collective_id=ident, has_side_effects=True, vmem_limit_bytes=48 * 2**20
        ),
    )(*args)


def project(source, w_query, w_keyval, live_mask):
    rows = source.shape[0]
    normed = rms_normed(source).astype(BF)
    queries = (
        jnp.dot(normed, w_query, preferred_element_type=F32) * (HEAD ** (-0.5) * LOG2E)
    ).astype(BF)
    heads = queries.shape[1] // HEAD
    stacked = jnp.transpose(queries.reshape(rows, heads, HEAD), (1, 0, 2)).reshape(
        heads * rows, HEAD
    )
    keyval = [jnp.dot(normed, w_keyval[part], preferred_element_type=F32) for part in range(2)]
    joined = jnp.where(live_mask[:, None], jnp.concatenate(keyval, axis=1), 0.0).astype(BF)
    return (stacked, joined)


def on_device(
    obs,
    a_query,
    a_keyval,
    a_out,
    w_policy,
    c_in,
    c_query,
    c_keyval,
    c_out,
    w_value,
    actions,
    advantages,
    old_logp,
    returns,
    robot_count,
):
    row_count = obs.shape[1]
    batch_index = lax.axis_index("sec")
    robot_total = robot_count[batch_index]
    total = robot_total.reshape(1)
    live_total = jnp.sum(robot_count).astype(F32)
    first_row = lax.axis_index("rep") * row_count
    live_mask = first_row + lax.iota(jnp.int32, row_count) < robot_total
    mdl_count = lax.axis_size("mdl")
    part_rows = row_count // mdl_count
    row_start = lax.axis_index("mdl") * part_rows
    obs_float = obs[0].astype(F32)

    queries, keyval = project(obs_float, a_query, a_keyval, live_mask)
    attended, a_out_full = attend(total, queries, keyval, a_out, 1)
    (hidden,) = output_call(attended, a_out_full, obs[0], BF, None, 3)
    embed_part = jnp.dot(hidden, c_in, preferred_element_type=F32).astype(BF)
    embedded = gather_columns(embed_part, 4)
    dhidden = policy_backward(
        hidden, actions[0], advantages[0], old_logp[0], live_mask, live_total, w_policy
    ).astype(BF)
    embed_float = embedded.astype(F32)
    critic_queries, critic_keyval = project(embed_float, c_query, c_keyval, live_mask)
    critic_attended, c_out_full = attend(total, critic_queries, critic_keyval, c_out, 2)
    mixed, actor_summed = output_call(
        critic_attended, c_out_full, embedded, F32, (attended, dhidden), 5
    )
    value_pred, dmixed = value_backward(mixed, returns[0], live_mask, live_total, w_value)
    value_part = lax.dynamic_slice_in_dim(value_pred, row_start, part_rows, 0)
    critic_summed = reduced_grad(critic_attended, dmixed.astype(BF), 6).astype(F32)
    return (value_part[None, :], actor_summed.astype(F32), critic_summed)


def solution(mesh):
    return jax.shard_map(
        on_device,
        mesh=mesh,
        in_specs=(
            P("sec", "rep", None),
            P(None, "mdl"),
            P(None, None, "mdl"),
            P("mdl", None),
            P(),
            P(None, "mdl"),
            P(None, "mdl"),
            P(None, None, "mdl"),
            P("mdl", None),
            P(),
            P("sec", "rep"),
            P("sec", "rep"),
            P("sec", "rep"),
            P("sec", "rep"),
            P(),
        ),
        out_specs=(P("sec", ("rep", "mdl")), P("mdl", None), P("mdl", None)),
        check_vma=False,
    )
```

```python
import functools

import jax
import jax.numpy as jnp
from jax import lax
from jax.experimental import pallas as pl
from jax.experimental.pallas import tpu as pltpu
from jax.sharding import PartitionSpec as P

HEAD = 128
LOG2E = 1.4426950408889634
MESH = pl.DeviceIdType.MESH
BF = jnp.bfloat16
F32 = jnp.float32

epsilon = 1e-05
clip_range = 0.2
masked_score = -1e30
sum_low = 1e-20
sum_high = 1e25


def rms_normed(values_in):
    return values_in * lax.rsqrt(jnp.mean(values_in * values_in, axis=-1, keepdims=True) + epsilon)


def norm_backward(source, normed, grad_in):
    factor = lax.rsqrt(jnp.mean(source * source, axis=-1, keepdims=True) + epsilon)
    return factor * (grad_in - normed * jnp.mean(grad_in * normed, axis=-1, keepdims=True))


def policy_backward(hidden, side, w_policy):
    source = hidden.astype(F32)
    factor = lax.rsqrt(jnp.mean(source * source, axis=-1, keepdims=True) + epsilon)
    normed = source * factor
    logits = jnp.dot(normed.astype(BF), w_policy, preferred_element_type=F32)
    shifted = logits - jnp.max(logits, axis=-1, keepdims=True)
    log_probs = shifted - jnp.log(jnp.sum(jnp.exp(shifted), axis=-1, keepdims=True))
    action, advantage, old_values, scale = (side[:, k : k + 1] for k in range(4))
    command = lax.broadcasted_iota(jnp.int32, logits.shape, 1).astype(F32)
    onehot = (action == command).astype(F32)
    chosen = jnp.sum(onehot * log_probs, axis=-1, keepdims=True)
    prob_ratio = jnp.exp(chosen - old_values)
    plain_term = prob_ratio * advantage
    bounded = jnp.clip(prob_ratio, 1.0 - clip_range, 1.0 + clip_range) * advantage
    slope_term = jnp.where((scale > 0.0) & (plain_term <= bounded), -plain_term * scale, 0.0)
    dlogits = slope_term * (onehot - jnp.exp(log_probs))
    dnormed = lax.dot_general(
        dlogits.astype(BF), w_policy, (((1,), (1,)), ((), ())), preferred_element_type=F32
    )
    return factor * (dnormed - normed * jnp.mean(dnormed * normed, axis=-1, keepdims=True))


def value_backward(mixed_out, target, live_mask, live_total, w_value):
    normed = rms_normed(mixed_out)
    value_pred = jnp.dot(normed.astype(BF), w_value, preferred_element_type=F32)
    slope_term = jnp.where(live_mask, value_pred - target, jnp.float32(0.0)) / live_total
    dnormed = slope_term[:, None] * w_value.astype(F32)[None, :]
    return (value_pred, norm_backward(mixed_out, normed, dnormed))


PIECES = 2


def attend_kernel(
    heads, count_ref, x_ref, wq_ref, wkv_ref, w_ref, out_ref, sums_ref, kvout_ref, wfull_ref, *refs
):
    buf, acc, q_ref, kv_ref, send, recv, local, wsend, wrecv, wlocal = refs
    rows = x_ref.shape[0]
    piece = rows // PIECES
    all_keys = buf.shape[0]
    me = lax.axis_index("rep")
    count = 16
    core = lax.rem(me, 2)
    xpos = lax.rem(me // 2, 2)
    other = me + 1 - 2 * core
    xpeer = me + 2 - 4 * xpos
    zp = lax.rem(me + 4, count)
    zm = lax.rem(me + 12, count)
    src = [
        zm,
        zp,
        lax.rem(me + 8, count),
        xpeer,
        lax.rem(xpeer + 12, count),
        lax.rem(xpeer + 4, count),
        lax.rem(xpeer + 8, count),
    ]
    src = src + [other] + [s + 1 - 2 * core for s in src]

    ypos = lax.axis_index("mdl")
    yp = lax.rem(ypos + 1, 4)
    ym = lax.rem(ypos + 3, 4)
    y2 = lax.rem(ypos + 2, 4)

    barrier = pltpu.get_barrier_semaphore()
    peers = [{"rep": zp}, {"rep": zm}, {"rep": xpeer}, {"rep": other}]
    peers += [{"mdl": yp}, {"mdl": ym}]
    for peer in peers:
        pl.semaphore_signal(barrier, inc=1, device_id=peer, device_id_type=MESH)

    total = count_ref[lax.axis_index("sec")]
    normed = rms_normed(x_ref[...].astype(F32)).astype(BF)
    live = me * rows + lax.broadcasted_iota(jnp.int32, (rows, HEAD), 0) < total
    for part in range(2):
        made = jnp.dot(normed, wkv_ref[part], preferred_element_type=F32)
        kv_ref[:, part * HEAD : (part + 1) * HEAD] = jnp.where(live, made, 0.0).astype(BF)
    pl.semaphore_wait(barrier, len(peers))

    def block_rows(block, part):
        return pl.ds(pl.multiple_of(block * rows + part * piece, piece), piece)

    def transfer(block, part, slot, target, lane, own=False):
        where = buf.at[block_rows(block, part), pl.ds(0, 2 * HEAD)]
        source = kv_ref.at[pl.ds(part * piece, piece)] if own else where
        return pltpu.make_async_remote_copy(
            src_ref=source,
            dst_ref=where,
            send_sem=send.at[lane, part],
            recv_sem=recv.at[slot, part],
            device_id={"rep": target},
            device_id_type=MESH,
        )

    plan = [
        (None, 3, xpeer),
        (None, 1, zm),
        (None, 0, zp),
        (None, 7, other),
        (1, 9, other),
        (0, 2, zp),
        (0, 8, other),
        (3, 5, zm),
        (3, 4, zp),
        (3, 11, other),
        (2, 10, other),
        (5, 6, zm),
        (5, 13, other),
        (4, 12, other),
        (6, 14, other),
    ]

    def plan_copy(index, part):
        from_slot, to_slot, target = plan[index]
        block = me if from_slot is None else src[from_slot]
        return transfer(block, part, to_slot, target, index, own=from_slot is None)

    def arrived(slot, part):
        where = buf.at[block_rows(src[slot], part), pl.ds(0, 2 * HEAD)]
        pltpu.make_async_copy(where, where, recv.at[slot, part]).wait()

    def keep(slot):
        block = me if slot is None else src[slot]
        where = pl.ds(pl.multiple_of(block * rows, rows), rows)
        index = 15 if slot is None else slot
        source = kv_ref if slot is None else buf.at[where, pl.ds(0, 2 * HEAD)]
        return pltpu.make_async_copy(source, kvout_ref.at[where], local.at[index])

    def pass_on(slot):
        for part in range(PIECES):
            arrived(slot, part)
            for index, (from_slot, _, _) in enumerate(plan):
                if from_slot == slot:
                    plan_copy(index, part).start()
        keep(slot).start()

    def take(slot):
        for part in range(PIECES):
            arrived(slot, part)
        keep(slot).start()

    for part in range(PIECES):
        for index in range(4):
            plan_copy(index, part).start()
    own_copy = pltpu.make_async_copy(
        kv_ref,
        buf.at[pl.ds(pl.multiple_of(me * rows, rows), rows), pl.ds(0, 2 * HEAD)],
        local.at[16],
    )
    own_copy.start()
    keep(None).start()

    wrows = w_ref.shape[0]
    wpiece = wrows // 4
    wown = pltpu.make_async_copy(w_ref, wfull_ref.at[ypos], wlocal.at[0])
    wown.start()

    wsrc = [ym, yp, y2]

    def wcopy(source_y, which, part, slot, target, lane, own=False):
        span = pl.ds((2 * which + part) * wpiece, wpiece)
        where = wfull_ref.at[source_y, span]
        return pltpu.make_async_remote_copy(
            src_ref=w_ref.at[span] if own else where,
            dst_ref=where,
            send_sem=wsend.at[lane, part],
            recv_sem=wrecv.at[slot, part],
            device_id=target,
            device_id_type=MESH,
        )

    def wfirst(part):
        return [
            wcopy(ypos, core, part, 0, {"mdl": yp}, 0, own=True),
            wcopy(ypos, core, part, 1, {"mdl": ym}, 1, own=True),
        ]

    def wrelay(part):
        if part == 0:
            return wcopy(ym, core, 0, 2, {"mdl": yp}, 2)
        return wcopy(yp, core, 1, 2, {"mdl": ym}, 2)

    def wshare(slot, part):
        return wcopy(wsrc[slot], core, part, 3 + slot, {"rep": other}, 3 + slot)

    def warrived(slot, part):
        which = core if slot < 3 else 1 - core
        span = pl.ds((2 * which + part) * wpiece, wpiece)
        where = wfull_ref.at[wsrc[slot % 3], span]
        pltpu.make_async_copy(where, where, wrecv.at[slot, part]).wait()

    for part in range(2):
        for copy in wfirst(part):
            copy.start()

    queries = jnp.dot(normed, wq_ref[...], preferred_element_type=F32) * (HEAD ** (-0.5) * LOG2E)
    for head in range(heads):
        q_ref[head * rows : (head + 1) * rows, :] = queries[
            :, head * HEAD : (head + 1) * HEAD
        ].astype(BF)
    key_index = lax.broadcasted_iota(jnp.int32, (all_keys, HEAD), 0)
    buf[:, 2 * HEAD :] = jnp.where(key_index < total, 1.0, 0.0).astype(BF)
    acc[...] = jnp.zeros_like(acc)
    own_copy.wait()

    chip_rows = 2 * rows
    zpos = me // 4

    def step(i, carry):
        @pl.when(i == 0)
        def _():
            take(7)

        @pl.when(i == 1)
        def _():
            pass_on(1)
            pass_on(0)
            take(9)

        @pl.when(i == 2)
        def _():
            pass_on(3)
            take(8)

        @pl.when(i == 3)
        def _():
            pass_on(2)
            take(10)

        @pl.when(i == 4)
        def _():
            pass_on(5)
            take(11)

        @pl.when(i == 5)
        def _():
            for part in range(2):
                warrived(0, part)
                warrived(1, part)
                wrelay(part).start()
                wshare(0, part).start()
                wshare(1, part).start()

        @pl.when(i == 5)
        def _():
            pass_on(4)
            take(13)

        @pl.when(i == 6)
        def _():
            pass_on(6)
            take(12)

        @pl.when(i == 7)
        def _():
            take(14)

        j = lax.rem(i, 4)
        dz = j + (j // 2) * (1 - 2 * lax.rem(j, 2))
        dx = i // 4
        chip = lax.rem(zpos + dz, 4) * 2 + lax.rem(xpos + dx, 2)
        span = pl.ds(pl.multiple_of(chip * chip_rows, chip_rows), chip_rows)
        scores = lax.dot_general(
            q_ref[...],
            buf[span, :HEAD],
            (((1,), (1,)), ((), ())),
            preferred_element_type=F32,
        )
        weights = jnp.exp2(scores).astype(BF)
        acc[...] += jnp.dot(weights, buf[span, HEAD:], preferred_element_type=F32)
        return carry

    lax.fori_loop(0, 8, step, 0)

    for part in range(2):
        warrived(2, part)
        wshare(2, part).start()

    for head in range(heads):
        part = acc[head * rows : (head + 1) * rows, :]
        sums = part[:, HEAD:]
        out_ref[:, head * HEAD : (head + 1) * HEAD] = (part[:, :HEAD] / sums).astype(BF)
        low = jnp.min(sums, axis=0, keepdims=True)
        high = jnp.max(sums, axis=0, keepdims=True)
        sums_ref[2 * head : 2 * head + 1, :] = low
        sums_ref[2 * head + 1 : 2 * head + 2, :] = high

    for slot in range(3, 6):
        for part in range(2):
            warrived(slot, part)
    for part in range(2):
        for copy in wfirst(part):
            copy.wait_send()
        wrelay(part).wait_send()
        for slot in range(3):
            wshare(slot, part).wait_send()
    wown.wait()
    for part in range(PIECES):
        for index in range(len(plan)):
            plan_copy(index, part).wait_send()
    keep(None).wait()
    for slot in range(15):
        keep(slot).wait()


def attend_call(counts, source, w_query, w_keyval, w, ident):
    heads = w_query.shape[1] // HEAD
    rows = source.shape[0]
    keys = rows * 16
    vmem = pl.BlockSpec(memory_space=pltpu.VMEM)
    hbm = pl.BlockSpec(memory_space=pltpu.HBM)
    return pl.pallas_call(
        functools.partial(attend_kernel, heads),
        out_shape=[
            jax.ShapeDtypeStruct((rows, heads * HEAD), BF),
            jax.ShapeDtypeStruct((2 * heads, HEAD), F32),
            pltpu.HBM((keys, 2 * HEAD), BF),
            pltpu.HBM((4,) + w.shape, BF),
        ],
        in_specs=[pl.BlockSpec(memory_space=pltpu.SMEM), vmem, vmem, vmem, hbm],
        out_specs=[vmem, vmem, hbm, hbm],
        scratch_shapes=[
            pltpu.VMEM((keys, 3 * HEAD), BF),
            pltpu.VMEM((heads * rows, 2 * HEAD), F32),
            pltpu.VMEM((heads * rows, HEAD), BF),
            pltpu.VMEM((rows, 2 * HEAD), BF),
            pltpu.SemaphoreType.DMA((15, PIECES)),
            pltpu.SemaphoreType.DMA((15, PIECES)),
            pltpu.SemaphoreType.DMA((17,)),
            pltpu.SemaphoreType.DMA((6, 2)),
            pltpu.SemaphoreType.DMA((6, 2)),
            pltpu.SemaphoreType.DMA((1,)),
        ],
        compiler_params=pltpu.CompilerParams(
            collective_id=ident, has_side_effects=True, vmem_limit_bytes=40 * 2**20
        ),
        cost_estimate=pl.CostEstimate(
            flops=4 * heads * rows * keys * HEAD,
            bytes_accessed=keys * 4 * HEAD,
            transcendentals=heads * rows * keys,
        ),
    )(counts, source, w_query, w_keyval, pltpu.with_memory_space_constraint(w, pltpu.HBM))


def careful_kernel(total_ref, q_ref, kv_ref, out_ref, top, acc, total_sum):
    step = pl.program_id(0)
    block = kv_ref.shape[0]

    @pl.when(step == 0)
    def _():
        top[...] = jnp.full_like(top, masked_score)
        acc[...] = jnp.zeros_like(acc)
        total_sum[...] = jnp.zeros_like(total_sum)

    scores = lax.dot_general(
        q_ref[...], kv_ref[:, :HEAD], (((1,), (1,)), ((), ())), preferred_element_type=F32
    )
    key_index = step * block + lax.broadcasted_iota(jnp.int32, scores.shape, 1)
    live = key_index < total_ref[0]
    scores = jnp.where(live, scores, masked_score)
    old = top[...]
    new = jnp.maximum(old, jnp.max(scores, axis=1, keepdims=True))
    top[...] = new
    rescale = jnp.exp2(old - new)
    weights = jnp.where(live, jnp.exp2(scores - new[:, :1]), 0.0)
    total_sum[...] = total_sum[...] * rescale + jnp.sum(weights, axis=1, keepdims=True)
    acc[...] = acc[...] * rescale + jnp.dot(
        weights.astype(BF), kv_ref[:, HEAD:], preferred_element_type=F32
    )

    @pl.when(step == pl.num_programs(0) - 1)
    def _():
        rows, width = out_ref.shape
        for head in range(width // HEAD):
            span = slice(head * rows, (head + 1) * rows)
            out_ref[:, head * HEAD : (head + 1) * HEAD] = (acc[span, :] / total_sum[span, :]).astype(
                BF
            )


def careful_call(total, queries, kv_full, rows):
    heads = queries.shape[0] // rows
    block = 256
    return pl.pallas_call(
        careful_kernel,
        out_shape=jax.ShapeDtypeStruct((rows, heads * HEAD), BF),
        grid=(kv_full.shape[0] // block,),
        in_specs=[
            pl.BlockSpec(memory_space=pltpu.SMEM),
            pl.BlockSpec(queries.shape, lambda i: (0, 0)),
            pl.BlockSpec((block, 2 * HEAD), lambda i: (i, 0)),
        ],
        out_specs=pl.BlockSpec((rows, heads * HEAD), lambda i: (0, 0)),
        scratch_shapes=[pltpu.VMEM((heads * rows, HEAD), F32)] * 3,
        compiler_params=pltpu.CompilerParams(vmem_limit_bytes=20 * 2**20),
    )(total, queries, kv_full)


def attend(counts, total, source, w_query, w_keyval, w, ident):
    plain, sums, kv_full, w_full = attend_call(counts, source, w_query, w_keyval, w, ident)
    safe = jnp.all((sums > sum_low) & (sums < sum_high))
    attended = lax.cond(
        safe,
        lambda: plain,
        lambda: careful_call(
            total, stacked_queries(source, w_query), kv_full, source.shape[0]
        ),
    )
    return (attended, w_full)


class YGather:
    def __init__(self, own_half, place, send, recv):
        self.ypos = lax.axis_index("mdl")
        self.yp = lax.rem(self.ypos + 1, 4)
        self.ym = lax.rem(self.ypos + 3, 4)
        self.y2 = lax.rem(self.ypos + 2, 4)
        self.own_half, self.place, self.send, self.recv = own_half, place, send, recv

    def greet(self, barrier):
        for peer in (self.yp, self.ym):
            pl.semaphore_signal(barrier, inc=1, device_id={"mdl": peer}, device_id_type=MESH)
        return 2

    def copy(self, source_y, part, slot, target, lane, own=False):
        return pltpu.make_async_remote_copy(
            src_ref=self.own_half(part) if own else self.place(source_y, part, lane - 2),
            dst_ref=self.place(source_y, part, slot),
            send_sem=self.send.at[lane, part],
            recv_sem=self.recv.at[slot, part],
            device_id={"mdl": target},
            device_id_type=MESH,
        )

    def first(self):
        return [
            self.copy(self.ypos, 0, 0, self.yp, 0, own=True),
            self.copy(self.ypos, 1, 1, self.ym, 1, own=True),
            self.copy(self.ypos, 1, 0, self.yp, 0, own=True),
            self.copy(self.ypos, 0, 1, self.ym, 1, own=True),
        ]

    def start(self):
        for item in self.first():
            item.start()

    def arrived(self, slot, part):
        where = self.place((self.ym, self.yp, self.y2)[slot], part, slot)
        pltpu.make_async_copy(where, where, self.recv.at[slot, part]).wait()

    def relay(self, part):
        if part == 0:
            return self.copy(self.ym, 0, 2, self.yp, 2)
        return self.copy(self.yp, 1, 2, self.ym, 3)

    def pass_on(self, part):
        self.arrived(part, part)
        self.relay(part).start()

    def wait_sent(self):
        for item in self.first():
            item.wait_send()
        for part in range(2):
            self.relay(part).wait_send()


class Geometry:
    def __init__(self, rows, columns, by_rows):
        self.by_rows = by_rows
        self.rows, self.columns = rows, columns
        if by_rows:
            self.half = (rows // 2, columns)
            self.quarter_shape = [(rows // 4, columns // 4)] * 2
            self.sub_shape = [(rows // 16, columns // 4)] * 2
        else:
            third = columns // 6
            self.half = (rows, columns // 2)
            self.quarter_shape = [(rows // 4, 2 * third), (rows // 4, third)]
            self.sub_shape = [(rows // 4, third // 2), (rows // 8, third // 2)]

    def whole(self, core):
        if self.by_rows:
            return (core * self.half[0], 0)
        return (0, core * self.half[1])

    def quarter(self, part, index):
        rows, columns = self.quarter_shape[part]
        if self.by_rows:
            return (part * rows, index * columns)
        return (index * rows, part * self.quarter_shape[0][1])

    def sub(self, part, index):
        rows, columns = self.sub_shape[part]
        if self.by_rows:
            return (index * rows, 0)
        if part == 0:
            return (0, index * columns)
        return ((index // 2) * rows, lax.rem(index, 2) * columns)

    def scatter_scratch(self):
        vmem = pltpu.VMEM
        return [vmem(self.half, BF)] * 3 + [vmem((3,) + q, BF) for q in self.quarter_shape]

    def sub_scratch(self):
        return [pltpu.VMEM((3,) + sub, BF) for sub in self.sub_shape]

    def semaphores(self):
        dma = pltpu.SemaphoreType.DMA
        return [dma((4, 2, 3)), dma((4, 2, 3)), dma((9,)), dma((9,))]


def box(start, shape):
    row, column = start
    return (
        pl.ds(row if isinstance(row, int) else pl.multiple_of(row, 16), shape[0]),
        pl.ds(column if isinstance(column, int) else pl.multiple_of(column, HEAD), shape[1]),
    )


def plus(left, right):
    return (left[0] + right[0], left[1] + right[1])


class Reduce:
    hops = (2, 1, 3)

    def __init__(self, shape, att_ref, d_ref, out_ref, scatter, sums, sub_in, semaphores):
        self.g = shape
        self.att, self.d, self.out = att_ref, d_ref, out_ref
        if scatter is not None:
            self.theirs, self.mine, self.got = scatter[:3]
            self.part_in = scatter[3:5]
        self.part_sum = sums
        self.sub_in = sub_in
        self.send, self.recv, self.csend, self.crecv = semaphores
        me = lax.axis_index("rep")
        self.me = me
        self.core = lax.rem(me, 2)
        self.other = me + 1 - 2 * self.core
        self.zpos = me // 4
        self.xpos = lax.rem(me // 2, 2) * 2 + lax.axis_index("sec")
        self.first = [self.xpos, self.zpos]
        self.second = [self.zpos, self.xpos]
        self.near = [self.at_x, self.at_z]

    def at_x(self, k):
        there = lax.rem(self.xpos + k, 4)
        return {"rep": self.zpos * 4 + (there // 2) * 2 + self.core, "sec": lax.rem(there, 2)}

    def at_z(self, k):
        return {"rep": lax.rem(self.me + 4 * k, 16)}

    def greet(self, barrier):
        for k in range(1, 4):
            pl.semaphore_signal(barrier, inc=1, device_id=self.at_x(k), device_id_type=MESH)
            pl.semaphore_signal(barrier, inc=1, device_id=self.at_z(k), device_id_type=MESH)
        pl.semaphore_signal(barrier, inc=1, device_id={"rep": self.other}, device_id_type=MESH)
        return 7

    def grad(self, which):
        left, right = self.att, self.d
        if self.g.by_rows:
            size = self.g.half[0]
            left = left[:, pl.ds(pl.multiple_of(which * size, size), size)]
            right = right[...]
        else:
            size = self.g.half[1]
            left = left[...]
            right = right[:, pl.ds(pl.multiple_of(which * size, HEAD), size)]
        return lax.dot_general(left, right, (((0,), (0,)), ((), ())), preferred_element_type=F32)

    def copy(self, source, target, send, recv, device):
        return pltpu.make_async_remote_copy(
            src_ref=source,
            dst_ref=target,
            send_sem=send,
            recv_sem=recv,
            device_id=device,
            device_id_type=MESH,
        )

    def swap(self):
        return self.copy(
            self.theirs, self.got, self.csend.at[0], self.crecv.at[0], {"rep": self.other}
        )

    def stage(self, level, part, k, source, target, device):
        return self.copy(
            source,
            target,
            self.send.at[level, part, k - 1],
            self.recv.at[level, part, k - 1],
            device,
        )

    def scatter_one(self, part, k):
        start = self.g.quarter(part, lax.rem(self.first[part] + k, 4))
        return self.stage(
            0,
            part,
            k,
            self.mine.at[box(start, self.g.quarter_shape[part])],
            self.part_in[part].at[k - 1],
            self.near[part](k),
        )

    def scatter_two(self, part, k):
        start = self.g.sub(part, lax.rem(self.second[part] + k, 4))
        return self.stage(
            1,
            part,
            k,
            self.part_sum[part].at[box(start, self.g.sub_shape[part])],
            self.sub_in[part].at[k - 1],
            self.near[1 - part](k),
        )

    def my_sub(self, part):
        start = plus(
            self.g.whole(self.core),
            plus(self.g.quarter(part, self.first[part]), self.g.sub(part, self.second[part])),
        )
        return box(start, self.g.sub_shape[part])

    def out_quarter(self, core, part, index):
        start = plus(self.g.whole(core), self.g.quarter(part, index))
        return self.out.at[box(start, self.g.quarter_shape[part])]

    def gather_two(self, part, k):
        where = self.out.at[self.my_sub(part)]
        return self.stage(2, part, k, where, where, self.near[1 - part](k))

    def gather_one(self, part, k):
        where = self.out_quarter(self.core, part, self.first[part])
        return self.stage(3, part, k, where, where, self.near[part](k))

    def share(self, part, k, core):
        where = self.out_quarter(core, part, lax.rem(self.first[part] + 4 - k, 4))
        index = 1 + part * 4 + k
        return self.copy(
            where, where, self.csend.at[index], self.crecv.at[index], {"rep": self.other}
        )

    def begin(self):
        self.theirs[...] = self.grad(1 - self.core).astype(BF)

    def swap_and_scatter(self):
        self.swap().start()
        own = self.grad(self.core)
        self.swap().wait_recv()
        self.mine[...] = (own + self.got[...].astype(F32)).astype(BF)
        for k in self.hops:
            for part in range(2):
                self.scatter_one(part, k).start()

    def first_sums(self):
        for part in range(2):
            start = self.g.quarter(part, self.first[part])
            total = self.mine[box(start, self.g.quarter_shape[part])].astype(F32)
            for k in (1, 3, 2):
                self.scatter_one(part, k).wait_recv()
                total += self.part_in[part][k - 1].astype(F32)
            self.part_sum[part][...] = total.astype(BF)

    def second_scatter(self):
        for k in self.hops:
            for part in range(2):
                self.scatter_two(part, k).start()

    def first_gather(self):
        for part in range(2):
            start = self.g.sub(part, self.second[part])
            total = self.part_sum[part][box(start, self.g.sub_shape[part])].astype(F32)
            for k in (1, 3, 2):
                self.scatter_two(part, k).wait_recv()
                total += self.sub_in[part][k - 1].astype(F32)
            self.out[self.my_sub(part)] = total.astype(BF)
            for k in self.hops:
                self.gather_two(part, k).start()

    def second_gather(self):
        for part in range(2):
            for k in range(1, 4):
                self.gather_two(part, k).wait_recv()
            for k in self.hops:
                self.gather_one(part, k).start()
            self.share(part, 0, self.core).start()

    def last_shares(self):
        for k in (1, 3, 2):
            for part in range(2):
                self.gather_one(part, k).wait_recv()
                self.share(part, k, self.core).start()

    def finish_scatter(self):
        self.swap().wait_send()
        for part in range(2):
            for k in range(1, 4):
                self.scatter_one(part, k).wait_send()

    def finish(self):
        for part in range(2):
            for k in range(4):
                self.share(part, k, 1 - self.core).wait_recv()
        for part in range(2):
            for k in range(1, 4):
                self.scatter_two(part, k).wait_send()
                self.gather_two(part, k).wait_send()
                self.gather_one(part, k).wait_send()
            for k in range(4):
                self.share(part, k, self.core).wait_send()


def reduce_kernel(shape, att_ref, d_ref, out_ref, *scratch):
    work = Reduce(
        shape, att_ref, d_ref, out_ref, scratch[:5], scratch[5:7], scratch[7:9], scratch[9:13]
    )
    barrier = pltpu.get_barrier_semaphore()
    expected = work.greet(barrier)
    work.begin()
    pl.semaphore_wait(barrier, expected)
    work.swap_and_scatter()
    work.first_sums()
    work.second_scatter()
    work.first_gather()
    work.second_gather()
    work.last_shares()
    work.finish_scatter()
    work.finish()


def reduced_grad(attended, grad_in, ident):
    shape = Geometry(attended.shape[1], grad_in.shape[1], True)
    vmem = pl.BlockSpec(memory_space=pltpu.VMEM)
    return pl.pallas_call(
        functools.partial(reduce_kernel, shape),
        out_shape=jax.ShapeDtypeStruct((shape.rows, shape.columns), BF),
        in_specs=[vmem, vmem],
        out_specs=vmem,
        scratch_shapes=shape.scatter_scratch()
        + [pltpu.VMEM(q, BF) for q in shape.quarter_shape]
        + shape.sub_scratch()
        + shape.semaphores(),
        compiler_params=pltpu.CompilerParams(
            collective_id=ident, has_side_effects=True, vmem_limit_bytes=24 * 2**20
        ),
    )(attended, grad_in)


def policy_kernel(
    shape, x_ref, cin_ref, wp_ref, side_ref, att_ref, out_ref, sum_a, sum_b, part_ref, d_ref, *refs
):
    scatter, semaphores, (send, recv, local) = refs[:5], refs[5:9], refs[9:]
    work = Reduce(shape, att_ref, d_ref, None, scatter, (sum_a, sum_b), None, semaphores)
    rows, width = part_ref.shape
    half = rows // 2

    def place(source_y, part, slot):
        return out_ref.at[
            pl.ds(part * half, half), pl.ds(pl.multiple_of(source_y * width, HEAD), width)
        ]

    ring = YGather(lambda part: part_ref.at[pl.ds(part * half, half)], place, send, recv)
    barrier = pltpu.get_barrier_semaphore()
    expected = ring.greet(barrier) + work.greet(barrier)
    part_ref[...] = jnp.dot(x_ref[...], cin_ref[...], preferred_element_type=F32).astype(BF)
    pl.semaphore_wait(barrier, expected)
    ring.start()
    mine = pltpu.make_async_copy(
        part_ref, out_ref.at[:, pl.ds(pl.multiple_of(ring.ypos * width, HEAD), width)], local.at[0]
    )
    mine.start()
    d_ref[...] = policy_backward(x_ref[...], side_ref[...], wp_ref[...]).astype(BF)
    ring.pass_on(0)
    ring.pass_on(1)
    work.begin()
    work.swap_and_scatter()
    ring.arrived(0, 1)
    ring.arrived(1, 0)
    work.first_sums()
    ring.arrived(2, 0)
    ring.arrived(2, 1)
    work.finish_scatter()
    ring.wait_sent()
    mine.wait()


def policy_call(hidden, c_in, w_policy, side, attended, ident):
    rows = hidden.shape[0]
    width = c_in.shape[1]
    shape = Geometry(attended.shape[1], hidden.shape[1], False)
    vmem = pl.BlockSpec(memory_space=pltpu.VMEM)
    return pl.pallas_call(
        functools.partial(policy_kernel, shape),
        out_shape=[jax.ShapeDtypeStruct((rows, 4 * width), BF)]
        + [jax.ShapeDtypeStruct(q, BF) for q in shape.quarter_shape],
        in_specs=[vmem] * 5,
        out_specs=[vmem] * 3,
        scratch_shapes=[pltpu.VMEM((rows, width), BF), pltpu.VMEM(hidden.shape, BF)]
        + shape.scatter_scratch()
        + shape.semaphores()
        + [
            pltpu.SemaphoreType.DMA((4, 2)),
            pltpu.SemaphoreType.DMA((3, 2)),
            pltpu.SemaphoreType.DMA((1,)),
        ],
        compiler_params=pltpu.CompilerParams(
            collective_id=ident, has_side_effects=True, vmem_limit_bytes=32 * 2**20
        ),
    )(hidden, c_in, w_policy, side, attended)


def output_kernel(shape, x_ref, w_hbm, base_ref, *refs):
    *refs, w_ref, loaded = refs
    if shape is None:
        out_ref, acc, blocks, send, recv = refs
        work = None
    else:
        sum_a, sum_b, out_ref, grad_ref, acc, blocks, send, recv = refs[:8]
        work = Reduce(shape, None, None, grad_ref, None, (sum_a, sum_b), refs[8:10], refs[10:14])
    rows = x_ref.shape[0]
    half = rows // 2
    ring = YGather(
        lambda part: x_ref.at[pl.ds(part * half, half)],
        lambda source_y, part, slot: blocks.at[slot, pl.ds(part * half, half)],
        send,
        recv,
    )
    loads = [
        pltpu.make_async_copy(w_hbm.at[there], w_ref.at[there], loaded.at[k])
        for k, there in enumerate((ring.ypos, ring.ym, ring.yp, ring.y2))
    ]
    for load in loads:
        load.start()
    barrier = pltpu.get_barrier_semaphore()
    expected = ring.greet(barrier)
    if work is not None:
        expected += work.greet(barrier)
    pl.semaphore_wait(barrier, expected)
    ring.start()
    if work is not None:
        work.second_scatter()
    for load in loads:
        load.wait()
    acc[...] = base_ref[...].astype(F32) + jnp.dot(
        x_ref[...], w_ref[ring.ypos], preferred_element_type=F32
    )

    def add(slot, part):
        source_y = (ring.ym, ring.yp, ring.y2)[slot]
        span = pl.ds(part * half, half)
        acc[span, :] += jnp.dot(
            blocks[slot, span, :], w_ref[source_y], preferred_element_type=F32
        )

    if work is not None:
        work.first_gather()
    ring.pass_on(0)
    ring.pass_on(1)
    add(0, 0)
    add(1, 1)
    if work is not None:
        work.second_gather()
    ring.arrived(0, 1)
    add(0, 1)
    ring.arrived(1, 0)
    add(1, 0)
    if work is not None:
        work.last_shares()
    ring.arrived(2, 0)
    add(2, 0)
    ring.arrived(2, 1)
    add(2, 1)
    out_ref[...] = acc[...].astype(out_ref.dtype)
    if work is not None:
        work.finish()
    ring.wait_sent()


def output_call(x, w_full, base, out_type, shape, sums, ident):
    rows, width = x.shape
    columns = w_full.shape[2]
    vmem = pl.BlockSpec(memory_space=pltpu.VMEM)
    args = [x, pltpu.with_memory_space_constraint(w_full, pltpu.HBM), base]
    out_shape = [jax.ShapeDtypeStruct((rows, columns), out_type)]
    scratch = [
        pltpu.VMEM((rows, columns), F32),
        pltpu.VMEM((3, rows, width), BF),
        pltpu.SemaphoreType.DMA((4, 2)),
        pltpu.SemaphoreType.DMA((3, 2)),
    ]
    if shape is not None:
        args += list(sums)
        out_shape.append(jax.ShapeDtypeStruct((shape.rows, shape.columns), BF))
        scratch += shape.sub_scratch() + shape.semaphores()
    scratch += [pltpu.VMEM(w_full.shape, BF), pltpu.SemaphoreType.DMA((4,))]
    return pl.pallas_call(
        functools.partial(output_kernel, shape),
        out_shape=out_shape,
        in_specs=[vmem, pl.BlockSpec(memory_space=pltpu.HBM)] + [vmem] * (len(args) - 2),
        out_specs=[vmem] * len(out_shape),
        scratch_shapes=scratch,
        compiler_params=pltpu.CompilerParams(
            collective_id=ident, has_side_effects=True, vmem_limit_bytes=40 * 2**20
        ),
    )(*args)


def stacked_queries(source, w_query):
    rows = source.shape[0]
    normed = rms_normed(source.astype(F32)).astype(BF)
    queries = (
        jnp.dot(normed, w_query, preferred_element_type=F32) * (HEAD ** (-0.5) * LOG2E)
    ).astype(BF)
    heads = queries.shape[1] // HEAD
    return jnp.transpose(queries.reshape(rows, heads, HEAD), (1, 0, 2)).reshape(heads * rows, HEAD)


def on_device(
    obs,
    a_query,
    a_keyval,
    a_out,
    w_policy,
    c_in,
    c_query,
    c_keyval,
    c_out,
    w_value,
    actions,
    advantages,
    old_logp,
    returns,
    robot_count,
):
    row_count = obs.shape[1]
    batch_index = lax.axis_index("sec")
    robot_total = robot_count[batch_index]
    total = robot_total.reshape(1)
    live_total = jnp.sum(robot_count).astype(F32)
    first_row = lax.axis_index("rep") * row_count
    live_mask = first_row + lax.iota(jnp.int32, row_count) < robot_total
    mdl_count = lax.axis_size("mdl")
    part_rows = row_count // mdl_count
    row_start = lax.axis_index("mdl") * part_rows
    side = jnp.stack(
        [
            actions[0].astype(F32),
            advantages[0],
            old_logp[0],
            jnp.where(live_mask, 1.0 / live_total, 0.0),
        ],
        axis=1,
    )

    attended, a_out_full = attend(robot_count, total, obs[0], a_query, a_keyval, a_out, 1)
    (hidden,) = output_call(attended, a_out_full, obs[0], BF, None, None, 3)
    embedded, *sums = policy_call(hidden, c_in, w_policy, side, attended, 4)
    critic_attended, c_out_full = attend(
        robot_count, total, embedded, c_query, c_keyval, c_out, 2
    )
    shape = Geometry(attended.shape[1], hidden.shape[1], False)
    mixed, actor_summed = output_call(critic_attended, c_out_full, embedded, F32, shape, sums, 5)
    value_pred, dmixed = value_backward(mixed, returns[0], live_mask, live_total, w_value)
    value_part = lax.dynamic_slice_in_dim(value_pred, row_start, part_rows, 0)
    critic_summed = reduced_grad(critic_attended, dmixed.astype(BF), 6).astype(F32)
    return (value_part[None, :], actor_summed.astype(F32), critic_summed)


def solution(mesh):
    return jax.shard_map(
        on_device,
        mesh=mesh,
        in_specs=(
            P("sec", "rep", None),
            P(None, "mdl"),
            P(None, None, "mdl"),
            P("mdl", None),
            P(),
            P(None, "mdl"),
            P(None, "mdl"),
            P(None, None, "mdl"),
            P("mdl", None),
            P(),
            P("sec", "rep"),
            P("sec", "rep"),
            P("sec", "rep"),
            P("sec", "rep"),
            P(),
        ),
        out_specs=(P("sec", ("rep", "mdl")), P("mdl", None), P("mdl", None)),
        check_vma=False,
    )
```

```python
import functools

import jax
import jax.numpy as jnp
from jax import lax
from jax.experimental import pallas as pl
from jax.experimental.pallas import tpu as pltpu
from jax.sharding import PartitionSpec as P

HEAD = 128
LOG2E = 1.4426950408889634
MESH = pl.DeviceIdType.MESH
BF = jnp.bfloat16
F32 = jnp.float32

epsilon = 1e-05
clip_range = 0.2
masked_score = -1e30
sum_low = 1e-20
sum_high = 1e25


def rms_normed(values_in):
    return values_in * lax.rsqrt(jnp.mean(values_in * values_in, axis=-1, keepdims=True) + epsilon)


def policy_backward(hidden, action, advantage, old_values, scale, w_policy):
    source = hidden.astype(F32)
    factor = lax.rsqrt(jnp.mean(source * source, axis=-1, keepdims=True) + epsilon)
    normed = source * factor
    logits = jnp.dot(normed.astype(BF), w_policy, preferred_element_type=F32)
    shifted = logits - jnp.max(logits, axis=-1, keepdims=True)
    log_probs = shifted - jnp.log(jnp.sum(jnp.exp(shifted), axis=-1, keepdims=True))
    command = lax.broadcasted_iota(jnp.int32, logits.shape, 1)
    onehot = (action == command).astype(F32)
    chosen = jnp.sum(onehot * log_probs, axis=-1, keepdims=True)
    prob_ratio = jnp.exp(chosen - old_values)
    plain_term = prob_ratio * advantage
    bounded = jnp.clip(prob_ratio, 1.0 - clip_range, 1.0 + clip_range) * advantage
    slope_term = jnp.where((scale > 0.0) & (plain_term <= bounded), -plain_term * scale, 0.0)
    dlogits = slope_term * (onehot - jnp.exp(log_probs))
    dnormed = lax.dot_general(
        dlogits.astype(BF), w_policy, (((1,), (1,)), ((), ())), preferred_element_type=F32
    )
    return factor * (dnormed - normed * jnp.mean(dnormed * normed, axis=-1, keepdims=True))


def value_backward(mixed_out, target, scale, w_value):
    factor = lax.rsqrt(jnp.mean(mixed_out * mixed_out, axis=-1, keepdims=True) + epsilon)
    normed = mixed_out * factor
    weight = w_value.astype(F32)
    value_pred = jnp.sum(normed.astype(BF).astype(F32) * weight, axis=-1, keepdims=True)
    slope_term = jnp.where(scale > 0.0, (value_pred - target) * scale, 0.0)
    dnormed = slope_term * weight
    inner = jnp.mean(dnormed * normed, axis=-1, keepdims=True)
    return (value_pred, (factor * (dnormed - normed * inner)).astype(BF))


def standing(row):
    return jnp.transpose(jnp.broadcast_to(row, (HEAD, row.shape[1])))


def live_scale(count_ref, rows):
    total = count_ref[lax.axis_index("sec")]
    both = jnp.full((rows, 1), count_ref[0] + count_ref[1], jnp.int32).astype(F32)
    index = lax.axis_index("rep") * rows + lax.broadcasted_iota(jnp.int32, (rows, 1), 0)
    return jnp.where(index < total, 1.0 / both, 0.0)


PIECES = 2


def attend_kernel(
    heads, count_ref, x_ref, wq_ref, wkv_ref, w_ref, out_ref, wfull_ref, *refs
):
    buf, acc, q_ref, kv_ref, send, recv, local, wsend, wrecv, wlocal = refs
    rows = x_ref.shape[0]
    piece = rows // PIECES
    all_keys = buf.shape[0]
    me = lax.axis_index("rep")
    count = 16
    core = lax.rem(me, 2)
    xpos = lax.rem(me // 2, 2)
    other = me + 1 - 2 * core
    xpeer = me + 2 - 4 * xpos
    zp = lax.rem(me + 4, count)
    zm = lax.rem(me + 12, count)
    src = [
        zm,
        zp,
        lax.rem(me + 8, count),
        xpeer,
        lax.rem(xpeer + 12, count),
        lax.rem(xpeer + 4, count),
        lax.rem(xpeer + 8, count),
    ]
    src = src + [other] + [s + 1 - 2 * core for s in src]

    ypos = lax.axis_index("mdl")
    yp = lax.rem(ypos + 1, 4)
    ym = lax.rem(ypos + 3, 4)
    y2 = lax.rem(ypos + 2, 4)

    barrier = pltpu.get_barrier_semaphore()
    peers = [{"rep": zp}, {"rep": zm}, {"rep": xpeer}, {"rep": other}]
    peers += [{"mdl": yp}, {"mdl": ym}]
    for peer in peers:
        pl.semaphore_signal(barrier, inc=1, device_id=peer, device_id_type=MESH)

    total = count_ref[lax.axis_index("sec")]
    normed = rms_normed(x_ref[...].astype(F32)).astype(BF)
    live = me * rows + lax.broadcasted_iota(jnp.int32, (rows, HEAD), 0) < total
    for part in range(2):
        made = jnp.dot(normed, wkv_ref[part], preferred_element_type=F32)
        kv_ref[:, part * HEAD : (part + 1) * HEAD] = jnp.where(live, made, 0.0).astype(BF)
    pl.semaphore_wait(barrier, len(peers))

    def block_rows(block, part):
        return pl.ds(pl.multiple_of(block * rows + part * piece, piece), piece)

    def transfer(block, part, slot, target, lane, own=False):
        where = buf.at[block_rows(block, part), pl.ds(0, 2 * HEAD)]
        source = kv_ref.at[pl.ds(part * piece, piece)] if own else where
        return pltpu.make_async_remote_copy(
            src_ref=source,
            dst_ref=where,
            send_sem=send.at[lane, part],
            recv_sem=recv.at[slot, part],
            device_id={"rep": target},
            device_id_type=MESH,
        )

    plan = [
        (None, 3, xpeer),
        (None, 1, zm),
        (None, 0, zp),
        (None, 7, other),
        (1, 9, other),
        (0, 2, zp),
        (0, 8, other),
        (3, 5, zm),
        (3, 4, zp),
        (3, 11, other),
        (2, 10, other),
        (5, 6, zm),
        (5, 13, other),
        (4, 12, other),
        (6, 14, other),
    ]

    def plan_copy(index, part):
        from_slot, to_slot, target = plan[index]
        block = me if from_slot is None else src[from_slot]
        return transfer(block, part, to_slot, target, index, own=from_slot is None)

    def arrived(slot, part):
        where = buf.at[block_rows(src[slot], part), pl.ds(0, 2 * HEAD)]
        pltpu.make_async_copy(where, where, recv.at[slot, part]).wait()

    def pass_on(slot):
        for part in range(PIECES):
            arrived(slot, part)
            for index, (from_slot, _, _) in enumerate(plan):
                if from_slot == slot:
                    plan_copy(index, part).start()

    def take(slot):
        for part in range(PIECES):
            arrived(slot, part)

    for part in range(PIECES):
        for index in range(4):
            plan_copy(index, part).start()
    own_copy = pltpu.make_async_copy(
        kv_ref,
        buf.at[pl.ds(pl.multiple_of(me * rows, rows), rows), pl.ds(0, 2 * HEAD)],
        local.at[0],
    )
    own_copy.start()

    wrows = w_ref.shape[0]
    wpiece = wrows // 4
    wown = pltpu.make_async_copy(w_ref, wfull_ref.at[ypos], wlocal.at[0])
    wown.start()

    wsrc = [ym, yp, y2]

    def wcopy(source_y, which, part, slot, target, lane, own=False):
        span = pl.ds((2 * which + part) * wpiece, wpiece)
        where = wfull_ref.at[source_y, span]
        return pltpu.make_async_remote_copy(
            src_ref=w_ref.at[span] if own else where,
            dst_ref=where,
            send_sem=wsend.at[lane, part],
            recv_sem=wrecv.at[slot, part],
            device_id=target,
            device_id_type=MESH,
        )

    def wfirst(part):
        return [
            wcopy(ypos, core, part, 0, {"mdl": yp}, 0, own=True),
            wcopy(ypos, core, part, 1, {"mdl": ym}, 1, own=True),
        ]

    def wrelay(part):
        if part == 0:
            return wcopy(ym, core, 0, 2, {"mdl": yp}, 2)
        return wcopy(yp, core, 1, 2, {"mdl": ym}, 2)

    def wshare(slot, part):
        return wcopy(wsrc[slot], core, part, 3 + slot, {"rep": other}, 3 + slot)

    def warrived(slot, part):
        which = core if slot < 3 else 1 - core
        span = pl.ds((2 * which + part) * wpiece, wpiece)
        where = wfull_ref.at[wsrc[slot % 3], span]
        pltpu.make_async_copy(where, where, wrecv.at[slot, part]).wait()

    for part in range(2):
        for copy in wfirst(part):
            copy.start()

    queries = jnp.dot(normed, wq_ref[...], preferred_element_type=F32) * (HEAD ** (-0.5) * LOG2E)
    for head in range(heads):
        q_ref[head * rows : (head + 1) * rows, :] = queries[
            :, head * HEAD : (head + 1) * HEAD
        ].astype(BF)
    key_index = lax.broadcasted_iota(jnp.int32, (all_keys, HEAD), 0)
    buf[:, 2 * HEAD :] = jnp.where(key_index < total, 1.0, 0.0).astype(BF)
    acc[...] = jnp.zeros_like(acc)
    own_copy.wait()

    chip_rows = 2 * rows
    zpos = me // 4

    def step(i, carry):
        @pl.when(i == 0)
        def _():
            take(7)

        @pl.when(i == 1)
        def _():
            pass_on(1)
            pass_on(0)
            take(9)

        @pl.when(i == 2)
        def _():
            pass_on(3)
            take(8)

        @pl.when(i == 3)
        def _():
            pass_on(2)
            take(10)

        @pl.when(i == 4)
        def _():
            pass_on(5)
            take(11)

        @pl.when(i == 5)
        def _():
            for part in range(2):
                warrived(0, part)
                warrived(1, part)
                wrelay(part).start()
                wshare(0, part).start()
                wshare(1, part).start()

        @pl.when(i == 5)
        def _():
            pass_on(4)
            take(13)

        @pl.when(i == 6)
        def _():
            pass_on(6)
            take(12)

        @pl.when(i == 7)
        def _():
            take(14)

        j = lax.rem(i, 4)
        dz = j + (j // 2) * (1 - 2 * lax.rem(j, 2))
        dx = i // 4
        chip = lax.rem(zpos + dz, 4) * 2 + lax.rem(xpos + dx, 2)
        span = pl.ds(pl.multiple_of(chip * chip_rows, chip_rows), chip_rows)
        scores = lax.dot_general(
            q_ref[...],
            buf[span, :HEAD],
            (((1,), (1,)), ((), ())),
            preferred_element_type=F32,
        )
        weights = jnp.exp2(scores).astype(BF)
        acc[...] += jnp.dot(weights, buf[span, HEAD:], preferred_element_type=F32)
        return carry

    lax.fori_loop(0, 8, step, 0)

    for part in range(2):
        warrived(2, part)
        wshare(2, part).start()

    for head in range(heads):
        part = acc[head * rows : (head + 1) * rows, :]
        sums = part[:, HEAD:]
        safe = (sums > sum_low) & (sums < sum_high)
        out_ref[:, head * HEAD : (head + 1) * HEAD] = jnp.where(
            safe, part[:, :HEAD] / sums, jnp.nan
        ).astype(BF)

    for slot in range(3, 6):
        for part in range(2):
            warrived(slot, part)
    for part in range(2):
        for copy in wfirst(part):
            copy.wait_send()
        wrelay(part).wait_send()
        for slot in range(3):
            wshare(slot, part).wait_send()
    wown.wait()
    for part in range(PIECES):
        for index in range(len(plan)):
            plan_copy(index, part).wait_send()


def attend_call(counts, source, w_query, w_keyval, w, ident):
    heads = w_query.shape[1] // HEAD
    rows = source.shape[0]
    keys = rows * 16
    vmem = pl.BlockSpec(memory_space=pltpu.VMEM)
    anywhere = pl.BlockSpec(memory_space=pl.ANY)
    return pl.pallas_call(
        functools.partial(attend_kernel, heads),
        out_shape=[
            jax.ShapeDtypeStruct((rows, heads * HEAD), BF),
            jax.ShapeDtypeStruct((4,) + w.shape, BF),
        ],
        in_specs=[pl.BlockSpec(memory_space=pltpu.SMEM), vmem, vmem, vmem, anywhere],
        out_specs=[vmem, anywhere],
        scratch_shapes=[
            pltpu.VMEM((keys, 3 * HEAD), BF),
            pltpu.VMEM((heads * rows, 2 * HEAD), F32),
            pltpu.VMEM((heads * rows, HEAD), BF),
            pltpu.VMEM((rows, 2 * HEAD), BF),
            pltpu.SemaphoreType.DMA((15, PIECES)),
            pltpu.SemaphoreType.DMA((15, PIECES)),
            pltpu.SemaphoreType.DMA((1,)),
            pltpu.SemaphoreType.DMA((6, 2)),
            pltpu.SemaphoreType.DMA((6, 2)),
            pltpu.SemaphoreType.DMA((1,)),
        ],
        compiler_params=pltpu.CompilerParams(
            collective_id=ident, has_side_effects=True, vmem_limit_bytes=40 * 2**20
        ),
        cost_estimate=pl.CostEstimate(
            flops=4 * heads * rows * keys * HEAD,
            bytes_accessed=keys * 4 * HEAD,
            transcendentals=heads * rows * keys,
        ),
    )(counts, source, w_query, w_keyval, w)


def careful_kernel(total_ref, q_ref, kv_ref, out_ref, top, acc, total_sum):
    step = pl.program_id(0)
    block = kv_ref.shape[0]

    @pl.when(step == 0)
    def _():
        top[...] = jnp.full_like(top, masked_score)
        acc[...] = jnp.zeros_like(acc)
        total_sum[...] = jnp.zeros_like(total_sum)

    scores = lax.dot_general(
        q_ref[...], kv_ref[:, :HEAD], (((1,), (1,)), ((), ())), preferred_element_type=F32
    )
    key_index = step * block + lax.broadcasted_iota(jnp.int32, scores.shape, 1)
    live = key_index < total_ref[0]
    scores = jnp.where(live, scores, masked_score)
    old = top[...]
    new = jnp.maximum(old, jnp.max(scores, axis=1, keepdims=True))
    top[...] = new
    rescale = jnp.exp2(old - new)
    weights = jnp.where(live, jnp.exp2(scores - new[:, :1]), 0.0)
    total_sum[...] = total_sum[...] * rescale + jnp.sum(weights, axis=1, keepdims=True)
    acc[...] = acc[...] * rescale + jnp.dot(
        weights.astype(BF), kv_ref[:, HEAD:], preferred_element_type=F32
    )

    @pl.when(step == pl.num_programs(0) - 1)
    def _():
        rows, width = out_ref.shape
        for head in range(width // HEAD):
            span = slice(head * rows, (head + 1) * rows)
            out_ref[:, head * HEAD : (head + 1) * HEAD] = (acc[span, :] / total_sum[span, :]).astype(
                BF
            )


def careful_call(total, queries, kv_full, rows):
    heads = queries.shape[0] // rows
    block = 256
    return pl.pallas_call(
        careful_kernel,
        out_shape=jax.ShapeDtypeStruct((rows, heads * HEAD), BF),
        grid=(kv_full.shape[0] // block,),
        in_specs=[
            pl.BlockSpec(memory_space=pltpu.SMEM),
            pl.BlockSpec(queries.shape, lambda i: (0, 0)),
            pl.BlockSpec((block, 2 * HEAD), lambda i: (i, 0)),
        ],
        out_specs=pl.BlockSpec((rows, heads * HEAD), lambda i: (0, 0)),
        scratch_shapes=[pltpu.VMEM((heads * rows, HEAD), F32)] * 3,
        compiler_params=pltpu.CompilerParams(vmem_limit_bytes=20 * 2**20),
    )(total, queries, kv_full)


class YGather:
    def __init__(self, own_half, place, send, recv):
        self.ypos = lax.axis_index("mdl")
        self.yp = lax.rem(self.ypos + 1, 4)
        self.ym = lax.rem(self.ypos + 3, 4)
        self.y2 = lax.rem(self.ypos + 2, 4)
        self.own_half, self.place, self.send, self.recv = own_half, place, send, recv

    def greet(self, barrier):
        for peer in (self.yp, self.ym):
            pl.semaphore_signal(barrier, inc=1, device_id={"mdl": peer}, device_id_type=MESH)
        return 2

    def copy(self, source_y, part, slot, target, lane, own=False):
        return pltpu.make_async_remote_copy(
            src_ref=self.own_half(part) if own else self.place(source_y, part, lane - 2),
            dst_ref=self.place(source_y, part, slot),
            send_sem=self.send.at[lane, part],
            recv_sem=self.recv.at[slot, part],
            device_id={"mdl": target},
            device_id_type=MESH,
        )

    def first(self):
        return [
            self.copy(self.ypos, 0, 0, self.yp, 0, own=True),
            self.copy(self.ypos, 1, 1, self.ym, 1, own=True),
            self.copy(self.ypos, 1, 0, self.yp, 0, own=True),
            self.copy(self.ypos, 0, 1, self.ym, 1, own=True),
        ]

    def start(self):
        for item in self.first():
            item.start()

    def arrived(self, slot, part):
        where = self.place((self.ym, self.yp, self.y2)[slot], part, slot)
        pltpu.make_async_copy(where, where, self.recv.at[slot, part]).wait()

    def relay(self, part):
        if part == 0:
            return self.copy(self.ym, 0, 2, self.yp, 2)
        return self.copy(self.yp, 1, 2, self.ym, 3)

    def pass_on(self, part):
        self.arrived(part, part)
        self.relay(part).start()

    def wait_sent(self):
        for item in self.first():
            item.wait_send()
        for part in range(2):
            self.relay(part).wait_send()


class Geometry:
    def __init__(self, rows, columns, by_rows):
        self.by_rows = by_rows
        self.rows, self.columns = rows, columns
        if by_rows:
            self.half = (rows // 2, columns)
            self.quarter_shape = [(rows // 4, columns // 4)] * 2
            self.sub_shape = [(rows // 16, columns // 4)] * 2
        else:
            third = columns // 6
            self.half = (rows, columns // 2)
            self.quarter_shape = [(rows // 4, 2 * third), (rows // 4, third)]
            self.sub_shape = [(rows // 4, third // 2), (rows // 8, third // 2)]

    def whole(self, core):
        if self.by_rows:
            return (core * self.half[0], 0)
        return (0, core * self.half[1])

    def quarter(self, part, index):
        rows, columns = self.quarter_shape[part]
        if self.by_rows:
            return (part * rows, index * columns)
        return (index * rows, part * self.quarter_shape[0][1])

    def sub(self, part, index):
        rows, columns = self.sub_shape[part]
        if self.by_rows:
            return (index * rows, 0)
        if part == 0:
            return (0, index * columns)
        return ((index // 2) * rows, lax.rem(index, 2) * columns)

    def scatter_scratch(self):
        vmem = pltpu.VMEM
        return [vmem(self.half, BF)] * 3 + [vmem((3,) + q, BF) for q in self.quarter_shape]

    def sub_scratch(self):
        return [pltpu.VMEM((3,) + sub, BF) for sub in self.sub_shape]

    def semaphores(self):
        dma = pltpu.SemaphoreType.DMA
        return [dma((4, 2, 3)), dma((4, 2, 3)), dma((9,)), dma((9,))]


def box(start, shape):
    row, column = start
    return (
        pl.ds(row if isinstance(row, int) else pl.multiple_of(row, 16), shape[0]),
        pl.ds(column if isinstance(column, int) else pl.multiple_of(column, HEAD), shape[1]),
    )


def plus(left, right):
    return (left[0] + right[0], left[1] + right[1])


class Reduce:
    hops = (2, 1, 3)

    def __init__(self, shape, att_ref, d_ref, out_ref, scatter, sums, sub_in, semaphores):
        self.g = shape
        self.att, self.d, self.out = att_ref, d_ref, out_ref
        if scatter is not None:
            self.theirs, self.mine, self.got = scatter[:3]
            self.part_in = scatter[3:5]
        self.part_sum = sums
        self.sub_in = sub_in
        self.send, self.recv, self.csend, self.crecv = semaphores
        me = lax.axis_index("rep")
        self.me = me
        self.core = lax.rem(me, 2)
        self.other = me + 1 - 2 * self.core
        self.zpos = me // 4
        self.xpos = lax.rem(me // 2, 2) * 2 + lax.axis_index("sec")
        self.first = [self.xpos, self.zpos]
        self.second = [self.zpos, self.xpos]
        self.near = [self.at_x, self.at_z]

    def at_x(self, k):
        there = lax.rem(self.xpos + k, 4)
        return {"rep": self.zpos * 4 + (there // 2) * 2 + self.core, "sec": lax.rem(there, 2)}

    def at_z(self, k):
        return {"rep": lax.rem(self.me + 4 * k, 16)}

    def greet(self, barrier):
        for k in range(1, 4):
            pl.semaphore_signal(barrier, inc=1, device_id=self.at_x(k), device_id_type=MESH)
            pl.semaphore_signal(barrier, inc=1, device_id=self.at_z(k), device_id_type=MESH)
        pl.semaphore_signal(barrier, inc=1, device_id={"rep": self.other}, device_id_type=MESH)
        return 7

    def grad(self, which):
        left, right = self.att, self.d
        if self.g.by_rows:
            size = self.g.half[0]
            left = left[:, pl.ds(pl.multiple_of(which * size, size), size)]
            right = right[...]
        else:
            size = self.g.half[1]
            left = left[...]
            right = right[:, pl.ds(pl.multiple_of(which * size, HEAD), size)]
        return lax.dot_general(left, right, (((0,), (0,)), ((), ())), preferred_element_type=F32)

    def copy(self, source, target, send, recv, device):
        return pltpu.make_async_remote_copy(
            src_ref=source,
            dst_ref=target,
            send_sem=send,
            recv_sem=recv,
            device_id=device,
            device_id_type=MESH,
        )

    def swap(self):
        return self.copy(
            self.theirs, self.got, self.csend.at[0], self.crecv.at[0], {"rep": self.other}
        )

    def stage(self, level, part, k, source, target, device):
        return self.copy(
            source,
            target,
            self.send.at[level, part, k - 1],
            self.recv.at[level, part, k - 1],
            device,
        )

    def scatter_one(self, part, k):
        start = self.g.quarter(part, lax.rem(self.first[part] + k, 4))
        return self.stage(
            0,
            part,
            k,
            self.mine.at[box(start, self.g.quarter_shape[part])],
            self.part_in[part].at[k - 1],
            self.near[part](k),
        )

    def scatter_two(self, part, k):
        start = self.g.sub(part, lax.rem(self.second[part] + k, 4))
        return self.stage(
            1,
            part,
            k,
            self.part_sum[part].at[box(start, self.g.sub_shape[part])],
            self.sub_in[part].at[k - 1],
            self.near[1 - part](k),
        )

    def my_sub(self, part):
        start = plus(
            self.g.whole(self.core),
            plus(self.g.quarter(part, self.first[part]), self.g.sub(part, self.second[part])),
        )
        return box(start, self.g.sub_shape[part])

    def out_quarter(self, core, part, index):
        start = plus(self.g.whole(core), self.g.quarter(part, index))
        return self.out.at[box(start, self.g.quarter_shape[part])]

    def gather_two(self, part, k):
        where = self.out.at[self.my_sub(part)]
        return self.stage(2, part, k, where, where, self.near[1 - part](k))

    def gather_one(self, part, k):
        where = self.out_quarter(self.core, part, self.first[part])
        return self.stage(3, part, k, where, where, self.near[part](k))

    def share(self, part, k, core):
        where = self.out_quarter(core, part, lax.rem(self.first[part] + 4 - k, 4))
        index = 1 + part * 4 + k
        return self.copy(
            where, where, self.csend.at[index], self.crecv.at[index], {"rep": self.other}
        )

    def begin(self):
        self.theirs[...] = self.grad(1 - self.core).astype(BF)

    def swap_and_scatter(self):
        self.swap().start()
        own = self.grad(self.core)
        self.swap().wait_recv()
        self.mine[...] = (own + self.got[...].astype(F32)).astype(BF)
        for k in self.hops:
            for part in range(2):
                self.scatter_one(part, k).start()

    def first_sums(self):
        for part in range(2):
            start = self.g.quarter(part, self.first[part])
            total = self.mine[box(start, self.g.quarter_shape[part])].astype(F32)
            for k in (1, 3, 2):
                self.scatter_one(part, k).wait_recv()
                total += self.part_in[part][k - 1].astype(F32)
            self.part_sum[part][...] = total.astype(BF)

    def second_scatter(self):
        for k in self.hops:
            for part in range(2):
                self.scatter_two(part, k).start()

    def first_gather(self):
        for part in range(2):
            start = self.g.sub(part, self.second[part])
            total = self.part_sum[part][box(start, self.g.sub_shape[part])].astype(F32)
            for k in (1, 3, 2):
                self.scatter_two(part, k).wait_recv()
                total += self.sub_in[part][k - 1].astype(F32)
            self.out[self.my_sub(part)] = total.astype(BF)
            for k in self.hops:
                self.gather_two(part, k).start()

    def second_gather(self):
        for part in range(2):
            for k in range(1, 4):
                self.gather_two(part, k).wait_recv()
            for k in self.hops:
                self.gather_one(part, k).start()
            self.share(part, 0, self.core).start()

    def last_shares(self):
        for k in (1, 3, 2):
            for part in range(2):
                self.gather_one(part, k).wait_recv()
                self.share(part, k, self.core).start()

    def finish_scatter(self):
        self.swap().wait_send()
        for part in range(2):
            for k in range(1, 4):
                self.scatter_one(part, k).wait_send()

    def finish(self):
        for part in range(2):
            for k in range(4):
                self.share(part, k, 1 - self.core).wait_recv()
        for part in range(2):
            for k in range(1, 4):
                self.scatter_two(part, k).wait_send()
                self.gather_two(part, k).wait_send()
                self.gather_one(part, k).wait_send()
            for k in range(4):
                self.share(part, k, self.core).wait_send()


def reduce_kernel(shape, att_ref, d_ref, out_ref, *scratch):
    work = Reduce(
        shape, att_ref, d_ref, out_ref, scratch[:5], scratch[5:7], scratch[7:9], scratch[9:13]
    )
    barrier = pltpu.get_barrier_semaphore()
    expected = work.greet(barrier)
    work.begin()
    pl.semaphore_wait(barrier, expected)
    work.swap_and_scatter()
    work.first_sums()
    work.second_scatter()
    work.first_gather()
    work.second_gather()
    work.last_shares()
    work.finish_scatter()
    work.finish()


def reduced_grad(attended, grad_in, ident):
    shape = Geometry(attended.shape[1], grad_in.shape[1], True)
    vmem = pl.BlockSpec(memory_space=pltpu.VMEM)
    return pl.pallas_call(
        functools.partial(reduce_kernel, shape),
        out_shape=jax.ShapeDtypeStruct((shape.rows, shape.columns), BF),
        in_specs=[vmem, vmem],
        out_specs=vmem,
        scratch_shapes=shape.scatter_scratch()
        + [pltpu.VMEM(q, BF) for q in shape.quarter_shape]
        + shape.sub_scratch()
        + shape.semaphores(),
        compiler_params=pltpu.CompilerParams(
            collective_id=ident, has_side_effects=True, vmem_limit_bytes=24 * 2**20
        ),
    )(attended, grad_in)


def policy_kernel(
    shape,
    count_ref,
    x_ref,
    cin_ref,
    wp_ref,
    action_ref,
    advantage_ref,
    old_ref,
    att_ref,
    out_ref,
    sum_a,
    sum_b,
    part_ref,
    d_ref,
    *refs,
):
    scatter, semaphores, (send, recv, local) = refs[:5], refs[5:9], refs[9:]
    work = Reduce(shape, att_ref, d_ref, None, scatter, (sum_a, sum_b), None, semaphores)
    rows, width = part_ref.shape
    half = rows // 2

    def place(source_y, part, slot):
        return out_ref.at[
            pl.ds(part * half, half), pl.ds(pl.multiple_of(source_y * width, HEAD), width)
        ]

    ring = YGather(lambda part: part_ref.at[pl.ds(part * half, half)], place, send, recv)
    barrier = pltpu.get_barrier_semaphore()
    expected = ring.greet(barrier) + work.greet(barrier)
    part_ref[...] = jnp.dot(x_ref[...], cin_ref[...], preferred_element_type=F32).astype(BF)
    pl.semaphore_wait(barrier, expected)
    ring.start()
    mine = pltpu.make_async_copy(
        part_ref, out_ref.at[:, pl.ds(pl.multiple_of(ring.ypos * width, HEAD), width)], local.at[0]
    )
    mine.start()
    d_ref[...] = policy_backward(
        x_ref[...],
        standing(action_ref[...]),
        standing(advantage_ref[...])[:, :1],
        standing(old_ref[...])[:, :1],
        live_scale(count_ref, rows),
        wp_ref[...],
    ).astype(BF)
    ring.pass_on(0)
    ring.pass_on(1)
    work.begin()
    work.swap_and_scatter()
    ring.arrived(0, 1)
    ring.arrived(1, 0)
    work.first_sums()
    ring.arrived(2, 0)
    ring.arrived(2, 1)
    work.finish_scatter()
    ring.wait_sent()
    mine.wait()


def policy_call(counts, hidden, c_in, w_policy, action, advantage, old_values, attended, ident):
    rows = hidden.shape[0]
    width = c_in.shape[1]
    shape = Geometry(attended.shape[1], hidden.shape[1], False)
    vmem = pl.BlockSpec(memory_space=pltpu.VMEM)
    return pl.pallas_call(
        functools.partial(policy_kernel, shape),
        out_shape=[jax.ShapeDtypeStruct((rows, 4 * width), BF)]
        + [jax.ShapeDtypeStruct(q, BF) for q in shape.quarter_shape],
        in_specs=[pl.BlockSpec(memory_space=pltpu.SMEM)] + [vmem] * 7,
        out_specs=[vmem] * 3,
        scratch_shapes=[pltpu.VMEM((rows, width), BF), pltpu.VMEM(hidden.shape, BF)]
        + shape.scatter_scratch()
        + shape.semaphores()
        + [
            pltpu.SemaphoreType.DMA((4, 2)),
            pltpu.SemaphoreType.DMA((3, 2)),
            pltpu.SemaphoreType.DMA((1,)),
        ],
        compiler_params=pltpu.CompilerParams(
            collective_id=ident, has_side_effects=True, vmem_limit_bytes=32 * 2**20
        ),
    )(counts, hidden, c_in, w_policy, action, advantage, old_values, attended)


def output_kernel(shape, x_ref, w_ref, base_ref, *refs):
    if shape is None:
        out_ref, acc, blocks, send, recv = refs
        work = None
    else:
        count_ref, return_ref, wv_ref, sum_a, sum_b, value_ref, out_ref, grad_ref = refs[:8]
        acc, blocks, send, recv = refs[8:12]
        work = Reduce(shape, None, None, grad_ref, None, (sum_a, sum_b), refs[12:14], refs[14:18])
    rows = x_ref.shape[0]
    half = rows // 2
    ring = YGather(
        lambda part: x_ref.at[pl.ds(part * half, half)],
        lambda source_y, part, slot: blocks.at[slot, pl.ds(part * half, half)],
        send,
        recv,
    )
    barrier = pltpu.get_barrier_semaphore()
    expected = ring.greet(barrier)
    if work is not None:
        expected += work.greet(barrier)
    pl.semaphore_wait(barrier, expected)
    ring.start()
    if work is not None:
        work.second_scatter()
    acc[...] = base_ref[...].astype(F32) + jnp.dot(
        x_ref[...], w_ref[ring.ypos], preferred_element_type=F32
    )

    def add(slot, part):
        source_y = (ring.ym, ring.yp, ring.y2)[slot]
        span = pl.ds(part * half, half)
        acc[span, :] += jnp.dot(
            blocks[slot, span, :], w_ref[source_y], preferred_element_type=F32
        )

    if work is not None:
        work.first_gather()
    ring.pass_on(0)
    ring.pass_on(1)
    add(0, 0)
    add(1, 1)
    if work is not None:
        work.second_gather()
    ring.arrived(0, 1)
    add(0, 1)
    ring.arrived(1, 0)
    add(1, 0)
    if work is not None:
        work.last_shares()
    ring.arrived(2, 0)
    add(2, 0)
    ring.arrived(2, 1)
    add(2, 1)
    if work is None:
        out_ref[...] = acc[...].astype(BF)
    else:
        value, out_ref[...] = value_backward(
            acc[...], standing(return_ref[...])[:, :1], live_scale(count_ref, rows), wv_ref[...]
        )
        value_ref[...] = jnp.transpose(jnp.broadcast_to(value, (rows, HEAD)))[:8]
    if work is not None:
        work.finish()
    ring.wait_sent()


def output_call(x, w_full, base, value_args, ident):
    rows, width = x.shape
    columns = w_full.shape[2]
    vmem = pl.BlockSpec(memory_space=pltpu.VMEM)
    args = [x, w_full, base]
    in_specs = [vmem] * 3
    out_shape = [jax.ShapeDtypeStruct((rows, columns), BF)]
    scratch = [
        pltpu.VMEM((rows, columns), F32),
        pltpu.VMEM((3, rows, width), BF),
        pltpu.SemaphoreType.DMA((4, 2)),
        pltpu.SemaphoreType.DMA((3, 2)),
    ]
    shape = None
    if value_args is not None:
        shape, counts, target, w_value, sums = value_args
        args += [counts, target, w_value] + list(sums)
        in_specs += [pl.BlockSpec(memory_space=pltpu.SMEM)] + [vmem] * 4
        out_shape = [jax.ShapeDtypeStruct((8, rows), F32)] + out_shape
        out_shape.append(jax.ShapeDtypeStruct((shape.rows, shape.columns), BF))
        scratch += shape.sub_scratch() + shape.semaphores()
    return pl.pallas_call(
        functools.partial(output_kernel, shape),
        out_shape=out_shape,
        in_specs=in_specs,
        out_specs=[vmem] * len(out_shape),
        scratch_shapes=scratch,
        compiler_params=pltpu.CompilerParams(
            collective_id=ident, has_side_effects=True, vmem_limit_bytes=(20 if shape is None else 32) * 2**20
        ),
    )(*args)


def stacked_queries(source, w_query):
    rows = source.shape[0]
    normed = rms_normed(source.astype(F32)).astype(BF)
    queries = (
        jnp.dot(normed, w_query, preferred_element_type=F32) * (HEAD ** (-0.5) * LOG2E)
    ).astype(BF)
    heads = queries.shape[1] // HEAD
    return jnp.transpose(queries.reshape(rows, heads, HEAD), (1, 0, 2)).reshape(heads * rows, HEAD)


def careful_attend(total, source, w_query, w_keyval):
    normed = rms_normed(source.astype(F32)).astype(BF)
    keyval = [jnp.dot(normed, w_keyval[part], preferred_element_type=F32) for part in range(2)]
    joined = jnp.concatenate(keyval, axis=1).astype(BF)
    everyone = lax.all_gather(joined, "rep", axis=0, tiled=True)
    return careful_call(total, stacked_queries(source, w_query), everyone, source.shape[0])


def summed_grad(attended, grad_in):
    grad = lax.dot_general(
        attended, grad_in, (((0,), (0,)), ((), ())), preferred_element_type=F32
    )
    return lax.psum(grad.astype(BF), ("rep", "sec")).astype(F32)


def careful_path(
    obs, a_query, a_keyval, a_out, w_policy, c_in, c_query, c_keyval, c_out, w_value, columns, total
):
    attended = careful_attend(total, obs, a_query, a_keyval)
    mixed_sum = lax.psum(jnp.dot(attended, a_out, preferred_element_type=F32), "mdl")
    hidden = (obs.astype(F32) + mixed_sum).astype(BF)
    action, advantage, old_values, target, scale = columns
    dhidden = policy_backward(hidden, action, advantage, old_values, scale, w_policy).astype(BF)
    embed_part = jnp.dot(hidden, c_in, preferred_element_type=F32).astype(BF)
    embedded = lax.all_gather(embed_part, "mdl", axis=1, tiled=True)
    critic_attended = careful_attend(total, embedded, c_query, c_keyval)
    critic_sum = lax.psum(jnp.dot(critic_attended, c_out, preferred_element_type=F32), "mdl")
    value, dmixed = value_backward(
        embedded.astype(F32) + critic_sum, target, scale, w_value[None, :]
    )
    return (value[:, 0], summed_grad(attended, dhidden), summed_grad(critic_attended, dmixed))


def on_device(
    obs,
    a_query,
    a_keyval,
    a_out,
    w_policy,
    c_in,
    c_query,
    c_keyval,
    c_out,
    w_value,
    actions,
    advantages,
    old_logp,
    returns,
    robot_count,
):
    rows = obs.shape[1]
    part_rows = rows // lax.axis_size("mdl")
    row_start = lax.axis_index("mdl") * part_rows

    def careful():
        total = robot_count[lax.axis_index("sec")]
        live = lax.axis_index("rep") * rows + lax.iota(jnp.int32, rows) < total
        scale = jnp.where(live, 1.0 / jnp.sum(robot_count).astype(F32), 0.0)
        columns = (actions[0], advantages[0], old_logp[0], returns[0], scale)
        return careful_path(
            obs[0],
            a_query,
            a_keyval,
            a_out,
            w_policy,
            c_in,
            c_query,
            c_keyval,
            c_out,
            w_value,
            tuple(column[:, None] for column in columns),
            total.reshape(1),
        )

    attended, a_out_full = attend_call(robot_count, obs[0], a_query, a_keyval, a_out, 1)
    (hidden,) = output_call(attended, a_out_full, obs[0], None, 3)
    embedded, *sums = policy_call(
        robot_count, hidden, c_in, w_policy, actions, advantages, old_logp, attended, 4
    )
    critic_attended, c_out_full = attend_call(
        robot_count, embedded, c_query, c_keyval, c_out, 2
    )
    shape = Geometry(attended.shape[1], hidden.shape[1], False)
    values, dmixed, actor_summed = output_call(
        critic_attended,
        c_out_full,
        embedded,
        (shape, robot_count, returns, w_value[None, :], sums),
        5,
    )
    critic_summed = reduced_grad(critic_attended, dmixed, 6)
    mark = critic_summed[0, 0].astype(F32)
    values, actor_grad, critic_grad = lax.cond(
        mark == mark,
        lambda: (values[0], actor_summed.astype(F32), critic_summed.astype(F32)),
        careful,
    )
    return (lax.dynamic_slice_in_dim(values, row_start, part_rows, 0)[None, :], actor_grad, critic_grad)


def solution(mesh):
    return jax.shard_map(
        on_device,
        mesh=mesh,
        in_specs=(
            P("sec", "rep", None),
            P(None, "mdl"),
            P(None, None, "mdl"),
            P("mdl", None),
            P(),
            P(None, "mdl"),
            P(None, "mdl"),
            P(None, None, "mdl"),
            P("mdl", None),
            P(),
            P("sec", "rep"),
            P("sec", "rep"),
            P("sec", "rep"),
            P("sec", "rep"),
            P(),
        ),
        out_specs=(P("sec", ("rep", "mdl")), P("mdl", None), P("mdl", None)),
        check_vma=False,
    )
```

```python
import functools

import jax
import jax.numpy as jnp
from jax import lax
from jax.experimental import pallas as pl
from jax.experimental.pallas import tpu as pltpu
from jax.sharding import PartitionSpec as P

HEAD = 128
LOG2E = 1.4426950408889634
MESH = pl.DeviceIdType.MESH
BF = jnp.bfloat16
F32 = jnp.float32

epsilon = 1e-05
clip_range = 0.2
masked_score = -1e30
sum_low = 1e-20
sum_high = 1e25


def rms_normed(values_in):
    return values_in * lax.rsqrt(jnp.mean(values_in * values_in, axis=-1, keepdims=True) + epsilon)


def policy_backward(hidden, action, advantage, old_values, scale, w_policy):
    source = hidden.astype(F32)
    factor = lax.rsqrt(jnp.mean(source * source, axis=-1, keepdims=True) + epsilon)
    normed = source * factor
    logits = jnp.dot(normed.astype(BF), w_policy, preferred_element_type=F32)
    shifted = logits - jnp.max(logits, axis=-1, keepdims=True)
    log_probs = shifted - jnp.log(jnp.sum(jnp.exp(shifted), axis=-1, keepdims=True))
    command = lax.broadcasted_iota(jnp.int32, logits.shape, 1)
    onehot = (action == command).astype(F32)
    chosen = jnp.sum(onehot * log_probs, axis=-1, keepdims=True)
    prob_ratio = jnp.exp(chosen - old_values)
    plain_term = prob_ratio * advantage
    bounded = jnp.clip(prob_ratio, 1.0 - clip_range, 1.0 + clip_range) * advantage
    slope_term = jnp.where((scale > 0.0) & (plain_term <= bounded), -plain_term * scale, 0.0)
    dlogits = slope_term * (onehot - jnp.exp(log_probs))
    dnormed = lax.dot_general(
        dlogits.astype(BF), w_policy, (((1,), (1,)), ((), ())), preferred_element_type=F32
    )
    return factor * (dnormed - normed * jnp.mean(dnormed * normed, axis=-1, keepdims=True))


def value_backward(mixed_out, target, scale, w_value):
    factor = lax.rsqrt(jnp.mean(mixed_out * mixed_out, axis=-1, keepdims=True) + epsilon)
    normed = mixed_out * factor
    weight = w_value.astype(F32)
    value_pred = jnp.sum(normed.astype(BF).astype(F32) * weight, axis=-1, keepdims=True)
    slope_term = jnp.where(scale > 0.0, (value_pred - target) * scale, 0.0)
    dnormed = slope_term * weight
    inner = jnp.mean(dnormed * normed, axis=-1, keepdims=True)
    return (value_pred, (factor * (dnormed - normed * inner)).astype(BF))


def standing(row):
    return jnp.transpose(jnp.broadcast_to(row, (HEAD, row.shape[1])))


def live_scale(count_ref, rows):
    total = count_ref[lax.axis_index("sec")]
    both = jnp.full((rows, 1), count_ref[0] + count_ref[1], jnp.int32).astype(F32)
    index = lax.axis_index("rep") * rows + lax.broadcasted_iota(jnp.int32, (rows, 1), 0)
    return jnp.where(index < total, 1.0 / both, 0.0)


PIECES = 2


def attend_kernel(
    heads, count_ref, x_ref, wq_ref, wkv_ref, w_ref, out_ref, wfull_ref, *refs
):
    buf, acc, q_ref, kv_ref, send, recv, local, wsend, wrecv, wlocal = refs
    rows = x_ref.shape[0]
    piece = rows // PIECES
    all_keys = buf.shape[0]
    me = lax.axis_index("rep")
    count = 16
    core = lax.rem(me, 2)
    xpos = lax.rem(me // 2, 2)
    other = me + 1 - 2 * core
    xpeer = me + 2 - 4 * xpos
    zp = lax.rem(me + 4, count)
    zm = lax.rem(me + 12, count)
    src = [
        zm,
        zp,
        lax.rem(me + 8, count),
        xpeer,
        lax.rem(xpeer + 12, count),
        lax.rem(xpeer + 4, count),
        lax.rem(xpeer + 8, count),
    ]
    src = src + [other] + [s + 1 - 2 * core for s in src]

    ypos = lax.axis_index("mdl")
    yp = lax.rem(ypos + 1, 4)
    ym = lax.rem(ypos + 3, 4)
    y2 = lax.rem(ypos + 2, 4)

    barrier = pltpu.get_barrier_semaphore()
    peers = [{"rep": zp}, {"rep": zm}, {"rep": xpeer}, {"rep": other}]
    peers += [{"mdl": yp}, {"mdl": ym}]
    for peer in peers:
        pl.semaphore_signal(barrier, inc=1, device_id=peer, device_id_type=MESH)

    total = count_ref[lax.axis_index("sec")]
    normed = rms_normed(x_ref[...].astype(F32)).astype(BF)
    live = me * rows + lax.broadcasted_iota(jnp.int32, (rows, HEAD), 0) < total
    for part in range(2):
        made = jnp.dot(normed, wkv_ref[part], preferred_element_type=F32)
        kv_ref[:, part * HEAD : (part + 1) * HEAD] = jnp.where(live, made, 0.0).astype(BF)
    pl.semaphore_wait(barrier, len(peers))

    def block_rows(block, part):
        return pl.ds(pl.multiple_of(block * rows + part * piece, piece), piece)

    def transfer(block, part, slot, target, lane, own=False):
        where = buf.at[block_rows(block, part), pl.ds(0, 2 * HEAD)]
        source = kv_ref.at[pl.ds(part * piece, piece)] if own else where
        return pltpu.make_async_remote_copy(
            src_ref=source,
            dst_ref=where,
            send_sem=send.at[lane, part],
            recv_sem=recv.at[slot, part],
            device_id={"rep": target},
            device_id_type=MESH,
        )

    plan = [
        (None, 3, xpeer),
        (None, 1, zm),
        (None, 0, zp),
        (None, 7, other),
        (1, 9, other),
        (0, 2, zp),
        (0, 8, other),
        (3, 5, zm),
        (3, 4, zp),
        (3, 11, other),
        (2, 10, other),
        (5, 6, zm),
        (5, 13, other),
        (4, 12, other),
        (6, 14, other),
    ]

    def plan_copy(index, part):
        from_slot, to_slot, target = plan[index]
        block = me if from_slot is None else src[from_slot]
        return transfer(block, part, to_slot, target, index, own=from_slot is None)

    def arrived(slot, part):
        where = buf.at[block_rows(src[slot], part), pl.ds(0, 2 * HEAD)]
        pltpu.make_async_copy(where, where, recv.at[slot, part]).wait()

    def pass_on(slot):
        for part in range(PIECES):
            arrived(slot, part)
            for index, (from_slot, _, _) in enumerate(plan):
                if from_slot == slot:
                    plan_copy(index, part).start()

    def take(slot):
        for part in range(PIECES):
            arrived(slot, part)

    for part in range(PIECES):
        for index in range(4):
            plan_copy(index, part).start()
    own_copy = pltpu.make_async_copy(
        kv_ref,
        buf.at[pl.ds(pl.multiple_of(me * rows, rows), rows), pl.ds(0, 2 * HEAD)],
        local.at[0],
    )
    own_copy.start()

    wrows = w_ref.shape[0]
    wpiece = wrows // 4
    wown = pltpu.make_async_copy(w_ref, wfull_ref.at[ypos], wlocal.at[0])
    wown.start()

    wsrc = [ym, yp, y2]

    def wcopy(source_y, which, part, slot, target, lane, own=False):
        span = pl.ds((2 * which + part) * wpiece, wpiece)
        where = wfull_ref.at[source_y, span]
        return pltpu.make_async_remote_copy(
            src_ref=w_ref.at[span] if own else where,
            dst_ref=where,
            send_sem=wsend.at[lane, part],
            recv_sem=wrecv.at[slot, part],
            device_id=target,
            device_id_type=MESH,
        )

    def wfirst(part):
        return [
            wcopy(ypos, core, part, 0, {"mdl": yp}, 0, own=True),
            wcopy(ypos, core, part, 1, {"mdl": ym}, 1, own=True),
        ]

    def wrelay(part):
        if part == 0:
            return wcopy(ym, core, 0, 2, {"mdl": yp}, 2)
        return wcopy(yp, core, 1, 2, {"mdl": ym}, 2)

    def wshare(slot, part):
        return wcopy(wsrc[slot], core, part, 3 + slot, {"rep": other}, 3 + slot)

    def warrived(slot, part):
        which = core if slot < 3 else 1 - core
        span = pl.ds((2 * which + part) * wpiece, wpiece)
        where = wfull_ref.at[wsrc[slot % 3], span]
        pltpu.make_async_copy(where, where, wrecv.at[slot, part]).wait()

    for part in range(2):
        for copy in wfirst(part):
            copy.start()

    queries = jnp.dot(normed, wq_ref[...], preferred_element_type=F32) * (HEAD ** (-0.5) * LOG2E)
    for head in range(heads):
        q_ref[head * rows : (head + 1) * rows, :] = queries[
            :, head * HEAD : (head + 1) * HEAD
        ].astype(BF)
    key_index = lax.broadcasted_iota(jnp.int32, (all_keys, HEAD), 0)
    buf[:, 2 * HEAD :] = jnp.where(key_index < total, 1.0, 0.0).astype(BF)
    acc[...] = jnp.zeros_like(acc)
    own_copy.wait()

    chip_rows = 2 * rows
    zpos = me // 4

    def step(i, carry):
        @pl.when(i == 0)
        def _():
            take(7)

        @pl.when(i == 1)
        def _():
            pass_on(1)
            pass_on(0)
            take(9)

        @pl.when(i == 2)
        def _():
            pass_on(3)
            take(8)

        @pl.when(i == 3)
        def _():
            pass_on(2)
            take(10)

        @pl.when(i == 4)
        def _():
            pass_on(5)
            take(11)

        @pl.when(i == 5)
        def _():
            for part in range(2):
                warrived(0, part)
                warrived(1, part)
                wrelay(part).start()
                wshare(0, part).start()
                wshare(1, part).start()

        @pl.when(i == 5)
        def _():
            pass_on(4)
            take(13)

        @pl.when(i == 6)
        def _():
            pass_on(6)
            take(12)

        @pl.when(i == 7)
        def _():
            take(14)

        j = lax.rem(i, 4)
        dz = j + (j // 2) * (1 - 2 * lax.rem(j, 2))
        dx = i // 4
        chip = lax.rem(zpos + dz, 4) * 2 + lax.rem(xpos + dx, 2)
        span = pl.ds(pl.multiple_of(chip * chip_rows, chip_rows), chip_rows)
        scores = lax.dot_general(
            q_ref[...],
            buf[span, :HEAD],
            (((1,), (1,)), ((), ())),
            preferred_element_type=F32,
        )
        weights = jnp.exp2(scores).astype(BF)
        acc[...] += jnp.dot(weights, buf[span, HEAD:], preferred_element_type=F32)
        return carry

    lax.fori_loop(0, 8, step, 0)

    for part in range(2):
        warrived(2, part)
        wshare(2, part).start()

    for head in range(heads):
        part = acc[head * rows : (head + 1) * rows, :]
        sums = part[:, HEAD:]
        safe = (sums > sum_low) & (sums < sum_high)
        out_ref[:, head * HEAD : (head + 1) * HEAD] = jnp.where(
            safe, part[:, :HEAD] / sums, jnp.nan
        ).astype(BF)

    for slot in range(3, 6):
        for part in range(2):
            warrived(slot, part)
    for part in range(2):
        for copy in wfirst(part):
            copy.wait_send()
        wrelay(part).wait_send()
        for slot in range(3):
            wshare(slot, part).wait_send()
    wown.wait()
    for part in range(PIECES):
        for index in range(len(plan)):
            plan_copy(index, part).wait_send()


def attend_call(counts, source, w_query, w_keyval, w, ident):
    heads = w_query.shape[1] // HEAD
    rows = source.shape[0]
    keys = rows * 16
    vmem = pl.BlockSpec(memory_space=pltpu.VMEM)
    anywhere = pl.BlockSpec(memory_space=pl.ANY)
    return pl.pallas_call(
        functools.partial(attend_kernel, heads),
        out_shape=[
            jax.ShapeDtypeStruct((rows, heads * HEAD), BF),
            jax.ShapeDtypeStruct((4,) + w.shape, BF),
        ],
        in_specs=[pl.BlockSpec(memory_space=pltpu.SMEM), vmem, vmem, vmem, anywhere],
        out_specs=[vmem, anywhere],
        scratch_shapes=[
            pltpu.VMEM((keys, 3 * HEAD), BF),
            pltpu.VMEM((heads * rows, 2 * HEAD), F32),
            pltpu.VMEM((heads * rows, HEAD), BF),
            pltpu.VMEM((rows, 2 * HEAD), BF),
            pltpu.SemaphoreType.DMA((15, PIECES)),
            pltpu.SemaphoreType.DMA((15, PIECES)),
            pltpu.SemaphoreType.DMA((1,)),
            pltpu.SemaphoreType.DMA((6, 2)),
            pltpu.SemaphoreType.DMA((6, 2)),
            pltpu.SemaphoreType.DMA((1,)),
        ],
        compiler_params=pltpu.CompilerParams(
            collective_id=ident, has_side_effects=True, vmem_limit_bytes=40 * 2**20
        ),
        cost_estimate=pl.CostEstimate(
            flops=4 * heads * rows * keys * HEAD,
            bytes_accessed=keys * 4 * HEAD,
            transcendentals=heads * rows * keys,
        ),
    )(counts, source, w_query, w_keyval, w)


def careful_kernel(total_ref, q_ref, kv_ref, out_ref, top, acc, total_sum):
    step = pl.program_id(0)
    block = kv_ref.shape[0]

    @pl.when(step == 0)
    def _():
        top[...] = jnp.full_like(top, masked_score)
        acc[...] = jnp.zeros_like(acc)
        total_sum[...] = jnp.zeros_like(total_sum)

    scores = lax.dot_general(
        q_ref[...], kv_ref[:, :HEAD], (((1,), (1,)), ((), ())), preferred_element_type=F32
    )
    key_index = step * block + lax.broadcasted_iota(jnp.int32, scores.shape, 1)
    live = key_index < total_ref[0]
    scores = jnp.where(live, scores, masked_score)
    old = top[...]
    new = jnp.maximum(old, jnp.max(scores, axis=1, keepdims=True))
    top[...] = new
    rescale = jnp.exp2(old - new)
    weights = jnp.where(live, jnp.exp2(scores - new[:, :1]), 0.0)
    total_sum[...] = total_sum[...] * rescale + jnp.sum(weights, axis=1, keepdims=True)
    acc[...] = acc[...] * rescale + jnp.dot(
        weights.astype(BF), kv_ref[:, HEAD:], preferred_element_type=F32
    )

    @pl.when(step == pl.num_programs(0) - 1)
    def _():
        rows, width = out_ref.shape
        for head in range(width // HEAD):
            span = slice(head * rows, (head + 1) * rows)
            out_ref[:, head * HEAD : (head + 1) * HEAD] = (acc[span, :] / total_sum[span, :]).astype(
                BF
            )


def careful_call(total, queries, kv_full, rows):
    heads = queries.shape[0] // rows
    block = 256
    return pl.pallas_call(
        careful_kernel,
        out_shape=jax.ShapeDtypeStruct((rows, heads * HEAD), BF),
        grid=(kv_full.shape[0] // block,),
        in_specs=[
            pl.BlockSpec(memory_space=pltpu.SMEM),
            pl.BlockSpec(queries.shape, lambda i: (0, 0)),
            pl.BlockSpec((block, 2 * HEAD), lambda i: (i, 0)),
        ],
        out_specs=pl.BlockSpec((rows, heads * HEAD), lambda i: (0, 0)),
        scratch_shapes=[pltpu.VMEM((heads * rows, HEAD), F32)] * 3,
        compiler_params=pltpu.CompilerParams(vmem_limit_bytes=20 * 2**20),
    )(total, queries, kv_full)


class YGather:
    def __init__(self, own_half, place, send, recv):
        self.ypos = lax.axis_index("mdl")
        self.yp = lax.rem(self.ypos + 1, 4)
        self.ym = lax.rem(self.ypos + 3, 4)
        self.y2 = lax.rem(self.ypos + 2, 4)
        self.own_half, self.place, self.send, self.recv = own_half, place, send, recv

    def greet(self, barrier):
        for peer in (self.yp, self.ym):
            pl.semaphore_signal(barrier, inc=1, device_id={"mdl": peer}, device_id_type=MESH)
        return 2

    def copy(self, source_y, part, slot, target, lane, own=False):
        return pltpu.make_async_remote_copy(
            src_ref=self.own_half(part) if own else self.place(source_y, part, lane - 2),
            dst_ref=self.place(source_y, part, slot),
            send_sem=self.send.at[lane, part],
            recv_sem=self.recv.at[slot, part],
            device_id={"mdl": target},
            device_id_type=MESH,
        )

    def first(self):
        return [
            self.copy(self.ypos, 0, 0, self.yp, 0, own=True),
            self.copy(self.ypos, 1, 1, self.ym, 1, own=True),
            self.copy(self.ypos, 1, 0, self.yp, 0, own=True),
            self.copy(self.ypos, 0, 1, self.ym, 1, own=True),
        ]

    def start(self):
        for item in self.first():
            item.start()

    def arrived(self, slot, part):
        where = self.place((self.ym, self.yp, self.y2)[slot], part, slot)
        pltpu.make_async_copy(where, where, self.recv.at[slot, part]).wait()

    def relay(self, part):
        if part == 0:
            return self.copy(self.ym, 0, 2, self.yp, 2)
        return self.copy(self.yp, 1, 2, self.ym, 3)

    def pass_on(self, part):
        self.arrived(part, part)
        self.relay(part).start()

    def wait_sent(self):
        for item in self.first():
            item.wait_send()
        for part in range(2):
            self.relay(part).wait_send()


class Geometry:
    def __init__(self, rows, columns, by_rows):
        self.by_rows = by_rows
        self.rows, self.columns = rows, columns
        if by_rows:
            self.half = (rows // 2, columns)
            self.quarter_shape = [(rows // 4, columns // 4)] * 2
            self.sub_shape = [(rows // 16, columns // 4)] * 2
        else:
            third = columns // 6
            self.half = (rows, columns // 2)
            self.quarter_shape = [(rows // 4, 2 * third), (rows // 4, third)]
            self.sub_shape = [(rows // 4, third // 2), (rows // 8, third // 2)]

    def whole(self, core):
        if self.by_rows:
            return (core * self.half[0], 0)
        return (0, core * self.half[1])

    def quarter(self, part, index):
        rows, columns = self.quarter_shape[part]
        if self.by_rows:
            return (part * rows, index * columns)
        return (index * rows, part * self.quarter_shape[0][1])

    def sub(self, part, index):
        rows, columns = self.sub_shape[part]
        if self.by_rows:
            return (index * rows, 0)
        if part == 0:
            return (0, index * columns)
        return ((index // 2) * rows, lax.rem(index, 2) * columns)

    def scatter_scratch(self):
        vmem = pltpu.VMEM
        return [vmem(self.half, BF)] * 3 + [vmem((3,) + q, BF) for q in self.quarter_shape]

    def sub_scratch(self):
        return [pltpu.VMEM((3,) + sub, BF) for sub in self.sub_shape]

    def semaphores(self):
        dma = pltpu.SemaphoreType.DMA
        return [dma((4, 2, 3)), dma((4, 2, 3)), dma((9,)), dma((9,))]


def box(start, shape):
    row, column = start
    return (
        pl.ds(row if isinstance(row, int) else pl.multiple_of(row, 16), shape[0]),
        pl.ds(column if isinstance(column, int) else pl.multiple_of(column, HEAD), shape[1]),
    )


def plus(left, right):
    return (left[0] + right[0], left[1] + right[1])


class Reduce:
    hops = (2, 1, 3)

    def __init__(self, shape, att_ref, d_ref, out_ref, scatter, sums, sub_in, semaphores):
        self.g = shape
        self.att, self.d, self.out = att_ref, d_ref, out_ref
        if scatter is not None:
            self.theirs, self.mine, self.got = scatter[:3]
            self.part_in = scatter[3:5]
        self.part_sum = sums
        self.sub_in = sub_in
        self.send, self.recv, self.csend, self.crecv = semaphores
        me = lax.axis_index("rep")
        self.me = me
        self.core = lax.rem(me, 2)
        self.other = me + 1 - 2 * self.core
        self.zpos = me // 4
        self.xpos = lax.rem(me // 2, 2) * 2 + lax.axis_index("sec")
        self.first = [self.xpos, self.zpos]
        self.second = [self.zpos, self.xpos]
        self.near = [self.at_x, self.at_z]

    def at_x(self, k):
        there = lax.rem(self.xpos + k, 4)
        return {"rep": self.zpos * 4 + (there // 2) * 2 + self.core, "sec": lax.rem(there, 2)}

    def at_z(self, k):
        return {"rep": lax.rem(self.me + 4 * k, 16)}

    def greet(self, barrier):
        for k in range(1, 4):
            pl.semaphore_signal(barrier, inc=1, device_id=self.at_x(k), device_id_type=MESH)
            pl.semaphore_signal(barrier, inc=1, device_id=self.at_z(k), device_id_type=MESH)
        pl.semaphore_signal(barrier, inc=1, device_id={"rep": self.other}, device_id_type=MESH)
        return 7

    def grad(self, which):
        left, right = self.att, self.d
        if self.g.by_rows:
            size = self.g.half[0]
            left = left[:, pl.ds(pl.multiple_of(which * size, size), size)]
            right = right[...]
        else:
            size = self.g.half[1]
            left = left[...]
            right = right[:, pl.ds(pl.multiple_of(which * size, HEAD), size)]
        return lax.dot_general(left, right, (((0,), (0,)), ((), ())), preferred_element_type=F32)

    def copy(self, source, target, send, recv, device):
        return pltpu.make_async_remote_copy(
            src_ref=source,
            dst_ref=target,
            send_sem=send,
            recv_sem=recv,
            device_id=device,
            device_id_type=MESH,
        )

    def swap(self):
        return self.copy(
            self.theirs, self.got, self.csend.at[0], self.crecv.at[0], {"rep": self.other}
        )

    def stage(self, level, part, k, source, target, device):
        return self.copy(
            source,
            target,
            self.send.at[level, part, k - 1],
            self.recv.at[level, part, k - 1],
            device,
        )

    def scatter_one(self, part, k):
        start = self.g.quarter(part, lax.rem(self.first[part] + k, 4))
        return self.stage(
            0,
            part,
            k,
            self.mine.at[box(start, self.g.quarter_shape[part])],
            self.part_in[part].at[k - 1],
            self.near[part](k),
        )

    def scatter_two(self, part, k):
        start = self.g.sub(part, lax.rem(self.second[part] + k, 4))
        return self.stage(
            1,
            part,
            k,
            self.part_sum[part].at[box(start, self.g.sub_shape[part])],
            self.sub_in[part].at[k - 1],
            self.near[1 - part](k),
        )

    def my_sub(self, part):
        start = plus(
            self.g.whole(self.core),
            plus(self.g.quarter(part, self.first[part]), self.g.sub(part, self.second[part])),
        )
        return box(start, self.g.sub_shape[part])

    def out_quarter(self, core, part, index):
        start = plus(self.g.whole(core), self.g.quarter(part, index))
        return self.out.at[box(start, self.g.quarter_shape[part])]

    def gather_two(self, part, k):
        where = self.out.at[self.my_sub(part)]
        return self.stage(2, part, k, where, where, self.near[1 - part](k))

    def gather_one(self, part, k):
        where = self.out_quarter(self.core, part, self.first[part])
        return self.stage(3, part, k, where, where, self.near[part](k))

    def share(self, part, k, core):
        where = self.out_quarter(core, part, lax.rem(self.first[part] + 4 - k, 4))
        index = 1 + part * 4 + k
        return self.copy(
            where, where, self.csend.at[index], self.crecv.at[index], {"rep": self.other}
        )

    def begin(self):
        self.theirs[...] = self.grad(1 - self.core).astype(BF)

    def swap_and_scatter(self):
        self.swap().start()
        self.scatter_own()

    def scatter_own(self):
        own = self.grad(self.core)
        self.swap().wait_recv()
        self.mine[...] = (own + self.got[...].astype(F32)).astype(BF)
        for k in self.hops:
            for part in range(2):
                self.scatter_one(part, k).start()

    def first_sums(self):
        for part in range(2):
            start = self.g.quarter(part, self.first[part])
            total = self.mine[box(start, self.g.quarter_shape[part])].astype(F32)
            for k in (1, 3, 2):
                self.scatter_one(part, k).wait_recv()
                total += self.part_in[part][k - 1].astype(F32)
            self.part_sum[part][...] = total.astype(BF)

    def second_scatter(self):
        for k in self.hops:
            for part in range(2):
                self.scatter_two(part, k).start()

    def first_gather(self):
        for part in range(2):
            start = self.g.sub(part, self.second[part])
            total = self.part_sum[part][box(start, self.g.sub_shape[part])].astype(F32)
            for k in (1, 3, 2):
                self.scatter_two(part, k).wait_recv()
                total += self.sub_in[part][k - 1].astype(F32)
            self.out[self.my_sub(part)] = total.astype(BF)
            for k in self.hops:
                self.gather_two(part, k).start()

    def second_gather(self):
        for part in range(2):
            for k in range(1, 4):
                self.gather_two(part, k).wait_recv()
            for k in self.hops:
                self.gather_one(part, k).start()
            self.share(part, 0, self.core).start()

    def last_shares(self):
        for k in (1, 3, 2):
            for part in range(2):
                self.gather_one(part, k).wait_recv()
                self.share(part, k, self.core).start()

    def finish_scatter(self):
        self.swap().wait_send()
        for part in range(2):
            for k in range(1, 4):
                self.scatter_one(part, k).wait_send()

    def finish(self):
        for part in range(2):
            for k in range(4):
                self.share(part, k, 1 - self.core).wait_recv()
        for part in range(2):
            for k in range(1, 4):
                self.scatter_two(part, k).wait_send()
                self.gather_two(part, k).wait_send()
                self.gather_one(part, k).wait_send()
            for k in range(4):
                self.share(part, k, self.core).wait_send()


def reduce_kernel(shape, att_ref, d_ref, out_ref, *scratch):
    each = len(scratch) // 2
    works = []
    for index in range(2):
        part = scratch[index * each : (index + 1) * each]
        span = pl.ds(index * shape.columns, shape.columns)
        works.append(
            Reduce(
                shape,
                att_ref,
                d_ref.at[:, span],
                out_ref.at[:, span],
                part[:5],
                part[5:7],
                part[7:9],
                part[9:13],
            )
        )
    early, late = works
    barrier = pltpu.get_barrier_semaphore()
    expected = early.greet(barrier)
    early.begin()
    pl.semaphore_wait(barrier, expected)
    early.swap().start()
    late.begin()
    late.swap().start()
    early.scatter_own()
    late.scatter_own()
    early.first_sums()
    early.second_scatter()
    late.first_sums()
    late.second_scatter()
    early.first_gather()
    late.first_gather()
    early.second_gather()
    late.second_gather()
    early.last_shares()
    late.last_shares()
    for work in works:
        work.finish_scatter()
        work.finish()


def reduced_grad(attended, grad_in, ident):
    shape = Geometry(attended.shape[1], grad_in.shape[1] // 2, True)
    vmem = pl.BlockSpec(memory_space=pltpu.VMEM)
    return pl.pallas_call(
        functools.partial(reduce_kernel, shape),
        out_shape=jax.ShapeDtypeStruct((attended.shape[1], grad_in.shape[1]), BF),
        in_specs=[vmem, vmem],
        out_specs=vmem,
        scratch_shapes=2
        * (
            shape.scatter_scratch()
            + [pltpu.VMEM(q, BF) for q in shape.quarter_shape]
            + shape.sub_scratch()
            + shape.semaphores()
        ),
        compiler_params=pltpu.CompilerParams(
            collective_id=ident, has_side_effects=True, vmem_limit_bytes=24 * 2**20
        ),
    )(attended, grad_in)


def policy_kernel(
    shape,
    count_ref,
    x_ref,
    cin_ref,
    wp_ref,
    action_ref,
    advantage_ref,
    old_ref,
    att_ref,
    out_ref,
    sum_a,
    sum_b,
    part_ref,
    d_ref,
    *refs,
):
    scatter, semaphores, (send, recv, local) = refs[:5], refs[5:9], refs[9:]
    work = Reduce(shape, att_ref, d_ref, None, scatter, (sum_a, sum_b), None, semaphores)
    rows, width = part_ref.shape
    half = rows // 2

    def place(source_y, part, slot):
        return out_ref.at[
            pl.ds(part * half, half), pl.ds(pl.multiple_of(source_y * width, HEAD), width)
        ]

    ring = YGather(lambda part: part_ref.at[pl.ds(part * half, half)], place, send, recv)
    barrier = pltpu.get_barrier_semaphore()
    expected = ring.greet(barrier) + work.greet(barrier)
    part_ref[...] = jnp.dot(x_ref[...], cin_ref[...], preferred_element_type=F32).astype(BF)
    pl.semaphore_wait(barrier, expected)
    ring.start()
    mine = pltpu.make_async_copy(
        part_ref, out_ref.at[:, pl.ds(pl.multiple_of(ring.ypos * width, HEAD), width)], local.at[0]
    )
    mine.start()
    d_ref[...] = policy_backward(
        x_ref[...],
        standing(action_ref[...]),
        standing(advantage_ref[...])[:, :1],
        standing(old_ref[...])[:, :1],
        live_scale(count_ref, rows),
        wp_ref[...],
    ).astype(BF)
    ring.pass_on(0)
    ring.pass_on(1)
    work.begin()
    work.swap_and_scatter()
    ring.arrived(0, 1)
    ring.arrived(1, 0)
    work.first_sums()
    ring.arrived(2, 0)
    ring.arrived(2, 1)
    work.finish_scatter()
    ring.wait_sent()
    mine.wait()


def policy_call(counts, hidden, c_in, w_policy, action, advantage, old_values, attended, ident):
    rows = hidden.shape[0]
    width = c_in.shape[1]
    shape = Geometry(attended.shape[1], hidden.shape[1], False)
    vmem = pl.BlockSpec(memory_space=pltpu.VMEM)
    return pl.pallas_call(
        functools.partial(policy_kernel, shape),
        out_shape=[jax.ShapeDtypeStruct((rows, 4 * width), BF)]
        + [jax.ShapeDtypeStruct(q, BF) for q in shape.quarter_shape],
        in_specs=[pl.BlockSpec(memory_space=pltpu.SMEM)] + [vmem] * 7,
        out_specs=[vmem] * 3,
        scratch_shapes=[pltpu.VMEM((rows, width), BF), pltpu.VMEM(hidden.shape, BF)]
        + shape.scatter_scratch()
        + shape.semaphores()
        + [
            pltpu.SemaphoreType.DMA((4, 2)),
            pltpu.SemaphoreType.DMA((3, 2)),
            pltpu.SemaphoreType.DMA((1,)),
        ],
        compiler_params=pltpu.CompilerParams(
            collective_id=ident, has_side_effects=True, vmem_limit_bytes=32 * 2**20
        ),
    )(counts, hidden, c_in, w_policy, action, advantage, old_values, attended)


def output_kernel(shape, x_ref, w_ref, base_ref, *refs):
    if shape is None:
        out_ref, acc, blocks, send, recv = refs
        work = None
    else:
        count_ref, return_ref, wv_ref, sum_a, sum_b, value_ref, out_ref, grad_ref = refs[:8]
        acc, blocks, send, recv, lanes = refs[8:13]
        work = Reduce(shape, None, None, grad_ref, None, (sum_a, sum_b), refs[13:15], refs[15:19])
    rows = x_ref.shape[0]
    half = rows // 2
    ring = YGather(
        lambda part: x_ref.at[pl.ds(part * half, half)],
        lambda source_y, part, slot: blocks.at[slot, pl.ds(part * half, half)],
        send,
        recv,
    )
    barrier = pltpu.get_barrier_semaphore()
    expected = ring.greet(barrier)
    if work is not None:
        expected += work.greet(barrier)
    pl.semaphore_wait(barrier, expected)
    ring.start()
    if work is not None:
        work.second_scatter()
    acc[...] = base_ref[...].astype(F32) + jnp.dot(
        x_ref[...], w_ref[ring.ypos], preferred_element_type=F32
    )

    def add(slot, part):
        source_y = (ring.ym, ring.yp, ring.y2)[slot]
        span = pl.ds(part * half, half)
        acc[span, :] += jnp.dot(
            blocks[slot, span, :], w_ref[source_y], preferred_element_type=F32
        )

    if work is not None:
        work.first_gather()
    ring.pass_on(0)
    ring.pass_on(1)
    add(0, 0)
    add(1, 1)
    if work is not None:
        work.second_gather()
    ring.arrived(0, 1)
    add(0, 1)
    ring.arrived(1, 0)
    add(1, 0)
    if work is not None:
        work.last_shares()
    ring.arrived(2, 0)
    add(2, 0)
    ring.arrived(2, 1)
    add(2, 1)
    if work is None:
        out_ref[...] = acc[...].astype(BF)
    else:
        value, out_ref[...] = value_backward(
            acc[...], standing(return_ref[...])[:, :1], live_scale(count_ref, rows), wv_ref[...]
        )
        lanes[...] = jnp.broadcast_to(value, lanes.shape)
        mine = lanes[pl.ds(pl.multiple_of(ring.ypos * value_ref.shape[1], 8), value_ref.shape[1]), :]
        value_ref[...] = jnp.transpose(mine)[:1]
    if work is not None:
        work.finish()
    ring.wait_sent()


def output_call(x, w_full, base, value_args, ident):
    rows, width = x.shape
    columns = w_full.shape[2]
    vmem = pl.BlockSpec(memory_space=pltpu.VMEM)
    args = [x, w_full, base]
    in_specs = [vmem] * 3
    out_shape = [jax.ShapeDtypeStruct((rows, columns), BF)]
    scratch = [
        pltpu.VMEM((rows, columns), F32),
        pltpu.VMEM((3, rows, width), BF),
        pltpu.SemaphoreType.DMA((4, 2)),
        pltpu.SemaphoreType.DMA((3, 2)),
    ]
    shape = None
    if value_args is not None:
        shape, counts, target, w_value, sums = value_args
        args += [counts, target, w_value] + list(sums)
        in_specs += [pl.BlockSpec(memory_space=pltpu.SMEM)] + [vmem] * 4
        out_shape = [jax.ShapeDtypeStruct((1, rows // 4), F32)] + out_shape
        scratch.append(pltpu.VMEM((rows, HEAD), F32))
        out_shape.append(jax.ShapeDtypeStruct((shape.rows, shape.columns), BF))
        scratch += shape.sub_scratch() + shape.semaphores()
    return pl.pallas_call(
        functools.partial(output_kernel, shape),
        out_shape=out_shape,
        in_specs=in_specs,
        out_specs=[vmem] * len(out_shape),
        scratch_shapes=scratch,
        compiler_params=pltpu.CompilerParams(
            collective_id=ident, has_side_effects=True, vmem_limit_bytes=(20 if shape is None else 32) * 2**20
        ),
    )(*args)


def stacked_queries(source, w_query):
    rows = source.shape[0]
    normed = rms_normed(source.astype(F32)).astype(BF)
    queries = (
        jnp.dot(normed, w_query, preferred_element_type=F32) * (HEAD ** (-0.5) * LOG2E)
    ).astype(BF)
    heads = queries.shape[1] // HEAD
    return jnp.transpose(queries.reshape(rows, heads, HEAD), (1, 0, 2)).reshape(heads * rows, HEAD)


def ring_gather(block, axis):
    count = lax.axis_size(axis)
    me = lax.axis_index(axis)
    onward = [(k, (k + 1) % count) for k in range(count)]
    blocks = jnp.zeros((count,) + block.shape, block.dtype)

    def turn(k, carried):
        blocks, moving = carried
        blocks = lax.dynamic_update_index_in_dim(blocks, moving, lax.rem(me + count - k, count), 0)
        return (blocks, lax.ppermute(moving, axis, onward))

    return lax.fori_loop(0, count, turn, (blocks, block))[0]


def ring_sum(block, axis):
    return jnp.sum(ring_gather(block, axis).astype(F32), axis=0)


def careful_attend(total, source, w_query, w_keyval):
    normed = rms_normed(source.astype(F32)).astype(BF)
    keyval = [jnp.dot(normed, w_keyval[part], preferred_element_type=F32) for part in range(2)]
    joined = jnp.concatenate(keyval, axis=1).astype(BF)
    everyone = ring_gather(joined, "rep").reshape(-1, 2 * HEAD)
    return careful_call(total, stacked_queries(source, w_query), everyone, source.shape[0])


def summed_grad(attended, grad_in):
    grad = lax.dot_general(
        attended, grad_in, (((0,), (0,)), ((), ())), preferred_element_type=F32
    )
    return ring_sum(ring_sum(grad.astype(BF), "rep").astype(BF), "sec")


def careful_path(
    obs, a_query, a_keyval, a_out, w_policy, c_in, c_query, c_keyval, c_out, w_value, columns, total
):
    attended = careful_attend(total, obs, a_query, a_keyval)
    mixed_sum = ring_sum(jnp.dot(attended, a_out, preferred_element_type=F32), "mdl")
    hidden = (obs.astype(F32) + mixed_sum).astype(BF)
    action, advantage, old_values, target, scale = columns
    dhidden = policy_backward(hidden, action, advantage, old_values, scale, w_policy).astype(BF)
    embed_part = jnp.dot(hidden, c_in, preferred_element_type=F32).astype(BF)
    embedded = jnp.concatenate(list(ring_gather(embed_part, "mdl")), axis=1)
    critic_attended = careful_attend(total, embedded, c_query, c_keyval)
    critic_sum = ring_sum(
        jnp.dot(critic_attended, c_out, preferred_element_type=F32), "mdl"
    )
    value, dmixed = value_backward(
        embedded.astype(F32) + critic_sum, target, scale, w_value[None, :]
    )
    part_rows = value.shape[0] // 4
    value = lax.dynamic_slice_in_dim(value[:, 0], lax.axis_index("mdl") * part_rows, part_rows, 0)
    return (value[None, :], summed_grad(attended, dhidden), summed_grad(critic_attended, dmixed))


def on_device(
    obs,
    a_query,
    a_keyval,
    a_out,
    w_policy,
    c_in,
    c_query,
    c_keyval,
    c_out,
    w_value,
    actions,
    advantages,
    old_logp,
    returns,
    robot_count,
):
    rows = obs.shape[1]

    def careful():
        total = robot_count[lax.axis_index("sec")]
        live = lax.axis_index("rep") * rows + lax.iota(jnp.int32, rows) < total
        scale = jnp.where(live, 1.0 / jnp.sum(robot_count).astype(F32), 0.0)
        columns = (actions[0], advantages[0], old_logp[0], returns[0], scale)
        return careful_path(
            obs[0],
            a_query,
            a_keyval,
            a_out,
            w_policy,
            c_in,
            c_query,
            c_keyval,
            c_out,
            w_value,
            tuple(column[:, None] for column in columns),
            total.reshape(1),
        )

    attended, a_out_full = attend_call(robot_count, obs[0], a_query, a_keyval, a_out, 1)
    (hidden,) = output_call(attended, a_out_full, obs[0], None, 3)
    embedded, *sums = policy_call(
        robot_count, hidden, c_in, w_policy, actions, advantages, old_logp, attended, 4
    )
    critic_attended, c_out_full = attend_call(
        robot_count, embedded, c_query, c_keyval, c_out, 2
    )
    shape = Geometry(attended.shape[1], hidden.shape[1], False)
    values, dmixed, actor_summed = output_call(
        critic_attended,
        c_out_full,
        embedded,
        (shape, robot_count, returns, w_value[None, :], sums),
        5,
    )
    critic_summed = reduced_grad(critic_attended, dmixed, 6)
    mark = critic_summed[0, 0].astype(F32)
    values, actor_grad, critic_grad = lax.cond(
        mark == mark,
        lambda: (values, actor_summed.astype(F32), critic_summed.astype(F32)),
        careful,
    )
    return (values, actor_grad, critic_grad)


def solution(mesh):
    return jax.shard_map(
        on_device,
        mesh=mesh,
        in_specs=(
            P("sec", "rep", None),
            P(None, "mdl"),
            P(None, None, "mdl"),
            P("mdl", None),
            P(),
            P(None, "mdl"),
            P(None, "mdl"),
            P(None, None, "mdl"),
            P("mdl", None),
            P(),
            P("sec", "rep"),
            P("sec", "rep"),
            P("sec", "rep"),
            P("sec", "rep"),
            P(),
        ),
        out_specs=(P("sec", ("rep", "mdl")), P("mdl", None), P("mdl", None)),
        check_vma=False,
    )
```

```python
import functools

import jax
import jax.numpy as jnp
from jax import lax
from jax.experimental import pallas as pl
from jax.experimental.pallas import tpu as pltpu
from jax.sharding import PartitionSpec as P

HEAD = 128
LOG2E = 1.4426950408889634
MESH = pl.DeviceIdType.MESH
BF = jnp.bfloat16
F32 = jnp.float32

epsilon = 1e-05
clip_range = 0.2
masked_score = -1e30
sum_low = 1e-20
sum_high = 1e25


def rms_normed(values_in):
    return values_in * lax.rsqrt(jnp.mean(values_in * values_in, axis=-1, keepdims=True) + epsilon)


def policy_backward(hidden, action, advantage, old_values, scale, w_policy):
    source = hidden.astype(F32)
    factor = lax.rsqrt(jnp.mean(source * source, axis=-1, keepdims=True) + epsilon)
    normed = source * factor
    logits = jnp.dot(normed.astype(BF), w_policy, preferred_element_type=F32)
    shifted = logits - jnp.max(logits, axis=-1, keepdims=True)
    log_probs = shifted - jnp.log(jnp.sum(jnp.exp(shifted), axis=-1, keepdims=True))
    command = lax.broadcasted_iota(jnp.int32, logits.shape, 1)
    onehot = (action == command).astype(F32)
    chosen = jnp.sum(onehot * log_probs, axis=-1, keepdims=True)
    prob_ratio = jnp.exp(chosen - old_values)
    plain_term = prob_ratio * advantage
    bounded = jnp.clip(prob_ratio, 1.0 - clip_range, 1.0 + clip_range) * advantage
    slope_term = jnp.where((scale > 0.0) & (plain_term <= bounded), -plain_term * scale, 0.0)
    dlogits = slope_term * (onehot - jnp.exp(log_probs))
    dnormed = lax.dot_general(
        dlogits.astype(BF), w_policy, (((1,), (1,)), ((), ())), preferred_element_type=F32
    )
    return factor * (dnormed - normed * jnp.mean(dnormed * normed, axis=-1, keepdims=True))


def value_backward(mixed_out, target, scale, w_value):
    factor = lax.rsqrt(jnp.mean(mixed_out * mixed_out, axis=-1, keepdims=True) + epsilon)
    normed = mixed_out * factor
    weight = w_value.astype(F32)
    value_pred = jnp.sum(normed.astype(BF).astype(F32) * weight, axis=-1, keepdims=True)
    slope_term = jnp.where(scale > 0.0, (value_pred - target) * scale, 0.0)
    dnormed = slope_term * weight
    inner = jnp.mean(dnormed * normed, axis=-1, keepdims=True)
    return (value_pred, (factor * (dnormed - normed * inner)).astype(BF))


def standing(row):
    return jnp.transpose(jnp.broadcast_to(row, (HEAD, row.shape[1])))


def live_scale(count_ref, rows):
    total = count_ref[lax.axis_index("sec")]
    both = jnp.full((rows, 1), count_ref[0] + count_ref[1], jnp.int32).astype(F32)
    index = lax.axis_index("rep") * rows + lax.broadcasted_iota(jnp.int32, (rows, 1), 0)
    return jnp.where(index < total, 1.0 / both, 0.0)


PIECES = 2


class WeightGather:
    def __init__(self, columns, own_ref, full_ref, semaphores):
        self.own, self.full = own_ref, full_ref
        self.send, self.recv, self.local = semaphores
        self.columns = pl.ds(*columns)
        self.piece = own_ref.shape[0] // 4
        me = lax.axis_index("rep")
        self.core = lax.rem(me, 2)
        self.other = me + 1 - 2 * self.core
        self.ypos = lax.axis_index("mdl")
        self.yp = lax.rem(self.ypos + 1, 4)
        self.ym = lax.rem(self.ypos + 3, 4)
        self.src = [self.ym, self.yp, lax.rem(self.ypos + 2, 4)]

    def span(self, which, part):
        return pl.ds(pl.multiple_of((2 * which + part) * self.piece, 16), self.piece)

    def copy(self, source_y, part, slot, target, lane, own=False):
        span = self.span(self.core, part)
        where = self.full.at[source_y, span]
        return pltpu.make_async_remote_copy(
            src_ref=self.own.at[span, self.columns] if own else where,
            dst_ref=where,
            send_sem=self.send.at[lane, part],
            recv_sem=self.recv.at[slot, part],
            device_id=target,
            device_id_type=MESH,
        )

    def first(self):
        up, down = {"mdl": self.yp}, {"mdl": self.ym}
        return [
            self.copy(self.ypos, 0, 0, up, 0, own=True),
            self.copy(self.ypos, 1, 1, down, 1, own=True),
            self.copy(self.ypos, 1, 0, up, 0, own=True),
            self.copy(self.ypos, 0, 1, down, 1, own=True),
        ]

    def kept(self):
        return pltpu.make_async_copy(
            self.own.at[:, self.columns], self.full.at[self.ypos], self.local.at[0]
        )

    def start(self):
        for item in self.first():
            item.start()
        self.kept().start()

    def relay(self, part):
        if part == 0:
            return self.copy(self.ym, 0, 2, {"mdl": self.yp}, 2)
        return self.copy(self.yp, 1, 2, {"mdl": self.ym}, 2)

    def share(self, slot, part):
        return self.copy(self.src[slot], part, 3 + slot, {"rep": self.other}, 3 + slot)

    def arrived(self, slot, part):
        which = self.core if slot < 3 else 1 - self.core
        where = self.full.at[self.src[slot % 3], self.span(which, part)]
        pltpu.make_async_copy(where, where, self.recv.at[slot, part]).wait()

    def pass_on(self):
        for part in range(2):
            self.arrived(part, part)
            self.relay(part).start()
            self.share(part, part).start()

    def take_rest(self):
        for part in range(2):
            self.arrived(1 - part, part)
            self.share(1 - part, part).start()

    def take_last(self):
        for part in range(2):
            self.arrived(2, part)
            self.share(2, part).start()

    def finish(self):
        for slot in range(3, 6):
            for part in range(2):
                self.arrived(slot, part)
        for item in self.first():
            item.wait_send()
        for part in range(2):
            self.relay(part).wait_send()
            for slot in range(3):
                self.share(slot, part).wait_send()
        self.kept().wait()


def attend_kernel(
    heads, spans, count_ref, x_ref, wq_ref, wkv_ref, *refs
):
    each = len(spans)
    w_refs, out_ref, full_refs = refs[:each], refs[each], refs[each + 1 : 2 * each + 1]
    buf, acc, q_ref, kv_ref, send, recv, local, *w_semaphores = refs[2 * each + 1 :]
    rows = x_ref.shape[0]
    piece = rows // PIECES
    all_keys = buf.shape[0]
    me = lax.axis_index("rep")
    count = 16
    core = lax.rem(me, 2)
    xpos = lax.rem(me // 2, 2)
    other = me + 1 - 2 * core
    xpeer = me + 2 - 4 * xpos
    zp = lax.rem(me + 4, count)
    zm = lax.rem(me + 12, count)
    src = [
        zm,
        zp,
        lax.rem(me + 8, count),
        xpeer,
        lax.rem(xpeer + 12, count),
        lax.rem(xpeer + 4, count),
        lax.rem(xpeer + 8, count),
    ]
    src = src + [other] + [s + 1 - 2 * core for s in src]

    ypos = lax.axis_index("mdl")
    yp = lax.rem(ypos + 1, 4)
    ym = lax.rem(ypos + 3, 4)

    barrier = pltpu.get_barrier_semaphore()
    peers = [{"rep": zp}, {"rep": zm}, {"rep": xpeer}, {"rep": other}]
    peers += [{"mdl": yp}, {"mdl": ym}]
    for peer in peers:
        pl.semaphore_signal(barrier, inc=1, device_id=peer, device_id_type=MESH)

    rings = [
        WeightGather(columns, w_refs[k], full_refs[k], w_semaphores[3 * k : 3 * k + 3])
        for k, columns in enumerate(spans)
    ]
    pl.semaphore_wait(barrier, len(peers))
    for ring in rings:
        ring.start()

    total = count_ref[lax.axis_index("sec")]
    normed = rms_normed(x_ref[...].astype(F32)).astype(BF)
    live = me * rows + lax.broadcasted_iota(jnp.int32, (rows, HEAD), 0) < total
    for part in range(2):
        made = jnp.dot(normed, wkv_ref[part], preferred_element_type=F32)
        kv_ref[:, part * HEAD : (part + 1) * HEAD] = jnp.where(live, made, 0.0).astype(BF)

    def block_rows(block, part):
        return pl.ds(pl.multiple_of(block * rows + part * piece, piece), piece)

    def transfer(block, part, slot, target, lane, own=False):
        where = buf.at[block_rows(block, part), pl.ds(0, 2 * HEAD)]
        source = kv_ref.at[pl.ds(part * piece, piece)] if own else where
        return pltpu.make_async_remote_copy(
            src_ref=source,
            dst_ref=where,
            send_sem=send.at[lane, part],
            recv_sem=recv.at[slot, part],
            device_id={"rep": target},
            device_id_type=MESH,
        )

    plan = [
        (None, 3, xpeer),
        (None, 1, zm),
        (None, 0, zp),
        (None, 7, other),
        (1, 9, other),
        (0, 2, zp),
        (0, 8, other),
        (3, 5, zm),
        (3, 4, zp),
        (3, 11, other),
        (2, 10, other),
        (5, 6, zm),
        (5, 13, other),
        (4, 12, other),
        (6, 14, other),
    ]

    def plan_copy(index, part):
        from_slot, to_slot, target = plan[index]
        block = me if from_slot is None else src[from_slot]
        return transfer(block, part, to_slot, target, index, own=from_slot is None)

    def arrived(slot, part):
        where = buf.at[block_rows(src[slot], part), pl.ds(0, 2 * HEAD)]
        pltpu.make_async_copy(where, where, recv.at[slot, part]).wait()

    def pass_on(slot):
        for part in range(PIECES):
            arrived(slot, part)
            for index, (from_slot, _, _) in enumerate(plan):
                if from_slot == slot:
                    plan_copy(index, part).start()

    def take(slot):
        for part in range(PIECES):
            arrived(slot, part)

    for part in range(PIECES):
        for index in range(4):
            plan_copy(index, part).start()
    own_copy = pltpu.make_async_copy(
        kv_ref,
        buf.at[pl.ds(pl.multiple_of(me * rows, rows), rows), pl.ds(0, 2 * HEAD)],
        local.at[0],
    )
    own_copy.start()

    queries = jnp.dot(normed, wq_ref[...], preferred_element_type=F32) * (HEAD ** (-0.5) * LOG2E)
    for head in range(heads):
        q_ref[head * rows : (head + 1) * rows, :] = queries[
            :, head * HEAD : (head + 1) * HEAD
        ].astype(BF)
    key_index = lax.broadcasted_iota(jnp.int32, (all_keys, HEAD), 0)
    buf[:, 2 * HEAD :] = jnp.where(key_index < total, 1.0, 0.0).astype(BF)
    acc[...] = jnp.zeros_like(acc)
    own_copy.wait()

    chip_rows = 2 * rows
    zpos = me // 4

    def step(i, carry):
        @pl.when(i == 0)
        def _():
            take(7)

        @pl.when(i == 1)
        def _():
            pass_on(1)
            pass_on(0)
            take(9)

        @pl.when(i == 2)
        def _():
            pass_on(3)
            take(8)

        @pl.when(i == 3)
        def _():
            pass_on(2)
            take(10)

        @pl.when(i == 4)
        def _():
            pass_on(5)
            take(11)

        for k, ring in enumerate(rings):
            pl.when(i == 3 + 2 * k)(ring.pass_on)
            pl.when(i == (5, 7)[k] if each > 1 else i == 7)(ring.take_rest)

        @pl.when(i == 5)
        def _():
            pass_on(4)
            take(13)

        @pl.when(i == 6)
        def _():
            pass_on(6)
            take(12)

        @pl.when(i == 7)
        def _():
            take(14)

        j = lax.rem(i, 4)
        dz = j + (j // 2) * (1 - 2 * lax.rem(j, 2))
        dx = i // 4
        chip = lax.rem(zpos + dz, 4) * 2 + lax.rem(xpos + dx, 2)
        span = pl.ds(pl.multiple_of(chip * chip_rows, chip_rows), chip_rows)
        scores = lax.dot_general(
            q_ref[...],
            buf[span, :HEAD],
            (((1,), (1,)), ((), ())),
            preferred_element_type=F32,
        )
        weights = jnp.exp2(scores).astype(BF)
        acc[...] += jnp.dot(weights, buf[span, HEAD:], preferred_element_type=F32)
        return carry

    lax.fori_loop(0, 8, step, 0)

    for ring in rings:
        ring.take_last()

    for head in range(heads):
        part = acc[head * rows : (head + 1) * rows, :]
        sums = part[:, HEAD:]
        safe = (sums > sum_low) & (sums < sum_high)
        out_ref[:, head * HEAD : (head + 1) * HEAD] = jnp.where(
            safe, part[:, :HEAD] / sums, jnp.nan
        ).astype(BF)

    for ring in rings:
        ring.finish()
    for part in range(PIECES):
        for index in range(len(plan)):
            plan_copy(index, part).wait_send()


def attend_call(counts, source, w_query, w_keyval, weights, ident):
    heads = w_query.shape[1] // HEAD
    rows = source.shape[0]
    keys = rows * 16
    vmem = pl.BlockSpec(memory_space=pltpu.VMEM)
    anywhere = pl.BlockSpec(memory_space=pl.ANY)
    return pl.pallas_call(
        functools.partial(attend_kernel, heads, tuple(columns for _, columns in weights)),
        out_shape=[
            jax.ShapeDtypeStruct((rows, heads * HEAD), BF),
        ]
        + [
            jax.ShapeDtypeStruct((4, w.shape[0], columns[1]), BF) for w, columns in weights
        ],
        in_specs=[pl.BlockSpec(memory_space=pltpu.SMEM), vmem, vmem, vmem]
        + [anywhere] * len(weights),
        out_specs=[vmem] + [anywhere] * len(weights),
        scratch_shapes=[
            pltpu.VMEM((keys, 3 * HEAD), BF),
            pltpu.VMEM((heads * rows, 2 * HEAD), F32),
            pltpu.VMEM((heads * rows, HEAD), BF),
            pltpu.VMEM((rows, 2 * HEAD), BF),
            pltpu.SemaphoreType.DMA((15, PIECES)),
            pltpu.SemaphoreType.DMA((15, PIECES)),
            pltpu.SemaphoreType.DMA((1,)),
        ]
        + [
            pltpu.SemaphoreType.DMA((6, 2)),
            pltpu.SemaphoreType.DMA((6, 2)),
            pltpu.SemaphoreType.DMA((1,)),
        ]
        * len(weights),
        compiler_params=pltpu.CompilerParams(
            collective_id=ident, has_side_effects=True, vmem_limit_bytes=40 * 2**20
        ),
        cost_estimate=pl.CostEstimate(
            flops=4 * heads * rows * keys * HEAD,
            bytes_accessed=keys * 4 * HEAD,
            transcendentals=heads * rows * keys,
        ),
    )(counts, source, w_query, w_keyval, *(w for w, _ in weights))


def careful_kernel(total_ref, q_ref, kv_ref, out_ref, top, acc, total_sum):
    step = pl.program_id(0)
    block = kv_ref.shape[0]

    @pl.when(step == 0)
    def _():
        top[...] = jnp.full_like(top, masked_score)
        acc[...] = jnp.zeros_like(acc)
        total_sum[...] = jnp.zeros_like(total_sum)

    scores = lax.dot_general(
        q_ref[...], kv_ref[:, :HEAD], (((1,), (1,)), ((), ())), preferred_element_type=F32
    )
    key_index = step * block + lax.broadcasted_iota(jnp.int32, scores.shape, 1)
    live = key_index < total_ref[0]
    scores = jnp.where(live, scores, masked_score)
    old = top[...]
    new = jnp.maximum(old, jnp.max(scores, axis=1, keepdims=True))
    top[...] = new
    rescale = jnp.exp2(old - new)
    weights = jnp.where(live, jnp.exp2(scores - new[:, :1]), 0.0)
    total_sum[...] = total_sum[...] * rescale + jnp.sum(weights, axis=1, keepdims=True)
    acc[...] = acc[...] * rescale + jnp.dot(
        weights.astype(BF), kv_ref[:, HEAD:], preferred_element_type=F32
    )

    @pl.when(step == pl.num_programs(0) - 1)
    def _():
        rows, width = out_ref.shape
        for head in range(width // HEAD):
            span = slice(head * rows, (head + 1) * rows)
            out_ref[:, head * HEAD : (head + 1) * HEAD] = (acc[span, :] / total_sum[span, :]).astype(
                BF
            )


def careful_call(total, queries, kv_full, rows):
    heads = queries.shape[0] // rows
    block = 256
    return pl.pallas_call(
        careful_kernel,
        out_shape=jax.ShapeDtypeStruct((rows, heads * HEAD), BF),
        grid=(kv_full.shape[0] // block,),
        in_specs=[
            pl.BlockSpec(memory_space=pltpu.SMEM),
            pl.BlockSpec(queries.shape, lambda i: (0, 0)),
            pl.BlockSpec((block, 2 * HEAD), lambda i: (i, 0)),
        ],
        out_specs=pl.BlockSpec((rows, heads * HEAD), lambda i: (0, 0)),
        scratch_shapes=[pltpu.VMEM((heads * rows, HEAD), F32)] * 3,
        compiler_params=pltpu.CompilerParams(vmem_limit_bytes=20 * 2**20),
    )(total, queries, kv_full)


class YGather:
    def __init__(self, own_half, place, send, recv):
        self.ypos = lax.axis_index("mdl")
        self.yp = lax.rem(self.ypos + 1, 4)
        self.ym = lax.rem(self.ypos + 3, 4)
        self.y2 = lax.rem(self.ypos + 2, 4)
        self.own_half, self.place, self.send, self.recv = own_half, place, send, recv

    def greet(self, barrier):
        for peer in (self.yp, self.ym):
            pl.semaphore_signal(barrier, inc=1, device_id={"mdl": peer}, device_id_type=MESH)
        return 2

    def copy(self, source_y, part, slot, target, lane, own=False):
        return pltpu.make_async_remote_copy(
            src_ref=self.own_half(part) if own else self.place(source_y, part, lane - 2),
            dst_ref=self.place(source_y, part, slot),
            send_sem=self.send.at[lane, part],
            recv_sem=self.recv.at[slot, part],
            device_id={"mdl": target},
            device_id_type=MESH,
        )

    def first(self):
        return [
            self.copy(self.ypos, 0, 0, self.yp, 0, own=True),
            self.copy(self.ypos, 1, 1, self.ym, 1, own=True),
            self.copy(self.ypos, 1, 0, self.yp, 0, own=True),
            self.copy(self.ypos, 0, 1, self.ym, 1, own=True),
        ]

    def start(self):
        for item in self.first():
            item.start()

    def arrived(self, slot, part):
        where = self.place((self.ym, self.yp, self.y2)[slot], part, slot)
        pltpu.make_async_copy(where, where, self.recv.at[slot, part]).wait()

    def relay(self, part):
        if part == 0:
            return self.copy(self.ym, 0, 2, self.yp, 2)
        return self.copy(self.yp, 1, 2, self.ym, 3)

    def pass_on(self, part):
        self.arrived(part, part)
        self.relay(part).start()

    def wait_sent(self):
        for item in self.first():
            item.wait_send()
        for part in range(2):
            self.relay(part).wait_send()


class Geometry:
    def __init__(self, rows, columns, by_rows):
        self.by_rows = by_rows
        self.rows, self.columns = rows, columns
        if by_rows:
            self.half = (rows // 2, columns)
            self.quarter_shape = [(rows // 4, columns // 4)] * 2
            self.sub_shape = [(rows // 16, columns // 4)] * 2
        else:
            third = columns // 6
            self.half = (rows, columns // 2)
            self.quarter_shape = [(rows // 4, 2 * third), (rows // 4, third)]
            self.sub_shape = [(rows // 4, third // 2), (rows // 8, third // 2)]

    def whole(self, core):
        if self.by_rows:
            return (core * self.half[0], 0)
        return (0, core * self.half[1])

    def quarter(self, part, index):
        rows, columns = self.quarter_shape[part]
        if self.by_rows:
            return (part * rows, index * columns)
        return (index * rows, part * self.quarter_shape[0][1])

    def sub(self, part, index):
        rows, columns = self.sub_shape[part]
        if self.by_rows:
            return (index * rows, 0)
        if part == 0:
            return (0, index * columns)
        return ((index // 2) * rows, lax.rem(index, 2) * columns)

    def scatter_scratch(self):
        vmem = pltpu.VMEM
        return [vmem(self.half, BF)] * 3 + [vmem((3,) + q, BF) for q in self.quarter_shape]

    def sub_scratch(self):
        return [pltpu.VMEM((3,) + sub, BF) for sub in self.sub_shape]

    def semaphores(self):
        dma = pltpu.SemaphoreType.DMA
        return [dma((4, 2, 3)), dma((4, 2, 3)), dma((9,)), dma((9,))]


def box(start, shape):
    row, column = start
    return (
        pl.ds(row if isinstance(row, int) else pl.multiple_of(row, 16), shape[0]),
        pl.ds(column if isinstance(column, int) else pl.multiple_of(column, HEAD), shape[1]),
    )


def plus(left, right):
    return (left[0] + right[0], left[1] + right[1])


class Reduce:
    hops = (2, 1, 3)

    def __init__(self, shape, att_ref, d_ref, out_ref, scatter, sums, sub_in, semaphores):
        self.g = shape
        self.att, self.d, self.out = att_ref, d_ref, out_ref
        if scatter is not None:
            self.theirs, self.mine, self.got = scatter[:3]
            self.part_in = scatter[3:5]
        self.part_sum = sums
        self.sub_in = sub_in
        self.send, self.recv, self.csend, self.crecv = semaphores
        me = lax.axis_index("rep")
        self.me = me
        self.core = lax.rem(me, 2)
        self.other = me + 1 - 2 * self.core
        self.zpos = me // 4
        self.xpos = lax.rem(me // 2, 2) * 2 + lax.axis_index("sec")
        self.first = [self.xpos, self.zpos]
        self.second = [self.zpos, self.xpos]
        self.near = [self.at_x, self.at_z]

    def at_x(self, k):
        there = lax.rem(self.xpos + k, 4)
        return {"rep": self.zpos * 4 + (there // 2) * 2 + self.core, "sec": lax.rem(there, 2)}

    def at_z(self, k):
        return {"rep": lax.rem(self.me + 4 * k, 16)}

    def greet(self, barrier):
        for k in range(1, 4):
            pl.semaphore_signal(barrier, inc=1, device_id=self.at_x(k), device_id_type=MESH)
            pl.semaphore_signal(barrier, inc=1, device_id=self.at_z(k), device_id_type=MESH)
        pl.semaphore_signal(barrier, inc=1, device_id={"rep": self.other}, device_id_type=MESH)
        return 7

    def grad(self, which):
        left, right = self.att, self.d
        if self.g.by_rows:
            size = self.g.half[0]
            left = left[:, pl.ds(pl.multiple_of(which * size, size), size)]
            right = right[...]
        else:
            size = self.g.half[1]
            left = left[...]
            right = right[:, pl.ds(pl.multiple_of(which * size, HEAD), size)]
        return lax.dot_general(left, right, (((0,), (0,)), ((), ())), preferred_element_type=F32)

    def copy(self, source, target, send, recv, device):
        return pltpu.make_async_remote_copy(
            src_ref=source,
            dst_ref=target,
            send_sem=send,
            recv_sem=recv,
            device_id=device,
            device_id_type=MESH,
        )

    def swap(self):
        return self.copy(
            self.theirs, self.got, self.csend.at[0], self.crecv.at[0], {"rep": self.other}
        )

    def stage(self, level, part, k, source, target, device):
        return self.copy(
            source,
            target,
            self.send.at[level, part, k - 1],
            self.recv.at[level, part, k - 1],
            device,
        )

    def scatter_one(self, part, k):
        start = self.g.quarter(part, lax.rem(self.first[part] + k, 4))
        return self.stage(
            0,
            part,
            k,
            self.mine.at[box(start, self.g.quarter_shape[part])],
            self.part_in[part].at[k - 1],
            self.near[part](k),
        )

    def scatter_two(self, part, k):
        start = self.g.sub(part, lax.rem(self.second[part] + k, 4))
        return self.stage(
            1,
            part,
            k,
            self.part_sum[part].at[box(start, self.g.sub_shape[part])],
            self.sub_in[part].at[k - 1],
            self.near[1 - part](k),
        )

    def my_sub(self, part):
        start = plus(
            self.g.whole(self.core),
            plus(self.g.quarter(part, self.first[part]), self.g.sub(part, self.second[part])),
        )
        return box(start, self.g.sub_shape[part])

    def out_quarter(self, core, part, index):
        start = plus(self.g.whole(core), self.g.quarter(part, index))
        return self.out.at[box(start, self.g.quarter_shape[part])]

    def gather_two(self, part, k):
        where = self.out.at[self.my_sub(part)]
        return self.stage(2, part, k, where, where, self.near[1 - part](k))

    def gather_one(self, part, k):
        where = self.out_quarter(self.core, part, self.first[part])
        return self.stage(3, part, k, where, where, self.near[part](k))

    def share(self, part, k, core):
        where = self.out_quarter(core, part, lax.rem(self.first[part] + 4 - k, 4))
        index = 1 + part * 4 + k
        return self.copy(
            where, where, self.csend.at[index], self.crecv.at[index], {"rep": self.other}
        )

    def begin(self):
        self.theirs[...] = self.grad(1 - self.core).astype(BF)

    def swap_and_scatter(self):
        self.swap().start()
        self.scatter_own()

    def scatter_own(self):
        own = self.grad(self.core)
        self.swap().wait_recv()
        self.mine[...] = (own + self.got[...].astype(F32)).astype(BF)
        for k in self.hops:
            for part in range(2):
                self.scatter_one(part, k).start()

    def first_sums(self):
        for part in range(2):
            start = self.g.quarter(part, self.first[part])
            total = self.mine[box(start, self.g.quarter_shape[part])].astype(F32)
            for k in (1, 3, 2):
                self.scatter_one(part, k).wait_recv()
                total += self.part_in[part][k - 1].astype(F32)
            self.part_sum[part][...] = total.astype(BF)

    def second_scatter(self):
        for k in self.hops:
            for part in range(2):
                self.scatter_two(part, k).start()

    def first_gather(self):
        for part in range(2):
            start = self.g.sub(part, self.second[part])
            total = self.part_sum[part][box(start, self.g.sub_shape[part])].astype(F32)
            for k in (1, 3, 2):
                self.scatter_two(part, k).wait_recv()
                total += self.sub_in[part][k - 1].astype(F32)
            self.out[self.my_sub(part)] = total.astype(BF)
            for k in self.hops:
                self.gather_two(part, k).start()

    def second_gather(self):
        for part in range(2):
            for k in range(1, 4):
                self.gather_two(part, k).wait_recv()
            for k in self.hops:
                self.gather_one(part, k).start()
            self.share(part, 0, self.core).start()

    def last_shares(self):
        for k in (1, 3, 2):
            for part in range(2):
                self.gather_one(part, k).wait_recv()
                self.share(part, k, self.core).start()

    def finish_scatter(self):
        self.swap().wait_send()
        for part in range(2):
            for k in range(1, 4):
                self.scatter_one(part, k).wait_send()

    def finish(self):
        for part in range(2):
            for k in range(4):
                self.share(part, k, 1 - self.core).wait_recv()
        for part in range(2):
            for k in range(1, 4):
                self.scatter_two(part, k).wait_send()
                self.gather_two(part, k).wait_send()
                self.gather_one(part, k).wait_send()
            for k in range(4):
                self.share(part, k, self.core).wait_send()


def reduce_kernel(shape, att_ref, d_ref, out_ref, *scratch):
    each = len(scratch) // 2
    works = []
    for index in range(2):
        part = scratch[index * each : (index + 1) * each]
        span = pl.ds(index * shape.columns, shape.columns)
        works.append(
            Reduce(
                shape,
                att_ref,
                d_ref.at[:, span],
                out_ref.at[:, span],
                part[:5],
                part[5:7],
                part[7:9],
                part[9:13],
            )
        )
    early, late = works
    barrier = pltpu.get_barrier_semaphore()
    expected = early.greet(barrier)
    early.begin()
    pl.semaphore_wait(barrier, expected)
    early.swap().start()
    late.begin()
    late.swap().start()
    early.scatter_own()
    late.scatter_own()
    early.first_sums()
    early.second_scatter()
    late.first_sums()
    late.second_scatter()
    early.first_gather()
    late.first_gather()
    early.second_gather()
    late.second_gather()
    early.last_shares()
    late.last_shares()
    for work in works:
        work.finish_scatter()
        work.finish()


def reduced_grad(attended, grad_in, ident):
    shape = Geometry(attended.shape[1], grad_in.shape[1] // 2, True)
    vmem = pl.BlockSpec(memory_space=pltpu.VMEM)
    return pl.pallas_call(
        functools.partial(reduce_kernel, shape),
        out_shape=jax.ShapeDtypeStruct((attended.shape[1], grad_in.shape[1]), BF),
        in_specs=[vmem, vmem],
        out_specs=vmem,
        scratch_shapes=2
        * (
            shape.scatter_scratch()
            + [pltpu.VMEM(q, BF) for q in shape.quarter_shape]
            + shape.sub_scratch()
            + shape.semaphores()
        ),
        compiler_params=pltpu.CompilerParams(
            collective_id=ident, has_side_effects=True, vmem_limit_bytes=24 * 2**20
        ),
    )(attended, grad_in)


def policy_kernel(
    shape,
    count_ref,
    x_ref,
    cin_ref,
    wp_ref,
    action_ref,
    advantage_ref,
    old_ref,
    att_ref,
    out_ref,
    sum_a,
    sum_b,
    part_ref,
    d_ref,
    *refs,
):
    scatter, semaphores, (send, recv, local) = refs[:5], refs[5:9], refs[9:]
    work = Reduce(shape, att_ref, d_ref, None, scatter, (sum_a, sum_b), None, semaphores)
    rows, width = part_ref.shape
    half = rows // 2

    def place(source_y, part, slot):
        return out_ref.at[
            pl.ds(part * half, half), pl.ds(pl.multiple_of(source_y * width, HEAD), width)
        ]

    ring = YGather(lambda part: part_ref.at[pl.ds(part * half, half)], place, send, recv)
    barrier = pltpu.get_barrier_semaphore()
    expected = ring.greet(barrier) + work.greet(barrier)
    part_ref[...] = jnp.dot(x_ref[...], cin_ref[...], preferred_element_type=F32).astype(BF)
    pl.semaphore_wait(barrier, expected)
    ring.start()
    mine = pltpu.make_async_copy(
        part_ref, out_ref.at[:, pl.ds(pl.multiple_of(ring.ypos * width, HEAD), width)], local.at[0]
    )
    mine.start()
    d_ref[...] = policy_backward(
        x_ref[...],
        standing(action_ref[...]),
        standing(advantage_ref[...])[:, :1],
        standing(old_ref[...])[:, :1],
        live_scale(count_ref, rows),
        wp_ref[...],
    ).astype(BF)
    ring.pass_on(0)
    ring.pass_on(1)
    work.begin()
    work.swap_and_scatter()
    ring.arrived(0, 1)
    ring.arrived(1, 0)
    work.first_sums()
    ring.arrived(2, 0)
    ring.arrived(2, 1)
    work.finish_scatter()
    ring.wait_sent()
    mine.wait()


def policy_call(counts, hidden, c_in, w_policy, action, advantage, old_values, attended, ident):
    rows = hidden.shape[0]
    width = c_in.shape[1]
    shape = Geometry(attended.shape[1], hidden.shape[1], False)
    vmem = pl.BlockSpec(memory_space=pltpu.VMEM)
    return pl.pallas_call(
        functools.partial(policy_kernel, shape),
        out_shape=[jax.ShapeDtypeStruct((rows, 4 * width), BF)]
        + [jax.ShapeDtypeStruct(q, BF) for q in shape.quarter_shape],
        in_specs=[pl.BlockSpec(memory_space=pltpu.SMEM)] + [vmem] * 7,
        out_specs=[vmem] * 3,
        scratch_shapes=[pltpu.VMEM((rows, width), BF), pltpu.VMEM(hidden.shape, BF)]
        + shape.scatter_scratch()
        + shape.semaphores()
        + [
            pltpu.SemaphoreType.DMA((4, 2)),
            pltpu.SemaphoreType.DMA((3, 2)),
            pltpu.SemaphoreType.DMA((1,)),
        ],
        compiler_params=pltpu.CompilerParams(
            collective_id=ident, has_side_effects=True, vmem_limit_bytes=32 * 2**20
        ),
    )(counts, hidden, c_in, w_policy, action, advantage, old_values, attended)


def output_kernel(shape, starts, x_ref, base_ref, *refs):
    w_refs, refs = refs[: len(starts)], refs[len(starts) :]
    if shape is None:
        out_ref, acc, blocks, send, recv = refs
        work = None
    else:
        count_ref, return_ref, wv_ref, sum_a, sum_b, value_ref, out_ref, grad_ref = refs[:8]
        acc, blocks, send, recv, lanes = refs[8:13]
        work = Reduce(shape, None, None, grad_ref, None, (sum_a, sum_b), refs[13:15], refs[15:19])
    rows = x_ref.shape[0]
    half = rows // 2
    ring = YGather(
        lambda part: x_ref.at[pl.ds(part * half, half)],
        lambda source_y, part, slot: blocks.at[slot, pl.ds(part * half, half)],
        send,
        recv,
    )
    barrier = pltpu.get_barrier_semaphore()
    expected = ring.greet(barrier)
    if work is not None:
        expected += work.greet(barrier)
    pl.semaphore_wait(barrier, expected)
    ring.start()
    if work is not None:
        work.second_scatter()
    for start, w_ref in zip(starts, w_refs):
        columns = slice(start, start + w_ref.shape[2])
        acc[:, columns] = base_ref[:, columns].astype(F32) + jnp.dot(
            x_ref[...], w_ref[ring.ypos], preferred_element_type=F32
        )

    def add(slot, part):
        source_y = (ring.ym, ring.yp, ring.y2)[slot]
        span = pl.ds(part * half, half)
        for start, w_ref in zip(starts, w_refs):
            columns = slice(start, start + w_ref.shape[2])
            acc[span, columns] += jnp.dot(
                blocks[slot, span, :], w_ref[source_y], preferred_element_type=F32
            )

    if work is not None:
        work.first_gather()
    ring.pass_on(0)
    ring.pass_on(1)
    add(0, 0)
    add(1, 1)
    if work is not None:
        work.second_gather()
    ring.arrived(0, 1)
    add(0, 1)
    ring.arrived(1, 0)
    add(1, 0)
    if work is not None:
        work.last_shares()
    ring.arrived(2, 0)
    add(2, 0)
    ring.arrived(2, 1)
    add(2, 1)
    if work is None:
        out_ref[...] = acc[...].astype(BF)
    else:
        value, out_ref[...] = value_backward(
            acc[...], standing(return_ref[...])[:, :1], live_scale(count_ref, rows), wv_ref[...]
        )
        lanes[...] = jnp.broadcast_to(value, lanes.shape)
        mine = lanes[pl.ds(pl.multiple_of(ring.ypos * value_ref.shape[1], 8), value_ref.shape[1]), :]
        value_ref[...] = jnp.transpose(mine)[:1]
    if work is not None:
        work.finish()
    ring.wait_sent()


def output_call(x, weights, base, value_args, ident):
    rows, width = x.shape
    columns = base.shape[1]
    starts = []
    for w_full in weights:
        starts.append(sum(other.shape[2] for other in weights[: len(starts)]))
    vmem = pl.BlockSpec(memory_space=pltpu.VMEM)
    args = [x, base] + list(weights)
    in_specs = [vmem] * len(args)
    out_shape = [jax.ShapeDtypeStruct((rows, columns), BF)]
    scratch = [
        pltpu.VMEM((rows, columns), F32),
        pltpu.VMEM((3, rows, width), BF),
        pltpu.SemaphoreType.DMA((4, 2)),
        pltpu.SemaphoreType.DMA((3, 2)),
    ]
    shape = None
    if value_args is not None:
        shape, counts, target, w_value, sums = value_args
        args += [counts, target, w_value] + list(sums)
        in_specs += [pl.BlockSpec(memory_space=pltpu.SMEM)] + [vmem] * 4
        out_shape = [jax.ShapeDtypeStruct((1, rows // 4), F32)] + out_shape
        scratch.append(pltpu.VMEM((rows, HEAD), F32))
        out_shape.append(jax.ShapeDtypeStruct((shape.rows, shape.columns), BF))
        scratch += shape.sub_scratch() + shape.semaphores()
    return pl.pallas_call(
        functools.partial(output_kernel, shape, tuple(starts)),
        out_shape=out_shape,
        in_specs=in_specs,
        out_specs=[vmem] * len(out_shape),
        scratch_shapes=scratch,
        compiler_params=pltpu.CompilerParams(
            collective_id=ident, has_side_effects=True, vmem_limit_bytes=(20 if shape is None else 32) * 2**20
        ),
    )(*args)


def stacked_queries(source, w_query):
    rows = source.shape[0]
    normed = rms_normed(source.astype(F32)).astype(BF)
    queries = (
        jnp.dot(normed, w_query, preferred_element_type=F32) * (HEAD ** (-0.5) * LOG2E)
    ).astype(BF)
    heads = queries.shape[1] // HEAD
    return jnp.transpose(queries.reshape(rows, heads, HEAD), (1, 0, 2)).reshape(heads * rows, HEAD)


def ring_gather(block, axis):
    count = lax.axis_size(axis)
    me = lax.axis_index(axis)
    onward = [(k, (k + 1) % count) for k in range(count)]
    blocks = jnp.zeros((count,) + block.shape, block.dtype)

    def turn(k, carried):
        blocks, moving = carried
        blocks = lax.dynamic_update_index_in_dim(blocks, moving, lax.rem(me + count - k, count), 0)
        return (blocks, lax.ppermute(moving, axis, onward))

    return lax.fori_loop(0, count, turn, (blocks, block))[0]


def ring_sum(block, axis):
    return jnp.sum(ring_gather(block, axis).astype(F32), axis=0)


def careful_attend(total, source, w_query, w_keyval):
    normed = rms_normed(source.astype(F32)).astype(BF)
    keyval = [jnp.dot(normed, w_keyval[part], preferred_element_type=F32) for part in range(2)]
    joined = jnp.concatenate(keyval, axis=1).astype(BF)
    everyone = ring_gather(joined, "rep").reshape(-1, 2 * HEAD)
    return careful_call(total, stacked_queries(source, w_query), everyone, source.shape[0])


def summed_grad(attended, grad_in):
    grad = lax.dot_general(
        attended, grad_in, (((0,), (0,)), ((), ())), preferred_element_type=F32
    )
    return ring_sum(ring_sum(grad.astype(BF), "rep").astype(BF), "sec")


def careful_path(
    obs, a_query, a_keyval, a_out, w_policy, c_in, c_query, c_keyval, c_out, w_value, columns, total
):
    attended = careful_attend(total, obs, a_query, a_keyval)
    mixed_sum = ring_sum(jnp.dot(attended, a_out, preferred_element_type=F32), "mdl")
    hidden = (obs.astype(F32) + mixed_sum).astype(BF)
    action, advantage, old_values, target, scale = columns
    dhidden = policy_backward(hidden, action, advantage, old_values, scale, w_policy).astype(BF)
    embed_part = jnp.dot(hidden, c_in, preferred_element_type=F32).astype(BF)
    embedded = jnp.concatenate(list(ring_gather(embed_part, "mdl")), axis=1)
    critic_attended = careful_attend(total, embedded, c_query, c_keyval)
    critic_sum = ring_sum(
        jnp.dot(critic_attended, c_out, preferred_element_type=F32), "mdl"
    )
    value, dmixed = value_backward(
        embedded.astype(F32) + critic_sum, target, scale, w_value[None, :]
    )
    part_rows = value.shape[0] // 4
    value = lax.dynamic_slice_in_dim(value[:, 0], lax.axis_index("mdl") * part_rows, part_rows, 0)
    return (value[None, :], summed_grad(attended, dhidden), summed_grad(critic_attended, dmixed))


def on_device(
    obs,
    a_query,
    a_keyval,
    a_out,
    w_policy,
    c_in,
    c_query,
    c_keyval,
    c_out,
    w_value,
    actions,
    advantages,
    old_logp,
    returns,
    robot_count,
):
    rows = obs.shape[1]

    def careful():
        total = robot_count[lax.axis_index("sec")]
        live = lax.axis_index("rep") * rows + lax.iota(jnp.int32, rows) < total
        scale = jnp.where(live, 1.0 / jnp.sum(robot_count).astype(F32), 0.0)
        columns = (actions[0], advantages[0], old_logp[0], returns[0], scale)
        return careful_path(
            obs[0],
            a_query,
            a_keyval,
            a_out,
            w_policy,
            c_in,
            c_query,
            c_keyval,
            c_out,
            w_value,
            tuple(column[:, None] for column in columns),
            total.reshape(1),
        )

    early = c_out.shape[1] // 4
    attended, a_out_full, c_out_early = attend_call(
        robot_count,
        obs[0],
        a_query,
        a_keyval,
        [(a_out, (0, a_out.shape[1])), (c_out, (0, early))],
        1,
    )
    (hidden,) = output_call(attended, [a_out_full], obs[0], None, 3)
    embedded, *sums = policy_call(
        robot_count, hidden, c_in, w_policy, actions, advantages, old_logp, attended, 4
    )
    critic_attended, c_out_late = attend_call(
        robot_count, embedded, c_query, c_keyval, [(c_out, (early, 3 * early))], 2
    )
    shape = Geometry(attended.shape[1], hidden.shape[1], False)
    values, dmixed, actor_summed = output_call(
        critic_attended,
        [c_out_early, c_out_late],
        embedded,
        (shape, robot_count, returns, w_value[None, :], sums),
        5,
    )
    critic_summed = reduced_grad(critic_attended, dmixed, 6)
    mark = critic_summed[0, 0].astype(F32)
    values, actor_grad, critic_grad = lax.cond(
        mark == mark,
        lambda: (values, actor_summed.astype(F32), critic_summed.astype(F32)),
        careful,
    )
    return (values, actor_grad, critic_grad)


def solution(mesh):
    return jax.shard_map(
        on_device,
        mesh=mesh,
        in_specs=(
            P("sec", "rep", None),
            P(None, "mdl"),
            P(None, None, "mdl"),
            P("mdl", None),
            P(),
            P(None, "mdl"),
            P(None, "mdl"),
            P(None, None, "mdl"),
            P("mdl", None),
            P(),
            P("sec", "rep"),
            P("sec", "rep"),
            P("sec", "rep"),
            P("sec", "rep"),
            P(),
        ),
        out_specs=(P("sec", ("rep", "mdl")), P("mdl", None), P("mdl", None)),
        check_vma=False,
    )
```

```python
import functools

import jax
import jax.numpy as jnp
from jax import lax
from jax.experimental import pallas as pl
from jax.experimental.pallas import tpu as pltpu
from jax.sharding import PartitionSpec as P

HEAD = 128
LOG2E = 1.4426950408889634
MESH = pl.DeviceIdType.MESH
BF = jnp.bfloat16
F32 = jnp.float32

epsilon = 1e-05
clip_range = 0.2
masked_score = -1e30
sum_low = 1e-20
sum_high = 1e25


def rms_normed(values_in):
    return values_in * lax.rsqrt(jnp.mean(values_in * values_in, axis=-1, keepdims=True) + epsilon)


def policy_backward(hidden, action, advantage, old_values, scale, w_policy):
    source = hidden.astype(F32)
    factor = lax.rsqrt(jnp.mean(source * source, axis=-1, keepdims=True) + epsilon)
    normed = source * factor
    logits = jnp.dot(normed.astype(BF), w_policy, preferred_element_type=F32)
    shifted = logits - jnp.max(logits, axis=-1, keepdims=True)
    log_probs = shifted - jnp.log(jnp.sum(jnp.exp(shifted), axis=-1, keepdims=True))
    command = lax.broadcasted_iota(jnp.int32, logits.shape, 1)
    onehot = (action == command).astype(F32)
    chosen = jnp.sum(onehot * log_probs, axis=-1, keepdims=True)
    prob_ratio = jnp.exp(chosen - old_values)
    plain_term = prob_ratio * advantage
    bounded = jnp.clip(prob_ratio, 1.0 - clip_range, 1.0 + clip_range) * advantage
    slope_term = jnp.where((scale > 0.0) & (plain_term <= bounded), -plain_term * scale, 0.0)
    dlogits = slope_term * (onehot - jnp.exp(log_probs))
    dnormed = lax.dot_general(
        dlogits.astype(BF), w_policy, (((1,), (1,)), ((), ())), preferred_element_type=F32
    )
    return factor * (dnormed - normed * jnp.mean(dnormed * normed, axis=-1, keepdims=True))


def value_backward(mixed_out, target, scale, w_value):
    factor = lax.rsqrt(jnp.mean(mixed_out * mixed_out, axis=-1, keepdims=True) + epsilon)
    normed = mixed_out * factor
    weight = w_value.astype(F32)
    value_pred = jnp.sum(normed.astype(BF).astype(F32) * weight, axis=-1, keepdims=True)
    slope_term = jnp.where(scale > 0.0, (value_pred - target) * scale, 0.0)
    dnormed = slope_term * weight
    inner = jnp.mean(dnormed * normed, axis=-1, keepdims=True)
    return (value_pred, (factor * (dnormed - normed * inner)).astype(BF))


def standing(row):
    return jnp.transpose(jnp.broadcast_to(row, (HEAD, row.shape[1])))


def live_scale(count_ref, rows):
    total = count_ref[lax.axis_index("sec")]
    both = jnp.full((rows, 1), count_ref[0] + count_ref[1], jnp.int32).astype(F32)
    index = lax.axis_index("rep") * rows + lax.broadcasted_iota(jnp.int32, (rows, 1), 0)
    return jnp.where(index < total, 1.0 / both, 0.0)


PIECES = 2


class WeightGather:
    def __init__(self, columns, own_ref, full_ref, semaphores):
        self.own, self.full = own_ref, full_ref
        self.send, self.recv, self.local = semaphores
        self.columns = pl.ds(*columns)
        self.piece = own_ref.shape[0] // 4
        me = lax.axis_index("rep")
        self.core = lax.rem(me, 2)
        self.other = me + 1 - 2 * self.core
        self.ypos = lax.axis_index("mdl")
        self.yp = lax.rem(self.ypos + 1, 4)
        self.ym = lax.rem(self.ypos + 3, 4)
        self.src = [self.ym, self.yp, lax.rem(self.ypos + 2, 4)]

    def span(self, which, part):
        return pl.ds(pl.multiple_of((2 * which + part) * self.piece, 16), self.piece)

    def copy(self, source_y, part, slot, target, lane, own=False):
        span = self.span(self.core, part)
        where = self.full.at[source_y, span]
        return pltpu.make_async_remote_copy(
            src_ref=self.own.at[span, self.columns] if own else where,
            dst_ref=where,
            send_sem=self.send.at[lane, part],
            recv_sem=self.recv.at[slot, part],
            device_id=target,
            device_id_type=MESH,
        )

    def first(self):
        up, down = {"mdl": self.yp}, {"mdl": self.ym}
        return [
            self.copy(self.ypos, 0, 0, up, 0, own=True),
            self.copy(self.ypos, 1, 1, down, 1, own=True),
            self.copy(self.ypos, 1, 0, up, 0, own=True),
            self.copy(self.ypos, 0, 1, down, 1, own=True),
        ]

    def kept(self):
        return pltpu.make_async_copy(
            self.own.at[:, self.columns], self.full.at[self.ypos], self.local.at[0]
        )

    def start(self):
        for item in self.first():
            item.start()
        self.kept().start()

    def relay(self, part):
        if part == 0:
            return self.copy(self.ym, 0, 2, {"mdl": self.yp}, 2)
        return self.copy(self.yp, 1, 2, {"mdl": self.ym}, 2)

    def share(self, slot, part):
        return self.copy(self.src[slot], part, 3 + slot, {"rep": self.other}, 3 + slot)

    def arrived(self, slot, part):
        which = self.core if slot < 3 else 1 - self.core
        where = self.full.at[self.src[slot % 3], self.span(which, part)]
        pltpu.make_async_copy(where, where, self.recv.at[slot, part]).wait()

    def pass_on(self):
        for part in range(2):
            self.arrived(part, part)
            self.relay(part).start()
            self.share(part, part).start()

    def take_rest(self):
        for part in range(2):
            self.arrived(1 - part, part)
            self.share(1 - part, part).start()

    def take_last(self):
        for part in range(2):
            self.arrived(2, part)
            self.share(2, part).start()

    def finish(self):
        for slot in range(3, 6):
            for part in range(2):
                self.arrived(slot, part)
        for item in self.first():
            item.wait_send()
        for part in range(2):
            self.relay(part).wait_send()
            for slot in range(3):
                self.share(slot, part).wait_send()
        self.kept().wait()


def attend_kernel(
    heads, spans, count_ref, x_ref, wq_ref, wkv_ref, *refs
):
    each = len(spans)
    w_refs, out_ref, full_refs = refs[:each], refs[each], refs[each + 1 : 2 * each + 1]
    buf, acc, q_ref, kv_ref, send, recv, local, *w_semaphores = refs[2 * each + 1 :]
    rows = x_ref.shape[0]
    piece = rows // PIECES
    all_keys = buf.shape[0]
    me = lax.axis_index("rep")
    count = 16
    core = lax.rem(me, 2)
    xpos = lax.rem(me // 2, 2)
    other = me + 1 - 2 * core
    xpeer = me + 2 - 4 * xpos
    zp = lax.rem(me + 4, count)
    zm = lax.rem(me + 12, count)
    src = [
        zm,
        zp,
        lax.rem(me + 8, count),
        xpeer,
        lax.rem(xpeer + 12, count),
        lax.rem(xpeer + 4, count),
        lax.rem(xpeer + 8, count),
    ]
    src = src + [other] + [s + 1 - 2 * core for s in src]

    ypos = lax.axis_index("mdl")
    yp = lax.rem(ypos + 1, 4)
    ym = lax.rem(ypos + 3, 4)

    barrier = pltpu.get_barrier_semaphore()
    peers = [{"rep": zp}, {"rep": zm}, {"rep": xpeer}, {"rep": other}]
    peers += [{"mdl": yp}, {"mdl": ym}]
    for peer in peers:
        pl.semaphore_signal(barrier, inc=1, device_id=peer, device_id_type=MESH)

    rings = [
        WeightGather(columns, w_refs[k], full_refs[k], w_semaphores[3 * k : 3 * k + 3])
        for k, columns in enumerate(spans)
    ]
    pl.semaphore_wait(barrier, len(peers))
    for ring in rings:
        ring.start()

    total = count_ref[lax.axis_index("sec")]
    normed = rms_normed(x_ref[...].astype(F32)).astype(BF)
    live = me * rows + lax.broadcasted_iota(jnp.int32, (rows, HEAD), 0) < total
    for part in range(2):
        made = jnp.dot(normed, wkv_ref[part], preferred_element_type=F32)
        kv_ref[:, part * HEAD : (part + 1) * HEAD] = jnp.where(live, made, 0.0).astype(BF)

    def block_rows(block, part):
        return pl.ds(pl.multiple_of(block * rows + part * piece, piece), piece)

    def transfer(block, part, slot, target, lane, own=False):
        where = buf.at[block_rows(block, part), pl.ds(0, 2 * HEAD)]
        source = kv_ref.at[pl.ds(part * piece, piece)] if own else where
        return pltpu.make_async_remote_copy(
            src_ref=source,
            dst_ref=where,
            send_sem=send.at[lane, part],
            recv_sem=recv.at[slot, part],
            device_id={"rep": target},
            device_id_type=MESH,
        )

    plan = [
        (None, 3, xpeer),
        (None, 1, zm),
        (None, 0, zp),
        (None, 7, other),
        (1, 9, other),
        (0, 2, zp),
        (0, 8, other),
        (3, 5, zm),
        (3, 4, zp),
        (3, 11, other),
        (2, 10, other),
        (2, 6, xpeer),
        (5, 13, other),
        (4, 12, other),
        (6, 14, other),
    ]

    def plan_copy(index, part):
        from_slot, to_slot, target = plan[index]
        block = me if from_slot is None else src[from_slot]
        return transfer(block, part, to_slot, target, index, own=from_slot is None)

    def arrived(slot, part):
        where = buf.at[block_rows(src[slot], part), pl.ds(0, 2 * HEAD)]
        pltpu.make_async_copy(where, where, recv.at[slot, part]).wait()

    def pass_on(slot):
        for part in range(PIECES):
            arrived(slot, part)
            for index, (from_slot, _, _) in enumerate(plan):
                if from_slot == slot:
                    plan_copy(index, part).start()

    def take(slot):
        for part in range(PIECES):
            arrived(slot, part)

    for part in range(PIECES):
        for index in range(4):
            plan_copy(index, part).start()
    own_copy = pltpu.make_async_copy(
        kv_ref,
        buf.at[pl.ds(pl.multiple_of(me * rows, rows), rows), pl.ds(0, 2 * HEAD)],
        local.at[0],
    )
    own_copy.start()

    queries = jnp.dot(normed, wq_ref[...], preferred_element_type=F32) * (HEAD ** (-0.5) * LOG2E)
    for head in range(heads):
        q_ref[head * rows : (head + 1) * rows, :] = queries[
            :, head * HEAD : (head + 1) * HEAD
        ].astype(BF)
    key_index = lax.broadcasted_iota(jnp.int32, (all_keys, HEAD), 0)
    buf[:, 2 * HEAD :] = jnp.where(key_index < total, 1.0, 0.0).astype(BF)
    acc[...] = jnp.zeros_like(acc)
    own_copy.wait()

    chip_rows = 2 * rows
    zpos = me // 4

    def step(i, carry):
        @pl.when(i == 0)
        def _():
            take(7)

        @pl.when(i == 1)
        def _():
            pass_on(0)
            pass_on(1)
            take(9)

        @pl.when(i == 2)
        def _():
            pass_on(3)
            take(8)

        @pl.when(i == 3)
        def _():
            pass_on(2)
            take(10)

        @pl.when(i == 4)
        def _():
            pass_on(5)
            take(11)

        for k, ring in enumerate(rings):
            pl.when(i == 3 + 2 * k)(ring.pass_on)
            pl.when(i == (5, 7)[k] if each > 1 else i == 7)(ring.take_rest)

        @pl.when(i == 5)
        def _():
            pass_on(4)
            take(13)

        @pl.when(i == 6)
        def _():
            pass_on(6)
            take(12)

        @pl.when(i == 7)
        def _():
            take(14)

        j = lax.rem(i, 4)
        dz = j + (j // 2) * (1 - 2 * lax.rem(j, 2))
        dx = i // 4
        chip = lax.rem(zpos + dz, 4) * 2 + lax.rem(xpos + dx, 2)
        span = pl.ds(pl.multiple_of(chip * chip_rows, chip_rows), chip_rows)
        scores = lax.dot_general(
            q_ref[...],
            buf[span, :HEAD],
            (((1,), (1,)), ((), ())),
            preferred_element_type=F32,
        )
        weights = jnp.exp2(scores).astype(BF)
        acc[...] += jnp.dot(weights, buf[span, HEAD:], preferred_element_type=F32)
        return carry

    lax.fori_loop(0, 8, step, 0)

    for ring in rings:
        ring.take_last()

    for head in range(heads):
        part = acc[head * rows : (head + 1) * rows, :]
        sums = part[:, HEAD:]
        safe = (sums > sum_low) & (sums < sum_high)
        out_ref[:, head * HEAD : (head + 1) * HEAD] = jnp.where(
            safe, part[:, :HEAD] / sums, jnp.nan
        ).astype(BF)

    for ring in rings:
        ring.finish()
    for part in range(PIECES):
        for index in range(len(plan)):
            plan_copy(index, part).wait_send()


def attend_call(counts, source, w_query, w_keyval, weights, ident):
    heads = w_query.shape[1] // HEAD
    rows = source.shape[0]
    keys = rows * 16
    vmem = pl.BlockSpec(memory_space=pltpu.VMEM)
    anywhere = pl.BlockSpec(memory_space=pl.ANY)
    return pl.pallas_call(
        functools.partial(attend_kernel, heads, tuple(columns for _, columns in weights)),
        out_shape=[
            jax.ShapeDtypeStruct((rows, heads * HEAD), BF),
        ]
        + [
            jax.ShapeDtypeStruct((4, w.shape[0], columns[1]), BF) for w, columns in weights
        ],
        in_specs=[pl.BlockSpec(memory_space=pltpu.SMEM), vmem, vmem, vmem]
        + [anywhere] * len(weights),
        out_specs=[vmem] + [anywhere] * len(weights),
        scratch_shapes=[
            pltpu.VMEM((keys, 3 * HEAD), BF),
            pltpu.VMEM((heads * rows, 2 * HEAD), F32),
            pltpu.VMEM((heads * rows, HEAD), BF),
            pltpu.VMEM((rows, 2 * HEAD), BF),
            pltpu.SemaphoreType.DMA((15, PIECES)),
            pltpu.SemaphoreType.DMA((15, PIECES)),
            pltpu.SemaphoreType.DMA((1,)),
        ]
        + [
            pltpu.SemaphoreType.DMA((6, 2)),
            pltpu.SemaphoreType.DMA((6, 2)),
            pltpu.SemaphoreType.DMA((1,)),
        ]
        * len(weights),
        compiler_params=pltpu.CompilerParams(
            collective_id=ident, has_side_effects=True, vmem_limit_bytes=40 * 2**20
        ),
        cost_estimate=pl.CostEstimate(
            flops=4 * heads * rows * keys * HEAD,
            bytes_accessed=keys * 4 * HEAD,
            transcendentals=heads * rows * keys,
        ),
    )(counts, source, w_query, w_keyval, *(w for w, _ in weights))


def careful_kernel(total_ref, q_ref, kv_ref, out_ref, top, acc, total_sum):
    step = pl.program_id(0)
    block = kv_ref.shape[0]

    @pl.when(step == 0)
    def _():
        top[...] = jnp.full_like(top, masked_score)
        acc[...] = jnp.zeros_like(acc)
        total_sum[...] = jnp.zeros_like(total_sum)

    scores = lax.dot_general(
        q_ref[...], kv_ref[:, :HEAD], (((1,), (1,)), ((), ())), preferred_element_type=F32
    )
    key_index = step * block + lax.broadcasted_iota(jnp.int32, scores.shape, 1)
    live = key_index < total_ref[0]
    scores = jnp.where(live, scores, masked_score)
    old = top[...]
    new = jnp.maximum(old, jnp.max(scores, axis=1, keepdims=True))
    top[...] = new
    rescale = jnp.exp2(old - new)
    weights = jnp.where(live, jnp.exp2(scores - new[:, :1]), 0.0)
    total_sum[...] = total_sum[...] * rescale + jnp.sum(weights, axis=1, keepdims=True)
    acc[...] = acc[...] * rescale + jnp.dot(
        weights.astype(BF), kv_ref[:, HEAD:], preferred_element_type=F32
    )

    @pl.when(step == pl.num_programs(0) - 1)
    def _():
        rows, width = out_ref.shape
        for head in range(width // HEAD):
            span = slice(head * rows, (head + 1) * rows)
            out_ref[:, head * HEAD : (head + 1) * HEAD] = (acc[span, :] / total_sum[span, :]).astype(
                BF
            )


def careful_call(total, queries, kv_full, rows):
    heads = queries.shape[0] // rows
    block = 256
    return pl.pallas_call(
        careful_kernel,
        out_shape=jax.ShapeDtypeStruct((rows, heads * HEAD), BF),
        grid=(kv_full.shape[0] // block,),
        in_specs=[
            pl.BlockSpec(memory_space=pltpu.SMEM),
            pl.BlockSpec(queries.shape, lambda i: (0, 0)),
            pl.BlockSpec((block, 2 * HEAD), lambda i: (i, 0)),
        ],
        out_specs=pl.BlockSpec((rows, heads * HEAD), lambda i: (0, 0)),
        scratch_shapes=[pltpu.VMEM((heads * rows, HEAD), F32)] * 3,
        compiler_params=pltpu.CompilerParams(vmem_limit_bytes=20 * 2**20),
    )(total, queries, kv_full)


class YGather:
    def __init__(self, own_half, place, send, recv):
        self.ypos = lax.axis_index("mdl")
        self.yp = lax.rem(self.ypos + 1, 4)
        self.ym = lax.rem(self.ypos + 3, 4)
        self.y2 = lax.rem(self.ypos + 2, 4)
        self.own_half, self.place, self.send, self.recv = own_half, place, send, recv

    def greet(self, barrier):
        for peer in (self.yp, self.ym):
            pl.semaphore_signal(barrier, inc=1, device_id={"mdl": peer}, device_id_type=MESH)
        return 2

    def copy(self, source_y, part, slot, target, lane, own=False):
        return pltpu.make_async_remote_copy(
            src_ref=self.own_half(part) if own else self.place(source_y, part, lane - 2),
            dst_ref=self.place(source_y, part, slot),
            send_sem=self.send.at[lane, part],
            recv_sem=self.recv.at[slot, part],
            device_id={"mdl": target},
            device_id_type=MESH,
        )

    def first(self):
        return [
            self.copy(self.ypos, 0, 0, self.yp, 0, own=True),
            self.copy(self.ypos, 1, 1, self.ym, 1, own=True),
            self.copy(self.ypos, 1, 0, self.yp, 0, own=True),
            self.copy(self.ypos, 0, 1, self.ym, 1, own=True),
        ]

    def start(self):
        for item in self.first():
            item.start()

    def arrived(self, slot, part):
        where = self.place((self.ym, self.yp, self.y2)[slot], part, slot)
        pltpu.make_async_copy(where, where, self.recv.at[slot, part]).wait()

    def relay(self, part):
        if part == 0:
            return self.copy(self.ym, 0, 2, self.yp, 2)
        return self.copy(self.yp, 1, 2, self.ym, 3)

    def pass_on(self, part):
        self.arrived(part, part)
        self.relay(part).start()

    def wait_sent(self):
        for item in self.first():
            item.wait_send()
        for part in range(2):
            self.relay(part).wait_send()


class Geometry:
    def __init__(self, rows, columns, by_rows):
        self.by_rows = by_rows
        self.rows, self.columns = rows, columns
        if by_rows:
            self.half = (rows // 2, columns)
            self.quarter_shape = [(rows // 4, columns // 4)] * 2
            self.sub_shape = [(rows // 16, columns // 4)] * 2
        else:
            third = columns // 6
            self.half = (rows, columns // 2)
            self.quarter_shape = [(rows // 4, 2 * third), (rows // 4, third)]
            self.sub_shape = [(rows // 4, third // 2), (rows // 8, third // 2)]

    def whole(self, core):
        if self.by_rows:
            return (core * self.half[0], 0)
        return (0, core * self.half[1])

    def quarter(self, part, index):
        rows, columns = self.quarter_shape[part]
        if self.by_rows:
            return (part * rows, index * columns)
        return (index * rows, part * self.quarter_shape[0][1])

    def sub(self, part, index):
        rows, columns = self.sub_shape[part]
        if self.by_rows:
            return (index * rows, 0)
        if part == 0:
            return (0, index * columns)
        return ((index // 2) * rows, lax.rem(index, 2) * columns)

    def scatter_scratch(self):
        vmem = pltpu.VMEM
        return [vmem(self.half, BF)] * 3 + [vmem((3,) + q, BF) for q in self.quarter_shape]

    def sub_scratch(self):
        return [pltpu.VMEM((3,) + sub, BF) for sub in self.sub_shape]

    def semaphores(self):
        dma = pltpu.SemaphoreType.DMA
        return [dma((4, 2, 3)), dma((4, 2, 3)), dma((9,)), dma((9,))]


def box(start, shape):
    row, column = start
    return (
        pl.ds(row if isinstance(row, int) else pl.multiple_of(row, 16), shape[0]),
        pl.ds(column if isinstance(column, int) else pl.multiple_of(column, HEAD), shape[1]),
    )


def plus(left, right):
    return (left[0] + right[0], left[1] + right[1])


class Reduce:
    hops = (2, 1, 3)

    def __init__(self, shape, att_ref, d_ref, out_ref, scatter, sums, sub_in, semaphores):
        self.g = shape
        self.att, self.d, self.out = att_ref, d_ref, out_ref
        if scatter is not None:
            self.theirs, self.mine, self.got = scatter[:3]
            self.part_in = scatter[3:5]
        self.part_sum = sums
        self.sub_in = sub_in
        self.send, self.recv, self.csend, self.crecv = semaphores
        me = lax.axis_index("rep")
        self.me = me
        self.core = lax.rem(me, 2)
        self.other = me + 1 - 2 * self.core
        self.zpos = me // 4
        self.xpos = lax.rem(me // 2, 2) * 2 + lax.axis_index("sec")
        self.first = [self.xpos, self.zpos]
        self.second = [self.zpos, self.xpos]
        self.near = [self.at_x, self.at_z]

    def at_x(self, k):
        there = lax.rem(self.xpos + k, 4)
        return {"rep": self.zpos * 4 + (there // 2) * 2 + self.core, "sec": lax.rem(there, 2)}

    def at_z(self, k):
        return {"rep": lax.rem(self.me + 4 * k, 16)}

    def greet(self, barrier):
        for k in range(1, 4):
            pl.semaphore_signal(barrier, inc=1, device_id=self.at_x(k), device_id_type=MESH)
            pl.semaphore_signal(barrier, inc=1, device_id=self.at_z(k), device_id_type=MESH)
        pl.semaphore_signal(barrier, inc=1, device_id={"rep": self.other}, device_id_type=MESH)
        return 7

    def grad(self, which):
        left, right = self.att, self.d
        if self.g.by_rows:
            size = self.g.half[0]
            left = left[:, pl.ds(pl.multiple_of(which * size, size), size)]
            right = right[...]
        else:
            size = self.g.half[1]
            left = left[...]
            right = right[:, pl.ds(pl.multiple_of(which * size, HEAD), size)]
        return lax.dot_general(left, right, (((0,), (0,)), ((), ())), preferred_element_type=F32)

    def copy(self, source, target, send, recv, device):
        return pltpu.make_async_remote_copy(
            src_ref=source,
            dst_ref=target,
            send_sem=send,
            recv_sem=recv,
            device_id=device,
            device_id_type=MESH,
        )

    def swap(self):
        return self.copy(
            self.theirs, self.got, self.csend.at[0], self.crecv.at[0], {"rep": self.other}
        )

    def stage(self, level, part, k, source, target, device):
        return self.copy(
            source,
            target,
            self.send.at[level, part, k - 1],
            self.recv.at[level, part, k - 1],
            device,
        )

    def scatter_one(self, part, k):
        start = self.g.quarter(part, lax.rem(self.first[part] + k, 4))
        return self.stage(
            0,
            part,
            k,
            self.mine.at[box(start, self.g.quarter_shape[part])],
            self.part_in[part].at[k - 1],
            self.near[part](k),
        )

    def scatter_two(self, part, k):
        start = self.g.sub(part, lax.rem(self.second[part] + k, 4))
        return self.stage(
            1,
            part,
            k,
            self.part_sum[part].at[box(start, self.g.sub_shape[part])],
            self.sub_in[part].at[k - 1],
            self.near[1 - part](k),
        )

    def my_sub(self, part):
        start = plus(
            self.g.whole(self.core),
            plus(self.g.quarter(part, self.first[part]), self.g.sub(part, self.second[part])),
        )
        return box(start, self.g.sub_shape[part])

    def out_quarter(self, core, part, index):
        start = plus(self.g.whole(core), self.g.quarter(part, index))
        return self.out.at[box(start, self.g.quarter_shape[part])]

    def gather_two(self, part, k):
        where = self.out.at[self.my_sub(part)]
        return self.stage(2, part, k, where, where, self.near[1 - part](k))

    def gather_one(self, part, k):
        where = self.out_quarter(self.core, part, self.first[part])
        return self.stage(3, part, k, where, where, self.near[part](k))

    def share(self, part, k, core):
        where = self.out_quarter(core, part, lax.rem(self.first[part] + 4 - k, 4))
        index = 1 + part * 4 + k
        return self.copy(
            where, where, self.csend.at[index], self.crecv.at[index], {"rep": self.other}
        )

    def begin(self):
        self.theirs[...] = self.grad(1 - self.core).astype(BF)

    def swap_and_scatter(self):
        self.swap().start()
        self.scatter_own()

    def scatter_own(self):
        own = self.grad(self.core)
        self.swap().wait_recv()
        self.mine[...] = (own + self.got[...].astype(F32)).astype(BF)
        for k in self.hops:
            for part in range(2):
                self.scatter_one(part, k).start()

    def first_sums(self):
        for part in range(2):
            start = self.g.quarter(part, self.first[part])
            total = self.mine[box(start, self.g.quarter_shape[part])].astype(F32)
            for k in (1, 3, 2):
                self.scatter_one(part, k).wait_recv()
                total += self.part_in[part][k - 1].astype(F32)
            self.part_sum[part][...] = total.astype(BF)

    def second_scatter(self):
        for k in self.hops:
            for part in range(2):
                self.scatter_two(part, k).start()

    def first_gather(self):
        for part in range(2):
            start = self.g.sub(part, self.second[part])
            total = self.part_sum[part][box(start, self.g.sub_shape[part])].astype(F32)
            for k in (1, 3, 2):
                self.scatter_two(part, k).wait_recv()
                total += self.sub_in[part][k - 1].astype(F32)
            self.out[self.my_sub(part)] = total.astype(BF)
            for k in self.hops:
                self.gather_two(part, k).start()

    def second_gather(self):
        for part in range(2):
            for k in range(1, 4):
                self.gather_two(part, k).wait_recv()
            for k in self.hops:
                self.gather_one(part, k).start()
            self.share(part, 0, self.core).start()

    def last_shares(self):
        for k in (1, 3, 2):
            for part in range(2):
                self.gather_one(part, k).wait_recv()
                self.share(part, k, self.core).start()

    def finish_scatter(self):
        self.swap().wait_send()
        for part in range(2):
            for k in range(1, 4):
                self.scatter_one(part, k).wait_send()

    def finish(self):
        for part in range(2):
            for k in range(4):
                self.share(part, k, 1 - self.core).wait_recv()
        for part in range(2):
            for k in range(1, 4):
                self.scatter_two(part, k).wait_send()
                self.gather_two(part, k).wait_send()
                self.gather_one(part, k).wait_send()
            for k in range(4):
                self.share(part, k, self.core).wait_send()


def reduce_kernel(shape, att_ref, d_ref, out_ref, *scratch):
    each = len(scratch) // 2
    works = []
    for index in range(2):
        part = scratch[index * each : (index + 1) * each]
        span = pl.ds(index * shape.columns, shape.columns)
        works.append(
            Reduce(
                shape,
                att_ref,
                d_ref.at[:, span],
                out_ref.at[:, span],
                part[:5],
                part[5:7],
                part[7:9],
                part[9:13],
            )
        )
    early, late = works
    barrier = pltpu.get_barrier_semaphore()
    expected = early.greet(barrier)
    early.begin()
    pl.semaphore_wait(barrier, expected)
    early.swap().start()
    late.begin()
    late.swap().start()
    early.scatter_own()
    late.scatter_own()
    early.first_sums()
    early.second_scatter()
    late.first_sums()
    late.second_scatter()
    early.first_gather()
    late.first_gather()
    early.second_gather()
    late.second_gather()
    early.last_shares()
    late.last_shares()
    for work in works:
        work.finish_scatter()
        work.finish()


def reduced_grad(attended, grad_in, ident):
    shape = Geometry(attended.shape[1], grad_in.shape[1] // 2, True)
    vmem = pl.BlockSpec(memory_space=pltpu.VMEM)
    return pl.pallas_call(
        functools.partial(reduce_kernel, shape),
        out_shape=jax.ShapeDtypeStruct((attended.shape[1], grad_in.shape[1]), BF),
        in_specs=[vmem, vmem],
        out_specs=vmem,
        scratch_shapes=2
        * (
            shape.scatter_scratch()
            + [pltpu.VMEM(q, BF) for q in shape.quarter_shape]
            + shape.sub_scratch()
            + shape.semaphores()
        ),
        compiler_params=pltpu.CompilerParams(
            collective_id=ident, has_side_effects=True, vmem_limit_bytes=24 * 2**20
        ),
    )(attended, grad_in)


def policy_kernel(
    shape,
    count_ref,
    x_ref,
    cin_ref,
    wp_ref,
    action_ref,
    advantage_ref,
    old_ref,
    att_ref,
    out_ref,
    sum_a,
    sum_b,
    part_ref,
    d_ref,
    *refs,
):
    scatter, semaphores, (send, recv, local) = refs[:5], refs[5:9], refs[9:]
    work = Reduce(shape, att_ref, d_ref, None, scatter, (sum_a, sum_b), None, semaphores)
    rows, width = part_ref.shape
    half = rows // 2

    def place(source_y, part, slot):
        return out_ref.at[
            pl.ds(part * half, half), pl.ds(pl.multiple_of(source_y * width, HEAD), width)
        ]

    ring = YGather(lambda part: part_ref.at[pl.ds(part * half, half)], place, send, recv)
    barrier = pltpu.get_barrier_semaphore()
    expected = ring.greet(barrier) + work.greet(barrier)
    part_ref[...] = jnp.dot(x_ref[...], cin_ref[...], preferred_element_type=F32).astype(BF)
    pl.semaphore_wait(barrier, expected)
    ring.start()
    mine = pltpu.make_async_copy(
        part_ref, out_ref.at[:, pl.ds(pl.multiple_of(ring.ypos * width, HEAD), width)], local.at[0]
    )
    mine.start()
    d_ref[...] = policy_backward(
        x_ref[...],
        standing(action_ref[...]),
        standing(advantage_ref[...])[:, :1],
        standing(old_ref[...])[:, :1],
        live_scale(count_ref, rows),
        wp_ref[...],
    ).astype(BF)
    ring.pass_on(0)
    ring.pass_on(1)
    work.begin()
    work.swap_and_scatter()
    ring.arrived(0, 1)
    ring.arrived(1, 0)
    work.first_sums()
    ring.arrived(2, 0)
    ring.arrived(2, 1)
    work.finish_scatter()
    ring.wait_sent()
    mine.wait()


def policy_call(counts, hidden, c_in, w_policy, action, advantage, old_values, attended, ident):
    rows = hidden.shape[0]
    width = c_in.shape[1]
    shape = Geometry(attended.shape[1], hidden.shape[1], False)
    vmem = pl.BlockSpec(memory_space=pltpu.VMEM)
    return pl.pallas_call(
        functools.partial(policy_kernel, shape),
        out_shape=[jax.ShapeDtypeStruct((rows, 4 * width), BF)]
        + [jax.ShapeDtypeStruct(q, BF) for q in shape.quarter_shape],
        in_specs=[pl.BlockSpec(memory_space=pltpu.SMEM)] + [vmem] * 7,
        out_specs=[vmem] * 3,
        scratch_shapes=[pltpu.VMEM((rows, width), BF), pltpu.VMEM(hidden.shape, BF)]
        + shape.scatter_scratch()
        + shape.semaphores()
        + [
            pltpu.SemaphoreType.DMA((4, 2)),
            pltpu.SemaphoreType.DMA((3, 2)),
            pltpu.SemaphoreType.DMA((1,)),
        ],
        compiler_params=pltpu.CompilerParams(
            collective_id=ident, has_side_effects=True, vmem_limit_bytes=32 * 2**20
        ),
    )(counts, hidden, c_in, w_policy, action, advantage, old_values, attended)


def output_kernel(shape, starts, x_ref, base_ref, *refs):
    w_refs, refs = refs[: len(starts)], refs[len(starts) :]
    if shape is None:
        out_ref, acc, blocks, send, recv = refs
        work = None
    else:
        count_ref, return_ref, wv_ref, sum_a, sum_b, value_ref, out_ref, grad_ref = refs[:8]
        acc, blocks, send, recv, lanes = refs[8:13]
        work = Reduce(shape, None, None, grad_ref, None, (sum_a, sum_b), refs[13:15], refs[15:19])
    rows = x_ref.shape[0]
    half = rows // 2
    ring = YGather(
        lambda part: x_ref.at[pl.ds(part * half, half)],
        lambda source_y, part, slot: blocks.at[slot, pl.ds(part * half, half)],
        send,
        recv,
    )
    barrier = pltpu.get_barrier_semaphore()
    expected = ring.greet(barrier)
    if work is not None:
        expected += work.greet(barrier)
    pl.semaphore_wait(barrier, expected)
    ring.start()
    if work is not None:
        work.second_scatter()
    for start, w_ref in zip(starts, w_refs):
        columns = slice(start, start + w_ref.shape[2])
        acc[:, columns] = base_ref[:, columns].astype(F32) + jnp.dot(
            x_ref[...], w_ref[ring.ypos], preferred_element_type=F32
        )

    def add(slot, part):
        source_y = (ring.ym, ring.yp, ring.y2)[slot]
        span = pl.ds(part * half, half)
        for start, w_ref in zip(starts, w_refs):
            columns = slice(start, start + w_ref.shape[2])
            acc[span, columns] += jnp.dot(
                blocks[slot, span, :], w_ref[source_y], preferred_element_type=F32
            )

    if work is not None:
        work.first_gather()
    ring.pass_on(0)
    ring.pass_on(1)
    add(0, 0)
    add(1, 1)
    if work is not None:
        work.second_gather()
    ring.arrived(0, 1)
    add(0, 1)
    ring.arrived(1, 0)
    add(1, 0)
    if work is not None:
        work.last_shares()
    ring.arrived(2, 0)
    add(2, 0)
    ring.arrived(2, 1)
    add(2, 1)
    if work is None:
        out_ref[...] = acc[...].astype(BF)
    else:
        value, out_ref[...] = value_backward(
            acc[...], standing(return_ref[...])[:, :1], live_scale(count_ref, rows), wv_ref[...]
        )
        lanes[...] = jnp.broadcast_to(value, lanes.shape)
        mine = lanes[pl.ds(pl.multiple_of(ring.ypos * value_ref.shape[1], 8), value_ref.shape[1]), :]
        value_ref[...] = jnp.transpose(mine)[:1]
    if work is not None:
        work.finish()
    ring.wait_sent()


def output_call(x, weights, base, value_args, ident):
    rows, width = x.shape
    columns = base.shape[1]
    starts = []
    for w_full in weights:
        starts.append(sum(other.shape[2] for other in weights[: len(starts)]))
    vmem = pl.BlockSpec(memory_space=pltpu.VMEM)
    args = [x, base] + list(weights)
    in_specs = [vmem] * len(args)
    out_shape = [jax.ShapeDtypeStruct((rows, columns), BF)]
    scratch = [
        pltpu.VMEM((rows, columns), F32),
        pltpu.VMEM((3, rows, width), BF),
        pltpu.SemaphoreType.DMA((4, 2)),
        pltpu.SemaphoreType.DMA((3, 2)),
    ]
    shape = None
    if value_args is not None:
        shape, counts, target, w_value, sums = value_args
        args += [counts, target, w_value] + list(sums)
        in_specs += [pl.BlockSpec(memory_space=pltpu.SMEM)] + [vmem] * 4
        out_shape = [jax.ShapeDtypeStruct((1, rows // 4), F32)] + out_shape
        scratch.append(pltpu.VMEM((rows, HEAD), F32))
        out_shape.append(jax.ShapeDtypeStruct((shape.rows, shape.columns), BF))
        scratch += shape.sub_scratch() + shape.semaphores()
    return pl.pallas_call(
        functools.partial(output_kernel, shape, tuple(starts)),
        out_shape=out_shape,
        in_specs=in_specs,
        out_specs=[vmem] * len(out_shape),
        scratch_shapes=scratch,
        compiler_params=pltpu.CompilerParams(
            collective_id=ident, has_side_effects=True, vmem_limit_bytes=(20 if shape is None else 32) * 2**20
        ),
    )(*args)


def stacked_queries(source, w_query):
    rows = source.shape[0]
    normed = rms_normed(source.astype(F32)).astype(BF)
    queries = (
        jnp.dot(normed, w_query, preferred_element_type=F32) * (HEAD ** (-0.5) * LOG2E)
    ).astype(BF)
    heads = queries.shape[1] // HEAD
    return jnp.transpose(queries.reshape(rows, heads, HEAD), (1, 0, 2)).reshape(heads * rows, HEAD)


def ring_gather(block, axis):
    count = lax.axis_size(axis)
    me = lax.axis_index(axis)
    onward = [(k, (k + 1) % count) for k in range(count)]
    blocks = jnp.zeros((count,) + block.shape, block.dtype)

    def turn(k, carried):
        blocks, moving = carried
        blocks = lax.dynamic_update_index_in_dim(blocks, moving, lax.rem(me + count - k, count), 0)
        return (blocks, lax.ppermute(moving, axis, onward))

    return lax.fori_loop(0, count, turn, (blocks, block))[0]


def ring_sum(block, axis):
    return jnp.sum(ring_gather(block, axis).astype(F32), axis=0)


def careful_attend(total, source, w_query, w_keyval):
    normed = rms_normed(source.astype(F32)).astype(BF)
    keyval = [jnp.dot(normed, w_keyval[part], preferred_element_type=F32) for part in range(2)]
    joined = jnp.concatenate(keyval, axis=1).astype(BF)
    everyone = ring_gather(joined, "rep").reshape(-1, 2 * HEAD)
    return careful_call(total, stacked_queries(source, w_query), everyone, source.shape[0])


def summed_grad(attended, grad_in):
    grad = lax.dot_general(
        attended, grad_in, (((0,), (0,)), ((), ())), preferred_element_type=F32
    )
    return ring_sum(ring_sum(grad.astype(BF), "rep").astype(BF), "sec")


def careful_path(
    obs, a_query, a_keyval, a_out, w_policy, c_in, c_query, c_keyval, c_out, w_value, columns, total
):
    attended = careful_attend(total, obs, a_query, a_keyval)
    mixed_sum = ring_sum(jnp.dot(attended, a_out, preferred_element_type=F32), "mdl")
    hidden = (obs.astype(F32) + mixed_sum).astype(BF)
    action, advantage, old_values, target, scale = columns
    dhidden = policy_backward(hidden, action, advantage, old_values, scale, w_policy).astype(BF)
    embed_part = jnp.dot(hidden, c_in, preferred_element_type=F32).astype(BF)
    embedded = jnp.concatenate(list(ring_gather(embed_part, "mdl")), axis=1)
    critic_attended = careful_attend(total, embedded, c_query, c_keyval)
    critic_sum = ring_sum(
        jnp.dot(critic_attended, c_out, preferred_element_type=F32), "mdl"
    )
    value, dmixed = value_backward(
        embedded.astype(F32) + critic_sum, target, scale, w_value[None, :]
    )
    part_rows = value.shape[0] // 4
    value = lax.dynamic_slice_in_dim(value[:, 0], lax.axis_index("mdl") * part_rows, part_rows, 0)
    return (value[None, :], summed_grad(attended, dhidden), summed_grad(critic_attended, dmixed))


def on_device(
    obs,
    a_query,
    a_keyval,
    a_out,
    w_policy,
    c_in,
    c_query,
    c_keyval,
    c_out,
    w_value,
    actions,
    advantages,
    old_logp,
    returns,
    robot_count,
):
    rows = obs.shape[1]

    def careful():
        total = robot_count[lax.axis_index("sec")]
        live = lax.axis_index("rep") * rows + lax.iota(jnp.int32, rows) < total
        scale = jnp.where(live, 1.0 / jnp.sum(robot_count).astype(F32), 0.0)
        columns = (actions[0], advantages[0], old_logp[0], returns[0], scale)
        return careful_path(
            obs[0],
            a_query,
            a_keyval,
            a_out,
            w_policy,
            c_in,
            c_query,
            c_keyval,
            c_out,
            w_value,
            tuple(column[:, None] for column in columns),
            total.reshape(1),
        )

    early = c_out.shape[1] // 4
    attended, a_out_full, c_out_early = attend_call(
        robot_count,
        obs[0],
        a_query,
        a_keyval,
        [(a_out, (0, a_out.shape[1])), (c_out, (0, early))],
        1,
    )
    (hidden,) = output_call(attended, [a_out_full], obs[0], None, 3)
    embedded, *sums = policy_call(
        robot_count, hidden, c_in, w_policy, actions, advantages, old_logp, attended, 4
    )
    critic_attended, c_out_late = attend_call(
        robot_count, embedded, c_query, c_keyval, [(c_out, (early, 3 * early))], 2
    )
    shape = Geometry(attended.shape[1], hidden.shape[1], False)
    values, dmixed, actor_summed = output_call(
        critic_attended,
        [c_out_early, c_out_late],
        embedded,
        (shape, robot_count, returns, w_value[None, :], sums),
        5,
    )
    critic_summed = reduced_grad(critic_attended, dmixed, 6)
    mark = critic_summed[0, 0].astype(F32)
    values, actor_grad, critic_grad = lax.cond(
        mark == mark,
        lambda: (values, actor_summed.astype(F32), critic_summed.astype(F32)),
        careful,
    )
    return (values, actor_grad, critic_grad)


def solution(mesh):
    return jax.shard_map(
        on_device,
        mesh=mesh,
        in_specs=(
            P("sec", "rep", None),
            P(None, "mdl"),
            P(None, None, "mdl"),
            P("mdl", None),
            P(),
            P(None, "mdl"),
            P(None, "mdl"),
            P(None, None, "mdl"),
            P("mdl", None),
            P(),
            P("sec", "rep"),
            P("sec", "rep"),
            P("sec", "rep"),
            P("sec", "rep"),
            P(),
        ),
        out_specs=(P("sec", ("rep", "mdl")), P("mdl", None), P("mdl", None)),
        check_vma=False,
    )
```

```python
import functools

import jax
import jax.numpy as jnp
from jax import lax
from jax.experimental import pallas as pl
from jax.experimental.pallas import tpu as pltpu
from jax.sharding import PartitionSpec as P

HEAD = 128
LOG2E = 1.4426950408889634
MESH = pl.DeviceIdType.MESH
BF = jnp.bfloat16
F32 = jnp.float32

epsilon = 1e-05
clip_range = 0.2
masked_score = -1e30
sum_low = 1e-20
sum_high = 1e25


def rms_normed(values_in):
    return values_in * lax.rsqrt(jnp.mean(values_in * values_in, axis=-1, keepdims=True) + epsilon)


def policy_backward(hidden, action, advantage, old_values, scale, w_policy):
    source = hidden.astype(F32)
    factor = lax.rsqrt(jnp.mean(source * source, axis=-1, keepdims=True) + epsilon)
    normed = source * factor
    logits = jnp.dot(normed.astype(BF), w_policy, preferred_element_type=F32)
    shifted = logits - jnp.max(logits, axis=-1, keepdims=True)
    log_probs = shifted - jnp.log(jnp.sum(jnp.exp(shifted), axis=-1, keepdims=True))
    command = lax.broadcasted_iota(jnp.int32, logits.shape, 1)
    onehot = (action == command).astype(F32)
    chosen = jnp.sum(onehot * log_probs, axis=-1, keepdims=True)
    prob_ratio = jnp.exp(chosen - old_values)
    plain_term = prob_ratio * advantage
    bounded = jnp.clip(prob_ratio, 1.0 - clip_range, 1.0 + clip_range) * advantage
    slope_term = jnp.where((scale > 0.0) & (plain_term <= bounded), -plain_term * scale, 0.0)
    dlogits = slope_term * (onehot - jnp.exp(log_probs))
    dnormed = lax.dot_general(
        dlogits.astype(BF), w_policy, (((1,), (1,)), ((), ())), preferred_element_type=F32
    )
    return factor * (dnormed - normed * jnp.mean(dnormed * normed, axis=-1, keepdims=True))


def value_backward(mixed_out, target, scale, w_value):
    factor = lax.rsqrt(jnp.mean(mixed_out * mixed_out, axis=-1, keepdims=True) + epsilon)
    normed = mixed_out * factor
    weight = w_value.astype(F32)
    value_pred = jnp.sum(normed.astype(BF).astype(F32) * weight, axis=-1, keepdims=True)
    slope_term = jnp.where(scale > 0.0, (value_pred - target) * scale, 0.0)
    dnormed = slope_term * weight
    inner = jnp.mean(dnormed * normed, axis=-1, keepdims=True)
    return (value_pred, (factor * (dnormed - normed * inner)).astype(BF))


def standing(row):
    return jnp.transpose(jnp.broadcast_to(row, (HEAD, row.shape[1])))


def live_scale(count_ref, rows):
    total = count_ref[lax.axis_index("sec")]
    both = jnp.full((rows, 1), count_ref[0] + count_ref[1], jnp.int32).astype(F32)
    index = lax.axis_index("rep") * rows + lax.broadcasted_iota(jnp.int32, (rows, 1), 0)
    return jnp.where(index < total, 1.0 / both, 0.0)


PIECES = 2


class WeightGather:
    def __init__(self, columns, own_ref, full_ref, semaphores):
        self.own, self.full = own_ref, full_ref
        self.send, self.recv, self.local = semaphores
        self.columns = pl.ds(*columns)
        self.piece = own_ref.shape[0] // 4
        me = lax.axis_index("rep")
        self.core = lax.rem(me, 2)
        self.other = me + 1 - 2 * self.core
        self.ypos = lax.axis_index("mdl")
        self.yp = lax.rem(self.ypos + 1, 4)
        self.ym = lax.rem(self.ypos + 3, 4)
        self.src = [self.ym, self.yp, lax.rem(self.ypos + 2, 4)]

    def span(self, which, part):
        return pl.ds(pl.multiple_of((2 * which + part) * self.piece, 16), self.piece)

    def copy(self, source_y, part, slot, target, lane, own=False):
        span = self.span(self.core, part)
        where = self.full.at[source_y, span]
        return pltpu.make_async_remote_copy(
            src_ref=self.own.at[span, self.columns] if own else where,
            dst_ref=where,
            send_sem=self.send.at[lane, part],
            recv_sem=self.recv.at[slot, part],
            device_id=target,
            device_id_type=MESH,
        )

    def first(self):
        up, down = {"mdl": self.yp}, {"mdl": self.ym}
        return [
            self.copy(self.ypos, 0, 0, up, 0, own=True),
            self.copy(self.ypos, 1, 1, down, 1, own=True),
            self.copy(self.ypos, 1, 0, up, 0, own=True),
            self.copy(self.ypos, 0, 1, down, 1, own=True),
        ]

    def kept(self):
        return pltpu.make_async_copy(
            self.own.at[:, self.columns], self.full.at[self.ypos], self.local.at[0]
        )

    def start(self):
        for item in self.first():
            item.start()
        self.kept().start()

    def relay(self, part):
        if part == 0:
            return self.copy(self.ym, 0, 2, {"mdl": self.yp}, 2)
        return self.copy(self.yp, 1, 2, {"mdl": self.ym}, 2)

    def share(self, slot, part):
        return self.copy(self.src[slot], part, 3 + slot, {"rep": self.other}, 3 + slot)

    def arrived(self, slot, part):
        which = self.core if slot < 3 else 1 - self.core
        where = self.full.at[self.src[slot % 3], self.span(which, part)]
        pltpu.make_async_copy(where, where, self.recv.at[slot, part]).wait()

    def pass_on(self):
        for part in range(2):
            self.arrived(part, part)
            self.relay(part).start()
            self.share(part, part).start()

    def take_rest(self):
        for part in range(2):
            self.arrived(1 - part, part)
            self.share(1 - part, part).start()

    def take_last(self):
        for part in range(2):
            self.arrived(2, part)
            self.share(2, part).start()

    def finish(self):
        for slot in range(3, 6):
            for part in range(2):
                self.arrived(slot, part)
        for item in self.first():
            item.wait_send()
        for part in range(2):
            self.relay(part).wait_send()
            for slot in range(3):
                self.share(slot, part).wait_send()
        self.kept().wait()


def attend_kernel(
    heads, spans, count_ref, x_ref, wq_ref, wkv_ref, *refs
):
    each = len(spans)
    w_refs, out_ref, full_refs = refs[:each], refs[each], refs[each + 1 : 2 * each + 1]
    buf, acc, q_ref, kv_ref, send, recv, local, *w_semaphores = refs[2 * each + 1 :]
    rows = x_ref.shape[0]
    piece = rows // PIECES
    all_keys = buf.shape[0]
    me = lax.axis_index("rep")
    count = 16
    core = lax.rem(me, 2)
    xpos = lax.rem(me // 2, 2)
    other = me + 1 - 2 * core
    xpeer = me + 2 - 4 * xpos
    zp = lax.rem(me + 4, count)
    zm = lax.rem(me + 12, count)
    src = [
        zm,
        zp,
        lax.rem(me + 8, count),
        xpeer,
        lax.rem(xpeer + 12, count),
        lax.rem(xpeer + 4, count),
        lax.rem(xpeer + 8, count),
    ]
    src = src + [other] + [s + 1 - 2 * core for s in src]

    ypos = lax.axis_index("mdl")
    yp = lax.rem(ypos + 1, 4)
    ym = lax.rem(ypos + 3, 4)

    barrier = pltpu.get_barrier_semaphore()
    peers = [{"rep": zp}, {"rep": zm}, {"rep": xpeer}, {"rep": other}]
    peers += [{"mdl": yp}, {"mdl": ym}]
    for peer in peers:
        pl.semaphore_signal(barrier, inc=1, device_id=peer, device_id_type=MESH)

    rings = [
        WeightGather(columns, w_refs[k], full_refs[k], w_semaphores[3 * k : 3 * k + 3])
        for k, columns in enumerate(spans)
    ]
    pl.semaphore_wait(barrier, len(peers))
    for ring in rings:
        ring.start()

    total = count_ref[lax.axis_index("sec")]
    normed = rms_normed(x_ref[...].astype(F32)).astype(BF)
    live = me * rows + lax.broadcasted_iota(jnp.int32, (rows, HEAD), 0) < total
    for part in range(2):
        made = jnp.dot(normed, wkv_ref[part], preferred_element_type=F32)
        kv_ref[:, part * HEAD : (part + 1) * HEAD] = jnp.where(live, made, 0.0).astype(BF)

    def block_rows(block, part):
        return pl.ds(pl.multiple_of(block * rows + part * piece, piece), piece)

    def transfer(block, part, slot, target, lane, own=False):
        where = buf.at[block_rows(block, part), pl.ds(0, 2 * HEAD)]
        source = kv_ref.at[pl.ds(part * piece, piece)] if own else where
        return pltpu.make_async_remote_copy(
            src_ref=source,
            dst_ref=where,
            send_sem=send.at[lane, part],
            recv_sem=recv.at[slot, part],
            device_id={"rep": target},
            device_id_type=MESH,
        )

    plan = [
        (None, 3, xpeer),
        (None, 1, zm),
        (None, 0, zp),
        (None, 7, other),
        (1, 9, other),
        (0, 2, zp),
        (1, 2, zm),
        (0, 8, other),
        (3, 5, zm),
        (3, 4, zp),
        (3, 11, other),
        (2, 10, other),
        (2, 6, xpeer),
        (5, 13, other),
        (4, 12, other),
        (6, 14, other),
    ]

    def parts_of(index):
        return {5: (0,), 6: (1,)}.get(index, range(PIECES))

    def plan_copy(index, part):
        from_slot, to_slot, target = plan[index]
        block = me if from_slot is None else src[from_slot]
        return transfer(block, part, to_slot, target, index, own=from_slot is None)

    def arrived(slot, part):
        where = buf.at[block_rows(src[slot], part), pl.ds(0, 2 * HEAD)]
        pltpu.make_async_copy(where, where, recv.at[slot, part]).wait()

    def pass_on(slot):
        for part in range(PIECES):
            arrived(slot, part)
            for index, (from_slot, _, _) in enumerate(plan):
                if from_slot == slot and part in parts_of(index):
                    plan_copy(index, part).start()

    def take(slot):
        for part in range(PIECES):
            arrived(slot, part)

    for part in range(PIECES):
        for index in range(4):
            plan_copy(index, part).start()
    own_copy = pltpu.make_async_copy(
        kv_ref,
        buf.at[pl.ds(pl.multiple_of(me * rows, rows), rows), pl.ds(0, 2 * HEAD)],
        local.at[0],
    )
    own_copy.start()

    queries = jnp.dot(normed, wq_ref[...], preferred_element_type=F32) * (HEAD ** (-0.5) * LOG2E)
    for head in range(heads):
        q_ref[head * rows : (head + 1) * rows, :] = queries[
            :, head * HEAD : (head + 1) * HEAD
        ].astype(BF)
    key_index = lax.broadcasted_iota(jnp.int32, (all_keys, HEAD), 0)
    buf[:, 2 * HEAD :] = jnp.where(key_index < total, 1.0, 0.0).astype(BF)
    acc[...] = jnp.zeros_like(acc)
    own_copy.wait()

    chip_rows = 2 * rows
    zpos = me // 4

    def step(i, carry):
        @pl.when(i == 0)
        def _():
            take(7)

        @pl.when(i == 1)
        def _():
            pass_on(0)
            pass_on(1)
            take(9)

        @pl.when(i == 2)
        def _():
            pass_on(3)
            take(8)

        @pl.when(i == 3)
        def _():
            pass_on(2)
            take(10)

        @pl.when(i == 4)
        def _():
            pass_on(5)
            take(11)

        for k, ring in enumerate(rings):
            pl.when(i == 3 + 2 * k)(ring.pass_on)
            pl.when(i == (5, 7)[k] if each > 1 else i == 7)(ring.take_rest)

        @pl.when(i == 5)
        def _():
            pass_on(4)
            take(13)

        @pl.when(i == 6)
        def _():
            pass_on(6)
            take(12)

        @pl.when(i == 7)
        def _():
            take(14)

        j = lax.rem(i, 4)
        dz = j + (j // 2) * (1 - 2 * lax.rem(j, 2))
        dx = i // 4
        chip = lax.rem(zpos + dz, 4) * 2 + lax.rem(xpos + dx, 2)
        span = pl.ds(pl.multiple_of(chip * chip_rows, chip_rows), chip_rows)
        scores = lax.dot_general(
            q_ref[...],
            buf[span, :HEAD],
            (((1,), (1,)), ((), ())),
            preferred_element_type=F32,
        )
        weights = jnp.exp2(scores).astype(BF)
        acc[...] += jnp.dot(weights, buf[span, HEAD:], preferred_element_type=F32)
        return carry

    lax.fori_loop(0, 8, step, 0)

    for ring in rings:
        ring.take_last()

    for head in range(heads):
        part = acc[head * rows : (head + 1) * rows, :]
        sums = part[:, HEAD:]
        safe = (sums > sum_low) & (sums < sum_high)
        out_ref[:, head * HEAD : (head + 1) * HEAD] = jnp.where(
            safe, part[:, :HEAD] / sums, jnp.nan
        ).astype(BF)

    for ring in rings:
        ring.finish()
    for index in range(len(plan)):
        for part in parts_of(index):
            plan_copy(index, part).wait_send()


def attend_call(counts, source, w_query, w_keyval, weights, ident):
    heads = w_query.shape[1] // HEAD
    rows = source.shape[0]
    keys = rows * 16
    vmem = pl.BlockSpec(memory_space=pltpu.VMEM)
    anywhere = pl.BlockSpec(memory_space=pl.ANY)
    return pl.pallas_call(
        functools.partial(attend_kernel, heads, tuple(columns for _, columns in weights)),
        out_shape=[
            jax.ShapeDtypeStruct((rows, heads * HEAD), BF),
        ]
        + [
            jax.ShapeDtypeStruct((4, w.shape[0], columns[1]), BF) for w, columns in weights
        ],
        in_specs=[pl.BlockSpec(memory_space=pltpu.SMEM), vmem, vmem, vmem]
        + [anywhere] * len(weights),
        out_specs=[vmem] + [anywhere] * len(weights),
        scratch_shapes=[
            pltpu.VMEM((keys, 3 * HEAD), BF),
            pltpu.VMEM((heads * rows, 2 * HEAD), F32),
            pltpu.VMEM((heads * rows, HEAD), BF),
            pltpu.VMEM((rows, 2 * HEAD), BF),
            pltpu.SemaphoreType.DMA((16, PIECES)),
            pltpu.SemaphoreType.DMA((15, PIECES)),
            pltpu.SemaphoreType.DMA((1,)),
        ]
        + [
            pltpu.SemaphoreType.DMA((6, 2)),
            pltpu.SemaphoreType.DMA((6, 2)),
            pltpu.SemaphoreType.DMA((1,)),
        ]
        * len(weights),
        compiler_params=pltpu.CompilerParams(
            collective_id=ident, has_side_effects=True, vmem_limit_bytes=40 * 2**20
        ),
        cost_estimate=pl.CostEstimate(
            flops=4 * heads * rows * keys * HEAD,
            bytes_accessed=keys * 4 * HEAD,
            transcendentals=heads * rows * keys,
        ),
    )(counts, source, w_query, w_keyval, *(w for w, _ in weights))


def careful_kernel(total_ref, q_ref, kv_ref, out_ref, top, acc, total_sum):
    step = pl.program_id(0)
    block = kv_ref.shape[0]

    @pl.when(step == 0)
    def _():
        top[...] = jnp.full_like(top, masked_score)
        acc[...] = jnp.zeros_like(acc)
        total_sum[...] = jnp.zeros_like(total_sum)

    scores = lax.dot_general(
        q_ref[...], kv_ref[:, :HEAD], (((1,), (1,)), ((), ())), preferred_element_type=F32
    )
    key_index = step * block + lax.broadcasted_iota(jnp.int32, scores.shape, 1)
    live = key_index < total_ref[0]
    scores = jnp.where(live, scores, masked_score)
    old = top[...]
    new = jnp.maximum(old, jnp.max(scores, axis=1, keepdims=True))
    top[...] = new
    rescale = jnp.exp2(old - new)
    weights = jnp.where(live, jnp.exp2(scores - new[:, :1]), 0.0)
    total_sum[...] = total_sum[...] * rescale + jnp.sum(weights, axis=1, keepdims=True)
    acc[...] = acc[...] * rescale + jnp.dot(
        weights.astype(BF), kv_ref[:, HEAD:], preferred_element_type=F32
    )

    @pl.when(step == pl.num_programs(0) - 1)
    def _():
        rows, width = out_ref.shape
        for head in range(width // HEAD):
            span = slice(head * rows, (head + 1) * rows)
            out_ref[:, head * HEAD : (head + 1) * HEAD] = (acc[span, :] / total_sum[span, :]).astype(
                BF
            )


def careful_call(total, queries, kv_full, rows):
    heads = queries.shape[0] // rows
    block = 256
    return pl.pallas_call(
        careful_kernel,
        out_shape=jax.ShapeDtypeStruct((rows, heads * HEAD), BF),
        grid=(kv_full.shape[0] // block,),
        in_specs=[
            pl.BlockSpec(memory_space=pltpu.SMEM),
            pl.BlockSpec(queries.shape, lambda i: (0, 0)),
            pl.BlockSpec((block, 2 * HEAD), lambda i: (i, 0)),
        ],
        out_specs=pl.BlockSpec((rows, heads * HEAD), lambda i: (0, 0)),
        scratch_shapes=[pltpu.VMEM((heads * rows, HEAD), F32)] * 3,
        compiler_params=pltpu.CompilerParams(vmem_limit_bytes=20 * 2**20),
    )(total, queries, kv_full)


class YGather:
    def __init__(self, own_half, place, send, recv):
        self.ypos = lax.axis_index("mdl")
        self.yp = lax.rem(self.ypos + 1, 4)
        self.ym = lax.rem(self.ypos + 3, 4)
        self.y2 = lax.rem(self.ypos + 2, 4)
        self.own_half, self.place, self.send, self.recv = own_half, place, send, recv

    def greet(self, barrier):
        for peer in (self.yp, self.ym):
            pl.semaphore_signal(barrier, inc=1, device_id={"mdl": peer}, device_id_type=MESH)
        return 2

    def copy(self, source_y, part, slot, target, lane, own=False):
        return pltpu.make_async_remote_copy(
            src_ref=self.own_half(part) if own else self.place(source_y, part, lane - 2),
            dst_ref=self.place(source_y, part, slot),
            send_sem=self.send.at[lane, part],
            recv_sem=self.recv.at[slot, part],
            device_id={"mdl": target},
            device_id_type=MESH,
        )

    def first(self):
        return [
            self.copy(self.ypos, 0, 0, self.yp, 0, own=True),
            self.copy(self.ypos, 1, 1, self.ym, 1, own=True),
            self.copy(self.ypos, 1, 0, self.yp, 0, own=True),
            self.copy(self.ypos, 0, 1, self.ym, 1, own=True),
        ]

    def start(self):
        for item in self.first():
            item.start()

    def arrived(self, slot, part):
        where = self.place((self.ym, self.yp, self.y2)[slot], part, slot)
        pltpu.make_async_copy(where, where, self.recv.at[slot, part]).wait()

    def relay(self, part):
        if part == 0:
            return self.copy(self.ym, 0, 2, self.yp, 2)
        return self.copy(self.yp, 1, 2, self.ym, 3)

    def pass_on(self, part):
        self.arrived(part, part)
        self.relay(part).start()

    def wait_sent(self):
        for item in self.first():
            item.wait_send()
        for part in range(2):
            self.relay(part).wait_send()


class Geometry:
    def __init__(self, rows, columns, by_rows):
        self.by_rows = by_rows
        self.rows, self.columns = rows, columns
        if by_rows:
            self.half = (rows // 2, columns)
            self.quarter_shape = [(rows // 4, columns // 4)] * 2
            self.sub_shape = [(rows // 16, columns // 4)] * 2
        else:
            third = columns // 6
            self.half = (rows, columns // 2)
            self.quarter_shape = [(rows // 4, 2 * third), (rows // 4, third)]
            self.sub_shape = [(rows // 4, third // 2), (rows // 8, third // 2)]

    def whole(self, core):
        if self.by_rows:
            return (core * self.half[0], 0)
        return (0, core * self.half[1])

    def quarter(self, part, index):
        rows, columns = self.quarter_shape[part]
        if self.by_rows:
            return (part * rows, index * columns)
        return (index * rows, part * self.quarter_shape[0][1])

    def sub(self, part, index):
        rows, columns = self.sub_shape[part]
        if self.by_rows:
            return (index * rows, 0)
        if part == 0:
            return (0, index * columns)
        return ((index // 2) * rows, lax.rem(index, 2) * columns)

    def scatter_scratch(self):
        vmem = pltpu.VMEM
        return [vmem(self.half, BF)] * 3 + [vmem((3,) + q, BF) for q in self.quarter_shape]

    def sub_scratch(self):
        return [pltpu.VMEM((3,) + sub, BF) for sub in self.sub_shape]

    def semaphores(self):
        dma = pltpu.SemaphoreType.DMA
        return [dma((4, 2, 3)), dma((4, 2, 3)), dma((9,)), dma((9,))]


def box(start, shape):
    row, column = start
    return (
        pl.ds(row if isinstance(row, int) else pl.multiple_of(row, 16), shape[0]),
        pl.ds(column if isinstance(column, int) else pl.multiple_of(column, HEAD), shape[1]),
    )


def plus(left, right):
    return (left[0] + right[0], left[1] + right[1])


class Reduce:
    hops = (2, 1, 3)

    def __init__(self, shape, att_ref, d_ref, out_ref, scatter, sums, sub_in, semaphores):
        self.g = shape
        self.att, self.d, self.out = att_ref, d_ref, out_ref
        if scatter is not None:
            self.theirs, self.mine, self.got = scatter[:3]
            self.part_in = scatter[3:5]
        self.part_sum = sums
        self.sub_in = sub_in
        self.send, self.recv, self.csend, self.crecv = semaphores
        me = lax.axis_index("rep")
        self.me = me
        self.core = lax.rem(me, 2)
        self.other = me + 1 - 2 * self.core
        self.zpos = me // 4
        self.xpos = lax.rem(me // 2, 2) * 2 + lax.axis_index("sec")
        self.first = [self.xpos, self.zpos]
        self.second = [self.zpos, self.xpos]
        self.near = [self.at_x, self.at_z]

    def at_x(self, k):
        there = lax.rem(self.xpos + k, 4)
        return {"rep": self.zpos * 4 + (there // 2) * 2 + self.core, "sec": lax.rem(there, 2)}

    def at_z(self, k):
        return {"rep": lax.rem(self.me + 4 * k, 16)}

    def greet(self, barrier):
        for k in range(1, 4):
            pl.semaphore_signal(barrier, inc=1, device_id=self.at_x(k), device_id_type=MESH)
            pl.semaphore_signal(barrier, inc=1, device_id=self.at_z(k), device_id_type=MESH)
        pl.semaphore_signal(barrier, inc=1, device_id={"rep": self.other}, device_id_type=MESH)
        return 7

    def grad(self, which):
        left, right = self.att, self.d
        if self.g.by_rows:
            size = self.g.half[0]
            left = left[:, pl.ds(pl.multiple_of(which * size, size), size)]
            right = right[...]
        else:
            size = self.g.half[1]
            left = left[...]
            right = right[:, pl.ds(pl.multiple_of(which * size, HEAD), size)]
        return lax.dot_general(left, right, (((0,), (0,)), ((), ())), preferred_element_type=F32)

    def copy(self, source, target, send, recv, device):
        return pltpu.make_async_remote_copy(
            src_ref=source,
            dst_ref=target,
            send_sem=send,
            recv_sem=recv,
            device_id=device,
            device_id_type=MESH,
        )

    def swap(self):
        return self.copy(
            self.theirs, self.got, self.csend.at[0], self.crecv.at[0], {"rep": self.other}
        )

    def stage(self, level, part, k, source, target, device):
        return self.copy(
            source,
            target,
            self.send.at[level, part, k - 1],
            self.recv.at[level, part, k - 1],
            device,
        )

    def scatter_one(self, part, k):
        start = self.g.quarter(part, lax.rem(self.first[part] + k, 4))
        return self.stage(
            0,
            part,
            k,
            self.mine.at[box(start, self.g.quarter_shape[part])],
            self.part_in[part].at[k - 1],
            self.near[part](k),
        )

    def scatter_two(self, part, k):
        start = self.g.sub(part, lax.rem(self.second[part] + k, 4))
        return self.stage(
            1,
            part,
            k,
            self.part_sum[part].at[box(start, self.g.sub_shape[part])],
            self.sub_in[part].at[k - 1],
            self.near[1 - part](k),
        )

    def my_sub(self, part):
        start = plus(
            self.g.whole(self.core),
            plus(self.g.quarter(part, self.first[part]), self.g.sub(part, self.second[part])),
        )
        return box(start, self.g.sub_shape[part])

    def out_quarter(self, core, part, index):
        start = plus(self.g.whole(core), self.g.quarter(part, index))
        return self.out.at[box(start, self.g.quarter_shape[part])]

    def gather_two(self, part, k):
        where = self.out.at[self.my_sub(part)]
        return self.stage(2, part, k, where, where, self.near[1 - part](k))

    def gather_one(self, part, k):
        where = self.out_quarter(self.core, part, self.first[part])
        return self.stage(3, part, k, where, where, self.near[part](k))

    def share(self, part, k, core):
        where = self.out_quarter(core, part, lax.rem(self.first[part] + 4 - k, 4))
        index = 1 + part * 4 + k
        return self.copy(
            where, where, self.csend.at[index], self.crecv.at[index], {"rep": self.other}
        )

    def begin(self):
        self.theirs[...] = self.grad(1 - self.core).astype(BF)

    def swap_and_scatter(self):
        self.swap().start()
        self.scatter_own()

    def scatter_own(self):
        own = self.grad(self.core)
        self.swap().wait_recv()
        self.mine[...] = (own + self.got[...].astype(F32)).astype(BF)
        for k in self.hops:
            for part in range(2):
                self.scatter_one(part, k).start()

    def first_sums(self):
        for part in range(2):
            start = self.g.quarter(part, self.first[part])
            total = self.mine[box(start, self.g.quarter_shape[part])].astype(F32)
            for k in (1, 3, 2):
                self.scatter_one(part, k).wait_recv()
                total += self.part_in[part][k - 1].astype(F32)
            self.part_sum[part][...] = total.astype(BF)

    def second_scatter(self):
        for k in self.hops:
            for part in range(2):
                self.scatter_two(part, k).start()

    def first_gather(self):
        for part in range(2):
            start = self.g.sub(part, self.second[part])
            total = self.part_sum[part][box(start, self.g.sub_shape[part])].astype(F32)
            for k in (1, 3, 2):
                self.scatter_two(part, k).wait_recv()
                total += self.sub_in[part][k - 1].astype(F32)
            self.out[self.my_sub(part)] = total.astype(BF)
            for k in self.hops:
                self.gather_two(part, k).start()

    def second_gather(self):
        for part in range(2):
            for k in range(1, 4):
                self.gather_two(part, k).wait_recv()
            for k in self.hops:
                self.gather_one(part, k).start()
            self.share(part, 0, self.core).start()

    def last_shares(self):
        for k in (1, 3, 2):
            for part in range(2):
                self.gather_one(part, k).wait_recv()
                self.share(part, k, self.core).start()

    def finish_scatter(self):
        self.swap().wait_send()
        for part in range(2):
            for k in range(1, 4):
                self.scatter_one(part, k).wait_send()

    def finish(self):
        for part in range(2):
            for k in range(4):
                self.share(part, k, 1 - self.core).wait_recv()
        for part in range(2):
            for k in range(1, 4):
                self.scatter_two(part, k).wait_send()
                self.gather_two(part, k).wait_send()
                self.gather_one(part, k).wait_send()
            for k in range(4):
                self.share(part, k, self.core).wait_send()


def reduce_kernel(shape, att_ref, d_ref, out_ref, *scratch):
    each = len(scratch) // 2
    works = []
    for index in range(2):
        part = scratch[index * each : (index + 1) * each]
        span = pl.ds(index * shape.columns, shape.columns)
        works.append(
            Reduce(
                shape,
                att_ref,
                d_ref.at[:, span],
                out_ref.at[:, span],
                part[:5],
                part[5:7],
                part[7:9],
                part[9:13],
            )
        )
    early, late = works
    barrier = pltpu.get_barrier_semaphore()
    expected = early.greet(barrier)
    early.begin()
    pl.semaphore_wait(barrier, expected)
    early.swap().start()
    late.begin()
    late.swap().start()
    early.scatter_own()
    late.scatter_own()
    early.first_sums()
    early.second_scatter()
    late.first_sums()
    late.second_scatter()
    early.first_gather()
    late.first_gather()
    early.second_gather()
    late.second_gather()
    early.last_shares()
    late.last_shares()
    for work in works:
        work.finish_scatter()
        work.finish()


def reduced_grad(attended, grad_in, ident):
    shape = Geometry(attended.shape[1], grad_in.shape[1] // 2, True)
    vmem = pl.BlockSpec(memory_space=pltpu.VMEM)
    return pl.pallas_call(
        functools.partial(reduce_kernel, shape),
        out_shape=jax.ShapeDtypeStruct((attended.shape[1], grad_in.shape[1]), BF),
        in_specs=[vmem, vmem],
        out_specs=vmem,
        scratch_shapes=2
        * (
            shape.scatter_scratch()
            + [pltpu.VMEM(q, BF) for q in shape.quarter_shape]
            + shape.sub_scratch()
            + shape.semaphores()
        ),
        compiler_params=pltpu.CompilerParams(
            collective_id=ident, has_side_effects=True, vmem_limit_bytes=24 * 2**20
        ),
    )(attended, grad_in)


def policy_kernel(
    shape,
    count_ref,
    x_ref,
    cin_ref,
    wp_ref,
    action_ref,
    advantage_ref,
    old_ref,
    att_ref,
    out_ref,
    sum_a,
    sum_b,
    part_ref,
    d_ref,
    *refs,
):
    scatter, semaphores, (send, recv, local) = refs[:5], refs[5:9], refs[9:]
    work = Reduce(shape, att_ref, d_ref, None, scatter, (sum_a, sum_b), None, semaphores)
    rows, width = part_ref.shape
    half = rows // 2

    def place(source_y, part, slot):
        return out_ref.at[
            pl.ds(part * half, half), pl.ds(pl.multiple_of(source_y * width, HEAD), width)
        ]

    ring = YGather(lambda part: part_ref.at[pl.ds(part * half, half)], place, send, recv)
    barrier = pltpu.get_barrier_semaphore()
    expected = ring.greet(barrier) + work.greet(barrier)
    part_ref[...] = jnp.dot(x_ref[...], cin_ref[...], preferred_element_type=F32).astype(BF)
    pl.semaphore_wait(barrier, expected)
    ring.start()
    mine = pltpu.make_async_copy(
        part_ref, out_ref.at[:, pl.ds(pl.multiple_of(ring.ypos * width, HEAD), width)], local.at[0]
    )
    mine.start()
    d_ref[...] = policy_backward(
        x_ref[...],
        standing(action_ref[...]),
        standing(advantage_ref[...])[:, :1],
        standing(old_ref[...])[:, :1],
        live_scale(count_ref, rows),
        wp_ref[...],
    ).astype(BF)
    ring.pass_on(0)
    ring.pass_on(1)
    work.begin()
    work.swap_and_scatter()
    ring.arrived(0, 1)
    ring.arrived(1, 0)
    work.first_sums()
    ring.arrived(2, 0)
    ring.arrived(2, 1)
    work.finish_scatter()
    ring.wait_sent()
    mine.wait()


def policy_call(counts, hidden, c_in, w_policy, action, advantage, old_values, attended, ident):
    rows = hidden.shape[0]
    width = c_in.shape[1]
    shape = Geometry(attended.shape[1], hidden.shape[1], False)
    vmem = pl.BlockSpec(memory_space=pltpu.VMEM)
    return pl.pallas_call(
        functools.partial(policy_kernel, shape),
        out_shape=[jax.ShapeDtypeStruct((rows, 4 * width), BF)]
        + [jax.ShapeDtypeStruct(q, BF) for q in shape.quarter_shape],
        in_specs=[pl.BlockSpec(memory_space=pltpu.SMEM)] + [vmem] * 7,
        out_specs=[vmem] * 3,
        scratch_shapes=[pltpu.VMEM((rows, width), BF), pltpu.VMEM(hidden.shape, BF)]
        + shape.scatter_scratch()
        + shape.semaphores()
        + [
            pltpu.SemaphoreType.DMA((4, 2)),
            pltpu.SemaphoreType.DMA((3, 2)),
            pltpu.SemaphoreType.DMA((1,)),
        ],
        compiler_params=pltpu.CompilerParams(
            collective_id=ident, has_side_effects=True, vmem_limit_bytes=32 * 2**20
        ),
    )(counts, hidden, c_in, w_policy, action, advantage, old_values, attended)


def output_kernel(shape, starts, x_ref, base_ref, *refs):
    w_refs, refs = refs[: len(starts)], refs[len(starts) :]
    if shape is None:
        out_ref, acc, blocks, send, recv = refs
        work = None
    else:
        count_ref, return_ref, wv_ref, sum_a, sum_b, value_ref, out_ref, grad_ref = refs[:8]
        acc, blocks, send, recv, lanes = refs[8:13]
        work = Reduce(shape, None, None, grad_ref, None, (sum_a, sum_b), refs[13:15], refs[15:19])
    rows = x_ref.shape[0]
    half = rows // 2
    ring = YGather(
        lambda part: x_ref.at[pl.ds(part * half, half)],
        lambda source_y, part, slot: blocks.at[slot, pl.ds(part * half, half)],
        send,
        recv,
    )
    barrier = pltpu.get_barrier_semaphore()
    expected = ring.greet(barrier)
    if work is not None:
        expected += work.greet(barrier)
    pl.semaphore_wait(barrier, expected)
    ring.start()
    if work is not None:
        work.second_scatter()
    for start, w_ref in zip(starts, w_refs):
        columns = slice(start, start + w_ref.shape[2])
        acc[:, columns] = base_ref[:, columns].astype(F32) + jnp.dot(
            x_ref[...], w_ref[ring.ypos], preferred_element_type=F32
        )

    def add(slot, part):
        source_y = (ring.ym, ring.yp, ring.y2)[slot]
        span = pl.ds(part * half, half)
        for start, w_ref in zip(starts, w_refs):
            columns = slice(start, start + w_ref.shape[2])
            acc[span, columns] += jnp.dot(
                blocks[slot, span, :], w_ref[source_y], preferred_element_type=F32
            )

    if work is not None:
        work.first_gather()
    ring.pass_on(0)
    ring.pass_on(1)
    add(0, 0)
    add(1, 1)
    if work is not None:
        work.second_gather()
    ring.arrived(0, 1)
    add(0, 1)
    ring.arrived(1, 0)
    add(1, 0)
    if work is not None:
        work.last_shares()
    ring.arrived(2, 0)
    add(2, 0)
    ring.arrived(2, 1)
    add(2, 1)
    if work is None:
        out_ref[...] = acc[...].astype(BF)
    else:
        value, out_ref[...] = value_backward(
            acc[...], standing(return_ref[...])[:, :1], live_scale(count_ref, rows), wv_ref[...]
        )
        lanes[...] = jnp.broadcast_to(value, lanes.shape)
        mine = lanes[pl.ds(pl.multiple_of(ring.ypos * value_ref.shape[1], 8), value_ref.shape[1]), :]
        value_ref[...] = jnp.transpose(mine)[:1]
    if work is not None:
        work.finish()
    ring.wait_sent()


def output_call(x, weights, base, value_args, ident):
    rows, width = x.shape
    columns = base.shape[1]
    starts = []
    for w_full in weights:
        starts.append(sum(other.shape[2] for other in weights[: len(starts)]))
    vmem = pl.BlockSpec(memory_space=pltpu.VMEM)
    args = [x, base] + list(weights)
    in_specs = [vmem] * len(args)
    out_shape = [jax.ShapeDtypeStruct((rows, columns), BF)]
    scratch = [
        pltpu.VMEM((rows, columns), F32),
        pltpu.VMEM((3, rows, width), BF),
        pltpu.SemaphoreType.DMA((4, 2)),
        pltpu.SemaphoreType.DMA((3, 2)),
    ]
    shape = None
    if value_args is not None:
        shape, counts, target, w_value, sums = value_args
        args += [counts, target, w_value] + list(sums)
        in_specs += [pl.BlockSpec(memory_space=pltpu.SMEM)] + [vmem] * 4
        out_shape = [jax.ShapeDtypeStruct((1, rows // 4), F32)] + out_shape
        scratch.append(pltpu.VMEM((rows, HEAD), F32))
        out_shape.append(jax.ShapeDtypeStruct((shape.rows, shape.columns), BF))
        scratch += shape.sub_scratch() + shape.semaphores()
    return pl.pallas_call(
        functools.partial(output_kernel, shape, tuple(starts)),
        out_shape=out_shape,
        in_specs=in_specs,
        out_specs=[vmem] * len(out_shape),
        scratch_shapes=scratch,
        compiler_params=pltpu.CompilerParams(
            collective_id=ident, has_side_effects=True, vmem_limit_bytes=(20 if shape is None else 32) * 2**20
        ),
    )(*args)


def stacked_queries(source, w_query):
    rows = source.shape[0]
    normed = rms_normed(source.astype(F32)).astype(BF)
    queries = (
        jnp.dot(normed, w_query, preferred_element_type=F32) * (HEAD ** (-0.5) * LOG2E)
    ).astype(BF)
    heads = queries.shape[1] // HEAD
    return jnp.transpose(queries.reshape(rows, heads, HEAD), (1, 0, 2)).reshape(heads * rows, HEAD)


def ring_gather(block, axis):
    count = lax.axis_size(axis)
    me = lax.axis_index(axis)
    onward = [(k, (k + 1) % count) for k in range(count)]
    blocks = jnp.zeros((count,) + block.shape, block.dtype)

    def turn(k, carried):
        blocks, moving = carried
        blocks = lax.dynamic_update_index_in_dim(blocks, moving, lax.rem(me + count - k, count), 0)
        return (blocks, lax.ppermute(moving, axis, onward))

    return lax.fori_loop(0, count, turn, (blocks, block))[0]


def ring_sum(block, axis):
    return jnp.sum(ring_gather(block, axis).astype(F32), axis=0)


def careful_attend(total, source, w_query, w_keyval):
    normed = rms_normed(source.astype(F32)).astype(BF)
    keyval = [jnp.dot(normed, w_keyval[part], preferred_element_type=F32) for part in range(2)]
    joined = jnp.concatenate(keyval, axis=1).astype(BF)
    everyone = ring_gather(joined, "rep").reshape(-1, 2 * HEAD)
    return careful_call(total, stacked_queries(source, w_query), everyone, source.shape[0])


def summed_grad(attended, grad_in):
    grad = lax.dot_general(
        attended, grad_in, (((0,), (0,)), ((), ())), preferred_element_type=F32
    )
    return ring_sum(ring_sum(grad.astype(BF), "rep").astype(BF), "sec")


def careful_path(
    obs, a_query, a_keyval, a_out, w_policy, c_in, c_query, c_keyval, c_out, w_value, columns, total
):
    attended = careful_attend(total, obs, a_query, a_keyval)
    mixed_sum = ring_sum(jnp.dot(attended, a_out, preferred_element_type=F32), "mdl")
    hidden = (obs.astype(F32) + mixed_sum).astype(BF)
    action, advantage, old_values, target, scale = columns
    dhidden = policy_backward(hidden, action, advantage, old_values, scale, w_policy).astype(BF)
    embed_part = jnp.dot(hidden, c_in, preferred_element_type=F32).astype(BF)
    embedded = jnp.concatenate(list(ring_gather(embed_part, "mdl")), axis=1)
    critic_attended = careful_attend(total, embedded, c_query, c_keyval)
    critic_sum = ring_sum(
        jnp.dot(critic_attended, c_out, preferred_element_type=F32), "mdl"
    )
    value, dmixed = value_backward(
        embedded.astype(F32) + critic_sum, target, scale, w_value[None, :]
    )
    part_rows = value.shape[0] // 4
    value = lax.dynamic_slice_in_dim(value[:, 0], lax.axis_index("mdl") * part_rows, part_rows, 0)
    return (value[None, :], summed_grad(attended, dhidden), summed_grad(critic_attended, dmixed))


def on_device(
    obs,
    a_query,
    a_keyval,
    a_out,
    w_policy,
    c_in,
    c_query,
    c_keyval,
    c_out,
    w_value,
    actions,
    advantages,
    old_logp,
    returns,
    robot_count,
):
    rows = obs.shape[1]

    def careful():
        total = robot_count[lax.axis_index("sec")]
        live = lax.axis_index("rep") * rows + lax.iota(jnp.int32, rows) < total
        scale = jnp.where(live, 1.0 / jnp.sum(robot_count).astype(F32), 0.0)
        columns = (actions[0], advantages[0], old_logp[0], returns[0], scale)
        return careful_path(
            obs[0],
            a_query,
            a_keyval,
            a_out,
            w_policy,
            c_in,
            c_query,
            c_keyval,
            c_out,
            w_value,
            tuple(column[:, None] for column in columns),
            total.reshape(1),
        )

    early = c_out.shape[1] // 4
    attended, a_out_full, c_out_early = attend_call(
        robot_count,
        obs[0],
        a_query,
        a_keyval,
        [(a_out, (0, a_out.shape[1])), (c_out, (0, early))],
        1,
    )
    (hidden,) = output_call(attended, [a_out_full], obs[0], None, 3)
    embedded, *sums = policy_call(
        robot_count, hidden, c_in, w_policy, actions, advantages, old_logp, attended, 4
    )
    critic_attended, c_out_late = attend_call(
        robot_count, embedded, c_query, c_keyval, [(c_out, (early, 3 * early))], 2
    )
    shape = Geometry(attended.shape[1], hidden.shape[1], False)
    values, dmixed, actor_summed = output_call(
        critic_attended,
        [c_out_early, c_out_late],
        embedded,
        (shape, robot_count, returns, w_value[None, :], sums),
        5,
    )
    critic_summed = reduced_grad(critic_attended, dmixed, 6)
    mark = critic_summed[0, 0].astype(F32)
    values, actor_grad, critic_grad = lax.cond(
        mark == mark,
        lambda: (values, actor_summed.astype(F32), critic_summed.astype(F32)),
        careful,
    )
    return (values, actor_grad, critic_grad)


def solution(mesh):
    return jax.shard_map(
        on_device,
        mesh=mesh,
        in_specs=(
            P("sec", "rep", None),
            P(None, "mdl"),
            P(None, None, "mdl"),
            P("mdl", None),
            P(),
            P(None, "mdl"),
            P(None, "mdl"),
            P(None, None, "mdl"),
            P("mdl", None),
            P(),
            P("sec", "rep"),
            P("sec", "rep"),
            P("sec", "rep"),
            P("sec", "rep"),
            P(),
        ),
        out_specs=(P("sec", ("rep", "mdl")), P("mdl", None), P("mdl", None)),
        check_vma=False,
    )
```
